32 devices in a mesh: dp: 4 (over y, x), blk: 8 (over z, core).
Axes of the slice: x: 2, y: 2, z: 4, core: 2. Of those that a mesh axis runs over, the one named last changes fastest.
Arguments:
- latents: bfloat16 [2, 4, 1024, 1152], P(None, 'dp', 'blk'), may hold values from -6 to 6
- conditions: bfloat16 [2, 4, 4, 1152], P(None, 'dp'), may hold values from -6 to 6
- doc_lengths: int32 [2, 4, 4], P(None, 'dp'), may hold values from 0 to 1024, as said below
- cotangent: bfloat16 [2, 4, 1024, 1152], P(None, 'dp', 'blk'), may hold values from -6 to 6
- ada_weight: bfloat16 [1152, 6912], P('dp'), may hold values from -0.1875 to 0.1875
- ada_bias: bfloat16 [6912], P('dp'), may hold values from -1.75 to 1.75
- qkv_weight: bfloat16 [1152, 3456], P('dp'), may hold values from -0.1875 to 0.1875
- qv_bias: bfloat16 [2, 1152], P(None, 'dp'), may hold values from -0.3125 to 0.3125
- proj_weight: bfloat16 [1152, 1152], P('dp'), may hold values from -2 to 2
- proj_bias: bfloat16 [1152], P('dp'), may hold values from -1.75 to 1.75
- fc1_weight: bfloat16 [1152, 4608], P('dp'), may hold values from -0.1875 to 0.1875
- fc1_bias: bfloat16 [4608], P('dp'), may hold values from -3 to 3
- fc2_weight: bfloat16 [4608, 1152], P('dp'), may hold values from -0.09375 to 0.09375
- fc2_bias: bfloat16 [1152], P('dp'), may hold values from -1.75 to 1.75
Outputs:
- block_out: bfloat16 [2, 4, 1024, 1152], P(None, 'dp', 'blk')
- latent_grad: float32 [2, 4, 1024, 1152], P(None, 'dp', 'blk')
- cond_grad: float32 [2, 4, 4, 1152], P(None, 'dp')
- ada_wgrad: float32 [1152, 6912], P('dp')
- ada_bgrad: float32 [6912], P('dp')
- qkv_wgrad: float32 [1152, 3456], P('dp')
- qv_bgrad: float32 [2, 1152], P(None, 'dp')
- proj_wgrad: float32 [1152, 1152], P('dp')
- proj_bgrad: float32 [1152], P('dp')
- fc1_wgrad: float32 [1152, 4608], P('dp')
- fc1_bgrad: float32 [4608], P('dp')
- fc2_wgrad: float32 [4608, 1152], P('dp')
- fc2_bgrad: float32 [1152], P('dp')
The draws below stay inside these ranges and needn't reach their ends.
Inputs may be any that keep to these rules, and one draw needn't show every extreme that they name: `doc_lengths`: in every row the 4 lengths sum to 1024; a row's positions are its slots' images in slot order, and a slot may be empty. Of the 2 rows that one index of dp holds over all micro-batches, exactly one is a single image in slot 0; every other row holds two or more images.
All inputs are finite; a program needn't handle non-finite values.
Results may differ from the reference program's by a relative error of at most 0.019.
Values may be sent and summed in bfloat16 or wider, within the bound.
No kernel may reach another device: no remote copies, remote signals or barrier semaphores. Data moves between devices by JAX's collectives and lax.ppermute only.
A program may use at most 208 MiB of HBM per device.

```python
import math
import jax
import jax.numpy as jnp
from jax import lax

D = 1152
HEADS = 16
HEAD = 72
FF = 4608
DOCS = 4
MICRO = 2
ROWS_DEV = 1
ROWS = 4
LEN = 1024


def draw_doc_lengths(key, part):
    key = jax.random.fold_in(key, 11)
    cut_key, pick_key = jax.random.split(key)
    cuts = jnp.sort(jax.random.randint(cut_key, (MICRO, ROWS, DOCS - 1), 1, LEN), axis=-1).astype(jnp.int32)
    lower = jnp.zeros((MICRO, ROWS, 1), jnp.int32)
    upper = jnp.full((MICRO, ROWS, 1), LEN, jnp.int32)
    edges = jnp.concatenate([lower, cuts, upper], axis=-1)
    spans = edges[:, :, 1:] - edges[:, :, :-1]
    groups = ROWS // ROWS_DEV
    chosen = jax.random.randint(pick_key, (1, groups, 1), 0, MICRO * ROWS_DEV).astype(jnp.int32)
    flat_ids = jnp.arange(MICRO, dtype=jnp.int32)[:, None, None] * ROWS_DEV + jnp.arange(ROWS_DEV, dtype=jnp.int32)[None, None, :]
    single = (flat_ids == chosen).reshape(MICRO, ROWS, 1)
    whole = jnp.concatenate([upper, jnp.zeros((MICRO, ROWS, DOCS - 1), jnp.int32)], axis=-1)
    return jnp.where(single, whole, spans)


def block_levels(rng, shape, pieces, low, high):
    level = 1.0
    for dim, shards_of in pieces:
        draws = jax.random.uniform(jax.random.fold_in(jax.random.fold_in(rng, 6), dim), (shards_of,), jnp.float32, low / len(pieces), high / len(pieces))
        level = level * jnp.repeat(jnp.exp(draws), shape[dim] // shards_of).reshape((-1,) + (1,) * (len(shape) - 1 - dim))
    return level


def gaussian(key, dims, width, most, shards=(), kind=jnp.bfloat16):
    drawn = jax.random.normal(key, dims, jnp.float32) * width
    if len(shards) > 0:
        drawn = block_levels(key, dims, shards, -0.22, 0.18) * drawn
    return jnp.clip(drawn, min=-most, max=most).astype(kind)


def setup_inputs(seed: int = 0) -> dict:
    key_of = jax.random.split(jax.random.key(seed), 15)
    latents = gaussian(key_of[0], (MICRO, ROWS, LEN, D), 1.0, 6.0, ((1, 4), (2, 8)))
    conditions = gaussian(key_of[1], (MICRO, ROWS, DOCS, D), 1.0, 6.0, ((1, 4),))
    doc_lengths = draw_doc_lengths(jax.random.fold_in(key_of[14], 71), 0)
    cotangent = gaussian(key_of[3], (MICRO, ROWS, LEN, D), 1.0, 6.0, ((1, 4), (2, 8)))
    ada_weight = gaussian(key_of[4], (D, 6 * D), D ** -0.5, 0.1875, ((0, 4),))
    ada_bias = gaussian(key_of[5], (6 * D,), 0.3, 1.75, ((0, 4),))
    qkv_weight = gaussian(key_of[6], (D, 3 * D), D ** -0.5, 0.1875, ((0, 4),))
    qv_bias = gaussian(key_of[7], (2, D), 0.05, 0.3125, ((1, 4),))
    proj_weight = gaussian(key_of[8], (D, D), (max(D // 128, 2)) ** -0.5, 2.0, ((0, 4),))
    proj_bias = gaussian(key_of[9], (D,), 0.3, 1.75, ((0, 4),))
    fc1_weight = gaussian(key_of[10], (D, FF), D ** -0.5, 0.1875, ((0, 4),))
    fc1_bias = gaussian(key_of[11], (FF,), 0.5, 3.0, ((0, 4),))
    fc2_weight = gaussian(key_of[12], (FF, D), FF ** -0.5, 0.09375, ((0, 4),))
    fc2_bias = gaussian(key_of[13], (D,), 0.3, 1.75, ((0, 4),))
    return {"latents": latents, "conditions": conditions, "doc_lengths": doc_lengths, "cotangent": cotangent, "ada_weight": ada_weight, "ada_bias": ada_bias, "qkv_weight": qkv_weight, "qv_bias": qv_bias, "proj_weight": proj_weight, "proj_bias": proj_bias, "fc1_weight": fc1_weight, "fc1_bias": fc1_bias, "fc2_weight": fc2_weight, "fc2_bias": fc2_bias}


@jax.custom_vjp
def reduced_precision(v):
    return lax.optimization_barrier(v.astype(jnp.bfloat16)).astype(jnp.float32)

@jax.custom_vjp
def low_back(v):
    return v

def low_keep(v):
    return (reduced_precision(v), None)

def low_pass(kept, grad):
    return (grad,)

def back_keep(v):
    return (v, None)

def back_low(kept, grad):
    return (reduced_precision(grad),)
reduced_precision.defvjp(low_keep, low_pass)
low_back.defvjp(back_keep, back_low)
highest = lax.Precision.HIGHEST
masked_score = -1e+30

def hi_dot(left, right):
    return jnp.dot(left, right, precision=highest, preferred_element_type=jnp.float32)

def layer_normalizer(values):
    center = lax.optimization_barrier(jnp.mean(values, axis=-1, keepdims=True))
    centred = values - center
    return centred * lax.rsqrt(lax.optimization_barrier(jnp.mean(centred * centred, axis=-1, keepdims=True)) + 1e-06)

def gelu_tanh(values):
    return jax.nn.gelu(values, approximate=True)

def attention(query, keys, values, doc_of):
    q_block = math.gcd(LEN, 512)
    query_heads = query.reshape(LEN // q_block, q_block, HEADS, HEAD)
    key_heads = keys.reshape(LEN, HEADS, HEAD)
    value_heads = values.reshape(LEN, HEADS, HEAD)
    doc_blocks = doc_of.reshape(LEN // q_block, q_block)
    inv_root = HEAD ** (-0.5)

    def one_block(block_item):
        query_blk, doc_blk = block_item
        scores = jnp.einsum('qhd,khd->hqk', query_blk, key_heads, precision=highest) * inv_root
        scores = low_back(scores)
        allowed = (doc_blk[:, None] == doc_of[None, :])[None]
        scores = jnp.where(allowed, scores, masked_score)
        maxima = lax.optimization_barrier(jnp.max(scores, axis=-1, keepdims=True))
        weight = jnp.where(allowed, jnp.exp(scores - maxima), 0.0)
        totals = lax.optimization_barrier(jnp.sum(weight, axis=-1, keepdims=True))
        mixed = jnp.einsum('hqk,khd->qhd', reduced_precision(weight), value_heads, precision=highest)
        return mixed / jnp.transpose(totals, (1, 0, 2))
    blocks_out = lax.map(jax.checkpoint(one_block), (query_heads, doc_blocks))
    return blocks_out.reshape(LEN, HEADS * HEAD)

def row_forward(token_rows, conds, weights, lengths):
    ada_weight, ada_bias, qkv_weight, qv_bias, proj_weight, proj_bias, fc1_weight, fc1_bias, fc2_weight, fc2_bias = weights
    features = token_rows.shape[-1]
    doc_ends = jnp.cumsum(lengths)
    positions = jnp.arange(LEN, dtype=jnp.int32)
    doc_of = lax.optimization_barrier(jnp.sum((positions[:, None] >= doc_ends[None, :]).astype(jnp.int32), axis=1))
    doc_pick = (doc_of[:, None] == jnp.arange(DOCS, dtype=jnp.int32)[None, :]).astype(jnp.float32)
    mod_all = low_back(hi_dot(reduced_precision(jax.nn.silu(conds)), ada_weight) + ada_bias)
    token_broadcast = hi_dot(doc_pick, mod_all)
    selfattention_shift, selfattention_scale, selfattention_gate, feedforward_shift, feedforward_scale, feedforward_gate = jnp.split(token_broadcast, 6, axis=-1)
    attention_input = reduced_precision(layer_normalizer(token_rows) * (1.0 + selfattention_scale) + selfattention_shift)
    proj_qkv = hi_dot(attention_input, qkv_weight)
    query = reduced_precision(low_back(proj_qkv[:, :features] + qv_bias[0]))
    keys = reduced_precision(low_back(proj_qkv[:, features:2 * features]))
    values = reduced_precision(low_back(proj_qkv[:, 2 * features:] + qv_bias[1]))
    attn_out = attention(query, keys, values, doc_of)
    attn_low = reduced_precision(low_back(attn_out))
    attention_projection = low_back(hi_dot(attn_low, proj_weight) + proj_bias)
    middle_state = token_rows + selfattention_gate * attention_projection
    mlp_in = reduced_precision(layer_normalizer(middle_state) * (1.0 + feedforward_scale) + feedforward_shift)
    fc1_out = low_back(hi_dot(mlp_in, fc1_weight) + fc1_bias)
    act_low = reduced_precision(gelu_tanh(fc1_out))
    fc2_out = low_back(hi_dot(act_low, fc2_weight) + fc2_bias)
    return middle_state + feedforward_gate * fc2_out

def reference(latents, conditions, doc_lengths, cotangent, ada_weight, ada_bias, qkv_weight, qv_bias, proj_weight, proj_bias, fc1_weight, fc1_bias, fc2_weight, fc2_bias):
    weights = tuple((param.astype(jnp.float32) for param in (ada_weight, ada_bias, qkv_weight, qv_bias, proj_weight, proj_bias, fc1_weight, fc1_bias, fc2_weight, fc2_bias)))
    row_total = MICRO * ROWS
    rows_x = latents.astype(jnp.float32).reshape(row_total, LEN, D)
    rows_c = conditions.astype(jnp.float32).reshape(row_total, DOCS, D)
    rows_l = doc_lengths.reshape(row_total, DOCS)
    rows_t = cotangent.astype(jnp.float32).reshape(row_total, LEN, D)

    def row_step(grad_sum, row_item):
        token_rows, conds, lengths, seeds = row_item

        def forward(tok_in, cond_in, weight_in):
            return row_forward(tok_in, cond_in, weight_in, lengths)
        result_out, pull = jax.vjp(forward, token_rows, conds, weights)
        grad_tok, grad_cond, grad_weights = pull(seeds)
        grad_sum = jax.tree.map(jnp.add, grad_sum, grad_weights)
        return (grad_sum, (result_out.astype(jnp.bfloat16), grad_tok, grad_cond))
    zeros_start = tuple((jnp.zeros_like(param) for param in weights))
    grad_sum, (outs_all, grads_x, grads_c) = lax.scan(row_step, zeros_start, (rows_x, rows_c, rows_l, rows_t))
    block_out = outs_all.reshape(MICRO, ROWS, LEN, D)
    latent_grad = grads_x.reshape(MICRO, ROWS, LEN, D)
    cond_grad = grads_c.reshape(MICRO, ROWS, DOCS, D)
    return (block_out, latent_grad, cond_grad, grad_sum[0], grad_sum[1], grad_sum[2], grad_sum[3], grad_sum[4], grad_sum[5], grad_sum[6], grad_sum[7], grad_sum[8], grad_sum[9])
```

```python
import functools

import jax
import jax.numpy as jnp
from jax import lax
from jax.experimental import pallas as pl
from jax.experimental.pallas import tpu as pltpu
from jax.sharding import PartitionSpec as P

HEADS = 16
HEAD = 72
DOCS = 4
NORM_EPS = 1e-06
MASKED = -1e30
LOG2E = 1.4426950408889634
SCALE = HEAD ** (-0.5)
VMEM_LIMIT = 56 * 1024 * 1024
HIGHEST = lax.Precision.HIGHEST
BF = jnp.bfloat16
F32 = jnp.float32


def normalize(values):
    center = jnp.mean(values, axis=-1, keepdims=True)
    centred = values - center
    inverse = lax.rsqrt(jnp.mean(centred * centred, axis=-1, keepdims=True) + NORM_EPS)
    return centred * inverse, inverse


def normalize_back(grad, normed, inverse):
    first = jnp.mean(grad, axis=-1, keepdims=True)
    second = jnp.mean(grad * normed, axis=-1, keepdims=True)
    return inverse * (grad - first - normed * second)


def dot_nn(a, b):
    return lax.dot_general(a, b, (((1,), (0,)), ((), ())), preferred_element_type=F32)


def dot_nt(a, b):
    return lax.dot_general(a, b, (((1,), (1,)), ((), ())), preferred_element_type=F32)


def dot_tn(a, b):
    return lax.dot_general(a, b, (((0,), (0,)), ((), ())), preferred_element_type=F32)


def swap(x, axis, mask):
    count = lax.axis_size(axis)
    return lax.ppermute(x, axis, [(i, i ^ mask) for i in range(count)])


def bits_of(low, high):
    out = []
    while low < high:
        out.append(low)
        low *= 2
    return out


def spread_dp(x):
    n = lax.axis_size("dp")
    blocks = {0: x}
    if n == 4:
        cut = x.shape[0] // 2
        blocks[1] = swap(x, "dp", 1)
        blocks[2] = swap(x, "dp", 2)
        upper = swap(blocks[1][:cut], "dp", 2)
        lower = swap(blocks[2][cut:], "dp", 1)
        blocks[3] = jnp.concatenate([upper, lower], axis=0)
        return blocks
    for bit in bits_of(1, n):
        for mask in list(blocks):
            blocks[mask | bit] = swap(blocks[mask], "dp", bit)
    return blocks


def collect_dp(blocks):
    n = lax.axis_size("dp")

    def add(a, b):
        return (a.astype(F32) + b.astype(F32)).astype(BF)

    if n == 4:
        cut = blocks[3].shape[0] // 2
        r1 = swap(blocks[3][:cut], "dp", 1)
        r2 = swap(blocks[3][cut:], "dp", 2)
        b2 = jnp.concatenate([add(blocks[2][:cut], r1), blocks[2][cut:]], axis=0)
        b1 = jnp.concatenate([blocks[1][:cut], add(blocks[1][cut:], r2)], axis=0)
        s1 = swap(b1, "dp", 1)
        s2 = swap(b2, "dp", 2)
        return blocks[0].astype(F32) + s1.astype(F32) + s2.astype(F32)
    blocks = dict(blocks)
    for bit in reversed(bits_of(1, n)):
        for mask in [m for m in blocks if m & bit]:
            blocks[mask ^ bit] = add(blocks[mask ^ bit], swap(blocks.pop(mask), "dp", bit))
    return blocks[0].astype(F32)


def direct(blocks, axis):
    return {m: (b if m == 0 else swap(b, axis, m)) for m, b in blocks.items()}


def spread_group(x, group):
    blocks = {0: x}
    for bit in bits_of(2, group):
        for mask in list(blocks):
            blocks[mask | bit] = swap(blocks[mask], "blk", bit)
    for mask in list(blocks):
        blocks[mask | 1] = swap(blocks[mask], "blk", 1)
    return blocks


def collect_group(blocks, group):
    blocks = dict(blocks)
    for mask in [m for m in blocks if m & 1]:
        got = swap(blocks.pop(mask), "blk", 1)
        blocks[mask ^ 1] = (blocks[mask ^ 1].astype(F32) + got.astype(F32)).astype(BF)
    for bit in reversed(bits_of(2, group)):
        for mask in [m for m in blocks if m & bit]:
            got = swap(blocks.pop(mask), "blk", bit)
            total = blocks[mask ^ bit].astype(F32) + got.astype(F32)
            blocks[mask ^ bit] = total if bit == 2 and group > 2 else total.astype(BF)
    return blocks[0].astype(F32)


def sum_line(x):
    count = lax.axis_size("blk")
    chips = count // 2
    place = lax.axis_index("blk") // 2
    mid = chips // 2

    def both(pairs):
        return [(2 * a + c, 2 * b + c) for a, b in pairs for c in range(2)]

    def add(a, b):
        return (a.astype(F32) + b.astype(F32)).astype(BF)

    for s in range(mid - 1):
        x = add(x, lax.ppermute(x, "blk", both([(s, s + 1), (chips - 1 - s, chips - 2 - s)])))
    x = add(x, lax.ppermute(x, "blk", both([(mid - 1, mid), (mid, mid - 1)])))
    for s in range(mid - 1):
        low, high = mid - 1 - s, mid + s
        got = lax.ppermute(x, "blk", both([(low, low - 1), (high, high + 1)]))
        x = jnp.where((place == low - 1) | (place == high + 1), got, x)
    return x


def in_order(blocks, mine):
    stack = jnp.stack([blocks[m] for m in range(len(blocks))])
    return [lax.dynamic_index_in_dim(stack, k ^ mine, 0, False) for k in range(len(blocks))]


def rows_in_order(blocks, mine):
    size = blocks[0].shape[0]
    out = jnp.zeros((size * len(blocks),) + blocks[0].shape[1:], blocks[0].dtype)
    for m in range(len(blocks)):
        out = lax.dynamic_update_slice_in_dim(out, blocks[m], (m ^ mine) * size, 0)
    return out


def allowed_mask(dock_ref, docq_ref, width):
    keys = dock_ref[...]
    keys = jnp.concatenate([keys] * (width // keys.shape[1]), axis=1)
    return keys == docq_ref[...]


def attend_kernel(hpd, block, qkv_ref, docq_ref, dock_ref, out_ref, outt_ref, peak_ref, vt_ref):
    i = pl.program_id(0)
    width = hpd * HEAD
    rows = pl.ds(pl.multiple_of(i * block, block), block)

    @pl.when(i == 0)
    def _():
        for h in range(hpd):
            v = qkv_ref[:, 2 * width + h * HEAD : 2 * width + (h + 1) * HEAD]
            vt_ref[h] = v.astype(F32).T.astype(BF)

    allowed = allowed_mask(dock_ref, docq_ref, block)
    outs, peaks = [], []
    for h in range(hpd):
        q = qkv_ref[rows, h * HEAD : (h + 1) * HEAD]
        k = qkv_ref[:, width + h * HEAD : width + (h + 1) * HEAD]
        scores = jnp.where(allowed, dot_nt(k, q), MASKED)
        peak = jnp.max(scores, axis=0, keepdims=True)
        weight = jnp.exp2((scores - peak) * (SCALE * LOG2E))
        total = jnp.sum(weight, axis=0, keepdims=True)
        outs.append(dot_nn(vt_ref[h], weight.astype(BF)) / total)
        peaks.append(peak + jnp.log(total) * (1.0 / SCALE))
    out = jnp.concatenate(outs, axis=0)
    outt_ref[...] = out
    out_ref[...] = out.T.astype(BF)
    peaks.append(jnp.zeros((8 - hpd, block), F32))
    peak_ref[...] = jnp.concatenate(peaks, axis=0)


def attend_back_kernel(
    hpd, block, steps, qkv_ref, do_ref, outt_ref, peak_ref, docq_ref, dock_ref, grad_ref, kt_ref, dk_ref, dv_ref
):
    i = pl.program_id(0)
    width = hpd * HEAD
    rows = pl.ds(pl.multiple_of(i * block, block), block)

    @pl.when(i == 0)
    def _():
        for h in range(hpd):
            k = qkv_ref[:, width + h * HEAD : width + (h + 1) * HEAD]
            kt_ref[h] = k.astype(F32).T.astype(BF)
        dk_ref[...] = jnp.zeros_like(dk_ref)
        dv_ref[...] = jnp.zeros_like(dv_ref)

    allowed = allowed_mask(dock_ref, docq_ref, block)
    dots = do_ref[rows, :].astype(F32).T * outt_ref[...]
    dqs = []
    for h in range(hpd):
        part = slice(h * HEAD, (h + 1) * HEAD)
        q = qkv_ref[rows, part]
        k = qkv_ref[:, width + h * HEAD : width + (h + 1) * HEAD]
        v = qkv_ref[:, 2 * width + h * HEAD : 2 * width + (h + 1) * HEAD]
        do = do_ref[rows, part]
        row_dot = jnp.sum(dots[part], axis=0, keepdims=True)
        scores = jnp.where(allowed, dot_nt(k, q), MASKED)
        probs = jnp.exp2((scores - peak_ref[h : h + 1, :]) * (SCALE * LOG2E))
        grad_scores = (probs * (dot_nt(v, do) - row_dot)).astype(BF)
        dv_ref[h] += dot_nn(probs.astype(BF), do)
        dk_ref[h] += dot_nn(grad_scores, q)
        dqs.append(dot_nn(kt_ref[h], grad_scores))
    grad_ref[rows, :width] = (jnp.concatenate(dqs, axis=0) * SCALE).T.astype(BF)

    @pl.when(i == steps - 1)
    def _():
        dk = jnp.concatenate([dk_ref[h] for h in range(hpd)], axis=1) * SCALE
        dv = jnp.concatenate([dv_ref[h] for h in range(hpd)], axis=1)
        grad_ref[:, width : 2 * width] = dk.astype(BF)
        grad_ref[:, 2 * width :] = dv.astype(BF)


def params():
    return pltpu.CompilerParams(vmem_limit_bytes=VMEM_LIMIT, dimension_semantics=("arbitrary",))


def attend(qkv, docq, dock, hpd):
    length, width = qkv.shape[0], hpd * HEAD
    block = min(256, length)
    cost = pl.CostEstimate(
        flops=4 * length * length * hpd * 128, bytes_accessed=16 * length * width, transcendentals=length * length * hpd
    )
    return pl.pallas_call(
        functools.partial(attend_kernel, hpd, block),
        grid=(length // block,),
        in_specs=[
            pl.BlockSpec((length, 3 * width), lambda i: (0, 0)),
            pl.BlockSpec((1, block), lambda i: (0, i)),
            pl.BlockSpec((length, 128), lambda i: (0, 0)),
        ],
        out_specs=[
            pl.BlockSpec((block, width), lambda i: (i, 0)),
            pl.BlockSpec((width, block), lambda i: (0, i)),
            pl.BlockSpec((8, block), lambda i: (0, i)),
        ],
        out_shape=[
            jax.ShapeDtypeStruct((length, width), BF),
            jax.ShapeDtypeStruct((width, length), F32),
            jax.ShapeDtypeStruct((8, length), F32),
        ],
        scratch_shapes=[pltpu.VMEM((hpd, HEAD, length), BF)],
        compiler_params=params(),
        cost_estimate=cost,
        name="attend",
    )(qkv, docq, dock)


def attend_back(qkv, grad_out, outt, peak, docq, dock, hpd):
    length, width = qkv.shape[0], hpd * HEAD
    block = min(256, length)
    steps = length // block
    cost = pl.CostEstimate(
        flops=10 * length * length * hpd * 128, bytes_accessed=20 * length * width, transcendentals=length * length * hpd
    )
    return pl.pallas_call(
        functools.partial(attend_back_kernel, hpd, block, steps),
        grid=(steps,),
        in_specs=[
            pl.BlockSpec((length, 3 * width), lambda i: (0, 0)),
            pl.BlockSpec((length, width), lambda i: (0, 0)),
            pl.BlockSpec((width, block), lambda i: (0, i)),
            pl.BlockSpec((8, block), lambda i: (0, i)),
            pl.BlockSpec((1, block), lambda i: (0, i)),
            pl.BlockSpec((length, 128), lambda i: (0, 0)),
        ],
        out_specs=pl.BlockSpec((length, 3 * width), lambda i: (0, 0)),
        out_shape=jax.ShapeDtypeStruct((length, 3 * width), BF),
        scratch_shapes=[
            pltpu.VMEM((hpd, HEAD, length), BF),
            pltpu.VMEM((hpd, length, HEAD), F32),
            pltpu.VMEM((hpd, length, HEAD), F32),
        ],
        compiler_params=params(),
        cost_estimate=cost,
        name="attend_back",
    )(qkv, grad_out, outt, peak, docq, dock)


def mlp_kernel(x_ref, g_ref, w1_ref, b1_ref, w2_ref, act_ref, gf1_ref, part_ref, back_ref):
    u = dot_nn(x_ref[...], w1_ref[...]) + b1_ref[...]
    root = 0.7978845608028654
    squared = u * u
    t = jnp.tanh(root * u * (1.0 + 0.044715 * squared))
    act = (0.5 * u * (1.0 + t)).astype(BF)
    slope = 0.5 * (1.0 + t) + 0.5 * u * (1.0 - t * t) * (root * (1.0 + 3 * 0.044715 * squared))
    gf1 = (dot_nt(g_ref[...], w2_ref[...]) * slope).astype(BF)
    act_ref[...] = act
    gf1_ref[...] = gf1
    back_ref[...] = dot_nt(gf1, w1_ref[...]).astype(BF)
    part_ref[...] = dot_nn(act, w2_ref[...]).astype(BF)


def mlp(x, g, w1, b1, w2):
    tokens, features = x.shape
    hidden = w1.shape[1]
    block = 256
    cost = pl.CostEstimate(
        flops=8 * tokens * features * hidden, bytes_accessed=8 * tokens * features, transcendentals=tokens * hidden
    )
    return pl.pallas_call(
        mlp_kernel,
        grid=(tokens // block,),
        in_specs=[
            pl.BlockSpec((block, features), lambda i: (i, 0)),
            pl.BlockSpec((block, features), lambda i: (i, 0)),
            pl.BlockSpec((features, hidden), lambda i: (0, 0)),
            pl.BlockSpec((1, hidden), lambda i: (0, 0)),
            pl.BlockSpec((hidden, features), lambda i: (0, 0)),
        ],
        out_specs=[
            pl.BlockSpec((block, hidden), lambda i: (i, 0)),
            pl.BlockSpec((block, hidden), lambda i: (i, 0)),
            pl.BlockSpec((block, features), lambda i: (i, 0)),
            pl.BlockSpec((block, features), lambda i: (i, 0)),
        ],
        out_shape=[
            jax.ShapeDtypeStruct((tokens, hidden), BF),
            jax.ShapeDtypeStruct((tokens, hidden), BF),
            jax.ShapeDtypeStruct((tokens, features), BF),
            jax.ShapeDtypeStruct((tokens, features), BF),
        ],
        compiler_params=params(),
        cost_estimate=cost,
        name="mlp",
    )(x, g, w1, b1, w2)


def place_qkv_kernel(group, rows, parts_ref, mine_ref, out_ref, bias_ref):
    mine = mine_ref[0]
    size = parts_ref.shape[2] // 3
    for j in range(group):
        got = parts_ref[j ^ mine].astype(F32)
        for p in range(3):
            at = p * group * size + j * size
            out_ref[:, at : at + size] = got[:rows, p * size : (p + 1) * size]
            bias_ref[:, at : at + size] = got[rows : rows + 8, p * size : (p + 1) * size]


def place_qkv(parts, mine, rows):
    group, total, width = parts.shape
    return pl.pallas_call(
        functools.partial(place_qkv_kernel, group, rows),
        in_specs=[pl.BlockSpec(memory_space=pltpu.VMEM), pl.BlockSpec(memory_space=pltpu.SMEM)],
        out_specs=[pl.BlockSpec(memory_space=pltpu.VMEM), pl.BlockSpec(memory_space=pltpu.VMEM)],
        out_shape=[
            jax.ShapeDtypeStruct((rows, group * width), F32),
            jax.ShapeDtypeStruct((8, group * width), F32),
        ],
        compiler_params=pltpu.CompilerParams(vmem_limit_bytes=VMEM_LIMIT),
        name="place_qkv",
    )(parts, jnp.reshape(mine, (1,)).astype(jnp.int32))


def local(
    latents,
    conditions,
    doc_lengths,
    cotangent,
    ada_weight,
    ada_bias,
    qkv_weight,
    qv_bias,
    proj_weight,
    proj_bias,
    fc1_weight,
    fc1_bias,
    fc2_weight,
    fc2_bias,
):
    n_dp, n_blk = lax.axis_size("dp"), lax.axis_size("blk")
    dp, blk = lax.axis_index("dp"), lax.axis_index("blk")
    half = n_blk // 2
    group = half
    core, micro, place = blk % 2, blk // half, blk % half
    seg, features = latents.shape[2], latents.shape[3]
    hidden = fc1_weight.shape[1]
    dshard = features // n_dp
    hpd = HEADS // group
    width = hpd * HEAD
    fslice = hidden // (2 * n_dp)
    hshard = dshard // 2

    def pick(x, index):
        return lax.dynamic_index_in_dim(x, index, 0, False)

    def rows_of(x, start, size):
        return lax.dynamic_slice_in_dim(x, start, size, 0)

    def take_row(x):
        other = swap(pick(x, 1 - micro)[0], "blk", half)
        return jnp.concatenate([pick(x, micro)[0], other], axis=0)

    latent = take_row(latents).astype(F32)
    cot = take_row(cotangent).astype(F32)

    ends = jnp.cumsum(pick(doc_lengths, micro)[0])

    def docs_at(index):
        spot = jnp.arange(seg, dtype=jnp.int32)
        spots = jnp.concatenate([index * seg + spot, (index ^ half) * seg + spot])
        return jnp.sum((spots[:, None] >= ends[None, :]).astype(jnp.int32), axis=1)

    cond = conditions[:, 0].astype(F32)
    cond_act = jax.nn.silu(cond).astype(BF).reshape(2 * DOCS, features)
    cond_from = direct({m: cond_act for m in range(n_dp)}, "dp")
    biases = jnp.concatenate([ada_bias, proj_bias, fc2_bias, qv_bias[0], qv_bias[1]])[None]
    biases = in_order(direct({m: biases for m in range(n_dp)}, "dp"), dp)
    cuts = [0, ada_bias.shape[0], dshard, dshard, dshard, dshard]
    cuts = [sum(cuts[: i + 1]) for i in range(len(cuts))]
    ada_b, proj_b, fc2_b, q_b, v_b = (
        jnp.concatenate([b[:, cuts[i] : cuts[i + 1]] for b in biases], axis=1).astype(F32) for i in range(5)
    )
    my_cond = {
        m: lax.dynamic_slice(c, (0, dp * dshard), (2 * DOCS, dshard)) for m, c in cond_from.items()
    }
    cond_cols = jnp.concatenate([my_cond[m] for m in range(n_dp)], axis=0)
    cond_rows = jnp.concatenate([rows_of(my_cond[m], micro * DOCS, DOCS) for m in range(n_dp)], axis=0)
    mod_part = dot_nn(cond_rows, ada_weight)
    mod_from = direct({m: mod_part[m * DOCS : (m + 1) * DOCS] for m in range(n_dp)}, "dp")
    mod_all = sum(mod_from[m] for m in range(n_dp)) + ada_b

    my_docs = docs_at(blk)
    doc_pick = (my_docs[:, None] == jnp.arange(DOCS, dtype=jnp.int32)[None, :]).astype(F32)

    def mod(k):
        piece = mod_all[:, k * features : (k + 1) * features]
        return sum(doc_pick[:, d : d + 1] * piece[d : d + 1] for d in range(DOCS))

    qkv_cols = jnp.concatenate(
        [
            lax.dynamic_slice(qkv_weight, (0, p * features + place * width), (dshard, width))
            for p in range(3)
        ],
        axis=1,
    )
    qkv_w = rows_in_order(spread_dp(qkv_cols), dp)
    q_bias = lax.dynamic_slice(q_b, (0, place * width), (1, width))
    v_bias = lax.dynamic_slice(v_b, (0, place * width), (1, width))
    qkv_bias = jnp.concatenate([q_bias, jnp.zeros_like(q_bias), v_bias], axis=1)

    proj_mine = spread_dp(rows_of(proj_weight, core * hshard, hshard))
    proj_w = jnp.zeros((n_dp, 2, hshard, features), BF)
    for m, b in proj_mine.items():
        pair = swap(b, "blk", 1)
        proj_w = lax.dynamic_update_slice(proj_w, b[None, None], (dp ^ m, core, 0, 0))
        proj_w = lax.dynamic_update_slice(proj_w, pair[None, None], (dp ^ m, 1 - core, 0, 0))
    proj_w = proj_w.reshape(features, features)
    proj_x = jnp.concatenate([rows_of(proj_w, (place ^ m) * width, width) for m in range(group)], axis=0)

    fc1_w = rows_in_order(
        direct(
            {
                m: lax.dynamic_slice(fc1_weight, (0, ((dp ^ m) * 2 + core) * fslice), (dshard, fslice))
                for m in range(n_dp)
            },
            "dp",
        ),
        dp,
    )
    fc1_b = lax.dynamic_slice(fc1_bias, (core * fslice,), (fslice,)).astype(F32)[None]
    fc2_w = rows_of(fc2_weight, core * fslice, fslice)

    normed, inverse = normalize(latent)
    attn_in = (normed * (1.0 + mod(1)) + mod(0)).astype(BF)
    grad_fc2 = (mod(5) * cot).astype(BF)
    row_in = spread_group(attn_in, group)
    row_in = jnp.concatenate([row_in[m] for m in range(group)], axis=0)
    row_docs = jnp.concatenate([docs_at(blk ^ m) for m in range(group)])
    docq = row_docs[None, :]
    dock = jnp.broadcast_to(row_docs[:, None], (row_docs.shape[0], 128))
    qkv = (dot_nn(row_in, qkv_w) + qkv_bias).astype(BF)
    out, outt, peak = attend(qkv, docq, dock, hpd)
    tokens = 2 * seg
    got = direct({m: out[m * tokens : (m + 1) * tokens] for m in range(group)}, "blk")
    attn_low = jnp.concatenate([got[m] for m in range(group)], axis=1)
    attn_proj = dot_nn(attn_low, proj_x) + proj_b
    mid = latent + mod(2) * attn_proj

    mid_normed, mid_inverse = normalize(mid)
    mlp_in = (mid_normed * (1.0 + mod(4)) + mod(3)).astype(BF)

    def spread_tokens(x):
        blocks = spread_dp(x)
        mine = jnp.concatenate([blocks[m] for m in range(n_dp)], axis=0)
        return jnp.concatenate([mine, swap(mine, "blk", 1)], axis=0)

    def collect_tokens(x):
        count = x.shape[0] // 2
        mine = x[:count].astype(F32) + swap(x[count:], "blk", 1).astype(F32)
        mine = mine.astype(BF)
        return collect_dp({m: mine[m * tokens : (m + 1) * tokens] for m in range(n_dp)})

    all_grad = spread_tokens(grad_fc2)
    all_in = spread_tokens(mlp_in)
    act, grad_fc1, fc2_part, mlp_back = mlp(all_in, all_grad, fc1_w, fc1_b, fc2_w)
    grad_mlp_in = collect_tokens(mlp_back)

    grad_mid = cot + normalize_back(grad_mlp_in * (1.0 + mod(4)), mid_normed, mid_inverse)
    grad_proj = (mod(2) * grad_mid).astype(BF)
    grad_attn = direct(
        {m: dot_nt(grad_proj, proj_x[m * width : (m + 1) * width]).astype(BF) for m in range(group)}, "blk"
    )
    grad_attn = jnp.concatenate([grad_attn[m] for m in range(group)], axis=0)
    grad_qkv = attend_back(qkv, grad_attn, outt, peak, docq, dock, hpd)
    attn_back = dot_nt(grad_qkv, qkv_w).astype(BF)
    grad_attn_in = collect_group({m: attn_back[m * tokens : (m + 1) * tokens] for m in range(group)}, group)
    latent_grad = grad_mid + normalize_back(grad_attn_in * (1.0 + mod(1)), normed, inverse)

    fc2_out = collect_tokens(fc2_part) + fc2_b
    block_out = (mid + mod(5) * fc2_out).astype(BF)

    def hand_back(x):
        other = swap(x[seg:].astype(BF), "blk", half).astype(x.dtype)
        both = jnp.stack([x[:seg], other])
        return jnp.where(micro == 0, both, both[::-1])[:, None]

    block_out = hand_back(block_out)
    latent_grad = hand_back(latent_grad)

    def extra_rows(rows, count=16):
        return jnp.pad(rows, ((0, count - rows.shape[0]), (0, 0))).astype(BF)

    fc2_bsum = jnp.sum(all_grad.astype(F32), axis=0, keepdims=True)
    fc1_bsum = jnp.sum(grad_fc1.astype(F32), axis=0, keepdims=True)
    both_b = jnp.concatenate([fc2_bsum, jnp.pad(fc1_bsum, ((0, 0), (0, features - fslice)))], axis=0)
    fc2_g = jnp.concatenate([dot_tn(act, all_grad).astype(BF), extra_rows(both_b)], axis=0)
    fc2_g = sum_line(fc2_g)

    fc1_g = dot_tn(all_in, grad_fc1).astype(BF).reshape(n_dp, dshard, fslice)
    fc1_g = direct({m: pick(fc1_g, dp ^ m) for m in range(n_dp)}, "dp")
    fc1_g = sum_line(jnp.concatenate([fc1_g[m] for m in range(n_dp)], axis=0))

    def core_pair(x):
        got = swap(x, "blk", 1)
        return jnp.where(core == 0, x, got), jnp.where(core == 0, got, x)

    fc2_lo, fc2_hi = core_pair(fc2_g)
    fc2_wgrad = jnp.concatenate([fc2_lo[:fslice], fc2_hi[:fslice]], axis=0).astype(F32)
    fc2_bgrad = lax.dynamic_slice(fc2_lo[fslice].astype(F32), (dp * dshard,), (dshard,))
    fc1_bgrad = jnp.concatenate([fc2_lo[fslice + 1, :fslice], fc2_hi[fslice + 1, :fslice]]).astype(F32)
    fc1_lo, fc1_hi = core_pair(fc1_g)
    fc1_wgrad = jnp.zeros((dshard, hidden), F32)
    for m in range(n_dp):
        rows = slice(m * dshard, (m + 1) * dshard)
        piece = jnp.concatenate([fc1_lo[rows], fc1_hi[rows]], axis=1).astype(F32)
        fc1_wgrad = lax.dynamic_update_slice(fc1_wgrad, piece, (0, (dp ^ m) * 2 * fslice))

    proj_g = dot_tn(attn_low, grad_proj).astype(BF).reshape(group, width, features)
    proj_g = jnp.concatenate([pick(proj_g, k ^ place) for k in range(group)], axis=0)
    proj_bsum = extra_rows(jnp.sum(grad_proj.astype(F32), axis=0, keepdims=True))
    proj_g = proj_g.reshape(n_dp, 2, hshard, features)
    proj_g = jnp.concatenate(
        [proj_g, jnp.broadcast_to(proj_bsum[None, None], (n_dp, 2) + proj_bsum.shape)], axis=2
    )
    keep = lax.dynamic_index_in_dim(proj_g, core, 1, False)
    send = lax.dynamic_index_in_dim(proj_g, 1 - core, 1, False)
    proj_g = (keep.astype(F32) + swap(send, "blk", 1).astype(F32)).astype(BF)
    proj_g = collect_dp({m: pick(proj_g, dp ^ m) for m in range(n_dp)}).astype(BF)
    proj_g = sum_line(proj_g)
    proj_lo, proj_hi = core_pair(proj_g)
    proj_wgrad = jnp.concatenate([proj_lo[:hshard], proj_hi[:hshard]], axis=0).astype(F32)
    proj_bgrad = lax.dynamic_slice(proj_lo[hshard].astype(F32), (dp * dshard,), (dshard,))

    qkv_bsum = extra_rows(jnp.sum(grad_qkv.astype(F32), axis=0, keepdims=True))
    qkv_g = dot_tn(row_in, grad_qkv).astype(BF).reshape(n_dp, dshard, 3 * width)
    qkv_g = collect_dp(
        {m: jnp.concatenate([pick(qkv_g, dp ^ m), qkv_bsum], axis=0) for m in range(n_dp)}
    ).astype(BF)
    qkv_g = (qkv_g.astype(F32) + swap(qkv_g, "blk", half).astype(F32)).astype(BF)
    qkv_g = spread_group(qkv_g, group)
    qkv_wgrad, qkv_rows = place_qkv(jnp.stack([qkv_g[m] for m in range(group)]), place, dshard)
    qv_bgrad = jnp.stack(
        [
            lax.dynamic_slice(qkv_rows[0], (p * features + dp * dshard,), (dshard,))
            for p in (0, 2)
        ]
    )

    grad_tok = jnp.concatenate(
        [
            grad_attn_in,
            grad_attn_in * normed,
            grad_mid * attn_proj,
            grad_mlp_in,
            grad_mlp_in * mid_normed,
            cot * fc2_out,
        ],
        axis=1,
    )
    grad_mod = lax.dot_general(
        doc_pick, grad_tok, (((0,), (0,)), ((), ())), precision=HIGHEST, preferred_element_type=F32
    )
    for bit in bits_of(1, group):
        grad_mod = grad_mod + swap(grad_mod, "blk", bit)
    grad_mod = grad_mod.astype(BF)
    other = swap(grad_mod, "blk", half)
    both = jnp.where(micro == 0, jnp.concatenate([grad_mod, other]), jnp.concatenate([other, grad_mod]))
    slots = direct({m: both for m in range(n_dp)}, "dp")
    slots = jnp.concatenate([slots[m] for m in range(n_dp)], axis=0)
    ada_wgrad = dot_tn(cond_cols, slots)
    ada_bgrad = jnp.sum(slots.astype(F32), axis=0)
    ada_bgrad = lax.dynamic_slice(ada_bgrad, (dp * ada_bias.shape[0],), ada_bias.shape)
    cond_part = dot_nt(slots, ada_weight)
    count = 2 * DOCS
    cond_got = in_order(direct({m: cond_part[m * count : (m + 1) * count] for m in range(n_dp)}, "dp"), dp)
    cond_act_grad = jnp.concatenate(cond_got, axis=1).reshape(2, 1, DOCS, features)
    sig = jax.nn.sigmoid(cond)[:, None]
    cond_grad = cond_act_grad * (sig * (1.0 + cond[:, None] * (1.0 - sig)))

    return (
        block_out,
        latent_grad,
        cond_grad,
        ada_wgrad,
        ada_bgrad,
        qkv_wgrad,
        qv_bgrad,
        proj_wgrad,
        proj_bgrad,
        fc1_wgrad,
        fc1_bgrad,
        fc2_wgrad,
        fc2_bgrad,
    )


def solution(mesh):
    in_specs = (
        P(None, "dp", "blk", None),
        P(None, "dp", None, None),
        P(None, "dp", None),
        P(None, "dp", "blk", None),
        P("dp", None),
        P("dp"),
        P("dp", None),
        P(None, "dp"),
        P("dp", None),
        P("dp"),
        P("dp", None),
        P("dp"),
        P("dp", None),
        P("dp"),
    )
    out_specs = (
        P(None, "dp", "blk", None),
        P(None, "dp", "blk", None),
        P(None, "dp", None, None),
        P("dp", None),
        P("dp"),
        P("dp", None),
        P(None, "dp"),
        P("dp", None),
        P("dp"),
        P("dp", None),
        P("dp"),
        P("dp", None),
        P("dp"),
    )
    return jax.shard_map(local, mesh=mesh, in_specs=in_specs, out_specs=out_specs, check_vma=False)
```

```python
import functools
import math
import types

import jax
import jax.numpy as jnp
from jax import lax
from jax.experimental import pallas as pl
from jax.experimental.pallas import tpu as pltpu
from jax.sharding import PartitionSpec as P

HEADS = 16
HEAD = 72
DOCS = 4
NORM_EPS = 1e-06
MASKED = -1e30
LOG2E = 1.4426950408889634
SCALE = HEAD ** (-0.5)
VMEM_LIMIT = 56 * 1024 * 1024
HIGHEST = lax.Precision.HIGHEST
BF = jnp.bfloat16
F32 = jnp.float32


def normalize(values):
    center = jnp.mean(values, axis=-1, keepdims=True)
    centred = values - center
    inverse = lax.rsqrt(jnp.mean(centred * centred, axis=-1, keepdims=True) + NORM_EPS)
    return centred * inverse, inverse


def normalize_back(grad, normed, inverse):
    first = jnp.mean(grad, axis=-1, keepdims=True)
    second = jnp.mean(grad * normed, axis=-1, keepdims=True)
    return inverse * (grad - first - normed * second)


def dot_nn(a, b):
    return lax.dot_general(a, b, (((1,), (0,)), ((), ())), preferred_element_type=F32)


def dot_nt(a, b):
    return lax.dot_general(a, b, (((1,), (1,)), ((), ())), preferred_element_type=F32)


def dot_tn(a, b):
    return lax.dot_general(a, b, (((0,), (0,)), ((), ())), preferred_element_type=F32)


def swap(x, axis, mask):
    count = lax.axis_size(axis)
    return lax.ppermute(x, axis, [(i, i ^ mask) for i in range(count)])


def bits_of(low, high):
    out = []
    while low < high:
        out.append(low)
        low *= 2
    return out


def direct(blocks, axis):
    return {m: (b if m == 0 else swap(b, axis, m)) for m, b in blocks.items()}


def spread_dp(x):
    n = lax.axis_size("dp")
    blocks = {0: [x]}
    if n == 4:
        cut = x.shape[0] // 2
        one, two = swap(x, "dp", 1), swap(x, "dp", 2)
        blocks[1], blocks[2] = [one], [two]
        blocks[3] = [swap(one[:cut], "dp", 2), swap(two[cut:], "dp", 1)]
        return [blocks[m] for m in range(n)]
    for bit in bits_of(1, n):
        for mask in list(blocks):
            blocks[mask | bit] = [swap(blocks[mask][0], "dp", bit)]
    return [blocks[m] for m in range(n)]


def line_pairs():
    chips = lax.axis_size("blk") // 2
    mid = chips // 2
    inward = [[(s, s + 1), (chips - 1 - s, chips - 2 - s)] for s in range(mid - 1)]
    outward = [[(mid - 1 - s, mid - 2 - s), (mid + s, mid + s + 1)] for s in range(mid - 1)]
    return inward, [(mid - 1, mid), (mid, mid - 1)], outward


def along(x, pairs):
    return lax.ppermute(x, "blk", [(2 * a + c, 2 * b + c) for a, b in pairs for c in range(2)])


class LineSum:
    def __init__(self, x, name):
        inward, middle, outward = line_pairs()
        self.steps = [("add", p) for p in inward] + [("add", middle)] + [("take", p) for p in outward]
        self.x, self.name, self.at = x, name, 0
        self.got = along(x, self.steps[0][1])

    def step(self):
        kind, pairs = self.steps[self.at]
        if kind == "add":
            self.x = sum_of([self.x, self.got], self.name)
        else:
            self.x = take_from(self.x, self.got, [b for _, b in pairs], self.name)
        self.at += 1
        if self.at < len(self.steps):
            self.got = along(self.x, self.steps[self.at][1])

    def until(self, left):
        while len(self.steps) - self.at > left:
            self.step()


class CubeSum:
    def __init__(self, keep, send, bits, name):
        self.x, self.bits, self.name = keep, bits, name
        self.got = swap(send, "blk", bits[0])

    def fold(self):
        for bit in self.bits[1:]:
            self.x, send = fold_sum([self.x, self.got], bit, self.name)
            self.got = swap(send, "blk", bit)

    def total(self):
        self.x = sum_of([self.x, self.got], self.name)
        self.got = swap(self.x, "blk", self.bits[-1])

    def join(self):
        for i in range(len(self.bits) - 1, 0, -1):
            self.x = join_rows(self.x, self.got, self.bits[i], self.name)
            self.got = swap(self.x, "blk", self.bits[i - 1])


def allowed_mask(dock_ref, docq_ref, width):
    keys = dock_ref[...]
    keys = jnp.concatenate([keys] * (width // keys.shape[1]), axis=1)
    return keys == docq_ref[...]


def attend_kernel(hpd, block, qkv_ref, docq_ref, dock_ref, out_ref, outt_ref, peak_ref, vt_ref):
    i = pl.program_id(0)
    width = hpd * HEAD
    rows = pl.ds(pl.multiple_of(i * block, block), block)

    @pl.when(i == 0)
    def _():
        for h in range(hpd):
            v = qkv_ref[:, 2 * width + h * HEAD : 2 * width + (h + 1) * HEAD]
            vt_ref[h] = v.astype(F32).T.astype(BF)

    allowed = allowed_mask(dock_ref, docq_ref, block)
    outs, peaks = [], []
    for h in range(hpd):
        q = qkv_ref[rows, h * HEAD : (h + 1) * HEAD]
        k = qkv_ref[:, width + h * HEAD : width + (h + 1) * HEAD]
        scores = jnp.where(allowed, dot_nt(k, q), MASKED)
        peak = jnp.max(scores, axis=0, keepdims=True)
        weight = jnp.exp2((scores - peak) * (SCALE * LOG2E))
        total = jnp.sum(weight, axis=0, keepdims=True)
        outs.append(dot_nn(vt_ref[h], weight.astype(BF)) / total)
        peaks.append(peak + jnp.log(total) * (1.0 / SCALE))
    out = jnp.concatenate(outs, axis=0)
    outt_ref[...] = out
    out_ref[...] = out.T.astype(BF)
    peaks.append(jnp.zeros((8 - hpd, block), F32))
    peak_ref[...] = jnp.concatenate(peaks, axis=0)


def attend_back_kernel(
    hpd, block, steps, qkv_ref, do_ref, outt_ref, peak_ref, docq_ref, dock_ref, grad_ref, kt_ref, dk_ref, dv_ref
):
    i = pl.program_id(0)
    width = hpd * HEAD
    rows = pl.ds(pl.multiple_of(i * block, block), block)

    @pl.when(i == 0)
    def _():
        for h in range(hpd):
            k = qkv_ref[:, width + h * HEAD : width + (h + 1) * HEAD]
            kt_ref[h] = k.astype(F32).T.astype(BF)
        dk_ref[...] = jnp.zeros_like(dk_ref)
        dv_ref[...] = jnp.zeros_like(dv_ref)

    allowed = allowed_mask(dock_ref, docq_ref, block)
    dots = do_ref[rows, :].astype(F32).T * outt_ref[...]
    dqs = []
    for h in range(hpd):
        part = slice(h * HEAD, (h + 1) * HEAD)
        q = qkv_ref[rows, part]
        k = qkv_ref[:, width + h * HEAD : width + (h + 1) * HEAD]
        v = qkv_ref[:, 2 * width + h * HEAD : 2 * width + (h + 1) * HEAD]
        do = do_ref[rows, part]
        row_dot = jnp.sum(dots[part], axis=0, keepdims=True)
        scores = jnp.where(allowed, dot_nt(k, q), MASKED)
        probs = jnp.exp2((scores - peak_ref[h : h + 1, :]) * (SCALE * LOG2E))
        grad_scores = (probs * (dot_nt(v, do) - row_dot)).astype(BF)
        dv_ref[h] += dot_nn(probs.astype(BF), do)
        dk_ref[h] += dot_nn(grad_scores, q)
        dqs.append(dot_nn(kt_ref[h], grad_scores))
    grad_ref[rows, :width] = (jnp.concatenate(dqs, axis=0) * SCALE).T.astype(BF)

    @pl.when(i == steps - 1)
    def _():
        dk = jnp.concatenate([dk_ref[h] for h in range(hpd)], axis=1) * SCALE
        dv = jnp.concatenate([dv_ref[h] for h in range(hpd)], axis=1)
        grad_ref[:, width : 2 * width] = dk.astype(BF)
        grad_ref[:, 2 * width :] = dv.astype(BF)


WORK = {"attend": 6, "attend_back": 8, "mlp": 4, "qkv_wgrad": 12, "mod_part": 8}


def params(name, grid, arrays, scratch):
    held = sum(a.size * a.dtype.itemsize for a in arrays) * (1 if grid is None or grid == (1,) else 2)
    held += sum(math.prod(x.shape) * jnp.dtype(x.dtype).itemsize for x in scratch)
    limit = min(VMEM_LIMIT, held + WORK.get(name, 6) * 1024 * 1024)
    return pltpu.CompilerParams(
        vmem_limit_bytes=limit, dimension_semantics=None if grid is None else ("arbitrary",)
    )


LIGHT = pl.CostEstimate(flops=1000, bytes_accessed=1000, transcendentals=0)
VM = pl.BlockSpec(memory_space=pltpu.VMEM)
SM = pl.BlockSpec(memory_space=pltpu.SMEM)
ANY = pl.BlockSpec(memory_space=pl.ANY)


def sds(shape, dtype):
    return jax.ShapeDtypeStruct(shape, dtype)


LAST = []


def launch(name, kernel, args, in_specs, out_specs, out_shape, scratch=(), grid=None):
    count, after = len(args), list(LAST)

    def body(*refs):
        kernel(*refs[:count], *refs[count + len(after) :])

    got = pl.pallas_call(
        body,
        **({} if grid is None else {"grid": grid}),
        in_specs=list(in_specs) + [ANY] * len(after),
        out_specs=list(out_specs),
        out_shape=list(out_shape),
        scratch_shapes=list(scratch),
        compiler_params=params(name, grid, list(args) + list(out_shape), scratch),
        cost_estimate=LIGHT,
        name=name,
    )(*args, *after)
    LAST[:] = [min(got, key=lambda a: a.size)]
    return got


def whole_call(kernel, name, outs, args, scratch=()):
    specs = [SM if a.dtype == jnp.int32 and a.ndim != 2 else VM for a in args]
    return launch(name, kernel, args, specs, [VM] * len(outs), outs, scratch)


CHUNK = 32


def by_rows(count, step):
    def inner(i, carry):
        step(pl.ds(pl.multiple_of(i * CHUNK, CHUNK), CHUNK))
        return carry

    lax.fori_loop(0, count // CHUNK, inner, 0, unroll=2)


def doc_sums(pick, grads):
    high = grads.astype(BF)
    low = (grads - high.astype(F32)).astype(BF)
    return dot_nn(pick, high) + dot_nn(pick, low)


def by_index(index, count, step):
    for i in range(count):

        @pl.when(index == i)
        def _():
            step(i)


def open_kernel(half, cond_ref, bias_ref, qv_ref, lat_ref, cot_ref, lengths_ref, *refs):
    pack_ref, lat_own, cot_own, send_ref, docq_ref, dock_ref, mod_ref, sum_ref = refs
    blk = lax.axis_index("blk")
    micro = blk // half
    group = half
    seg, features = lat_own.shape
    tokens = 2 * seg
    dshard = qv_ref.shape[1]
    cond = jnp.concatenate([cond_ref[0, 0], cond_ref[1, 0]], axis=0).astype(F32)
    silu = cond / (1.0 + jnp.exp(-cond))
    small = jnp.concatenate(
        [bias_ref[...].astype(F32).reshape(1, dshard), qv_ref[0:1, :].astype(F32), qv_ref[1:2, :].astype(F32)], axis=1
    )
    small = jnp.pad(small, ((0, 7), (0, features - 3 * dshard)))
    pack_ref[...] = jnp.concatenate([silu, small], axis=0).astype(BF)
    lat_own[...] = lat_ref[micro, 0]
    cot_own[...] = cot_ref[micro, 0]
    send_ref[:seg, :] = lat_ref[1 - micro, 0]
    send_ref[seg:, :] = cot_ref[1 - micro, 0]
    ends, last = [], 0
    for d in range(DOCS):
        last = last + lengths_ref[micro, 0, d]
        ends.append(last)

    def docs(index, shape, dim):
        spot = lax.broadcasted_iota(jnp.int32, shape, dim) + index * seg
        found = jnp.zeros(shape, jnp.int32)
        for d in range(DOCS):
            found = found + jnp.where(spot >= ends[d], 1, 0)
        return found

    for i in range(group):
        mask = 2 * (i % (group // 2)) + i // (group // 2)
        for part in range(2):
            at = i * tokens + part * seg
            index = (blk ^ mask) ^ (half * part)
            dock_ref[at : at + seg, :] = docs(index, (seg, 128), 0)
            docq_ref[:, at : at + seg] = docs(index, (8, seg), 1)[:1]
    for part in range(2):
        at = part * seg
        index = blk ^ (half * part)
        col = lax.broadcasted_iota(jnp.int32, (seg, 32), 1)
        same = (col % DOCS == docs(index, (seg, 32), 0)) & (col < 3 * DOCS)
        mod_ref[at : at + seg, :] = jnp.where(same, 1.0, 0.0).astype(BF)
        row = lax.broadcasted_iota(jnp.int32, (16, seg), 0)
        same = (row == docs(index, (16, seg), 1)) | (row == DOCS)
        sum_ref[:, at : at + seg] = jnp.where(same, 1.0, 0.0).astype(BF)


def qkv_cols_kernel(group, w_ref, out_ref):
    width = out_ref.shape[1] // 3

    def step(j):
        for p in range(3):
            at = p * group * width + j * width
            out_ref[:, p * width : (p + 1) * width] = w_ref[:, at : at + width]

    by_index(lax.axis_index("blk") % group, group, step)


def cuts_kernel(n, fc1_ref, proj_ref, *outs):
    core = lax.axis_index("blk") % 2
    size = outs[0].shape[0] // 2
    hidden = fc1_ref.shape[1] // n

    def half(ref, cols):
        return jnp.where(core == 0, ref[:size, cols], ref[size:, cols])

    def step(d):
        for m in range(n):
            outs[m][:size, :hidden] = half(fc1_ref, slice((d ^ m) * hidden, ((d ^ m) + 1) * hidden))

    by_index(lax.axis_index("dp"), n, step)
    for m in range(n):
        outs[m][size:, :] = half(proj_ref, slice(None))


def stack_kernel(n, *refs):
    for m in range(n):
        refs[-1][m] = refs[m][...]


def whole_rows(own_ref, other_ref, out_ref, rows, cols):
    dp, core = lax.axis_index("dp"), lax.axis_index("blk") % 2
    n, size = own_ref.shape[0], rows.stop - rows.start
    for k in range(n):
        own, other = own_ref[k ^ dp, rows, cols], other_ref[k ^ dp, rows, cols]
        out_ref[2 * k * size : (2 * k + 1) * size, :] = jnp.where(core == 0, own, other)
        out_ref[(2 * k + 1) * size : (2 * k + 2) * size, :] = jnp.where(core == 0, other, own)


def mod_part_kernel(n, group, *refs):
    packs = refs[:n]
    w_ref, bias_ref = refs[n : n + 2]
    parts = refs[n + 2 : 2 * n + 2]
    cols_ref, projb_ref, qkvb_ref, add_ref, slab_ref = refs[2 * n + 2 :]
    dp, blk = lax.axis_index("dp"), lax.axis_index("blk")
    micro = blk // group
    dshard, span = w_ref.shape[0], bias_ref.shape[0]
    features = dshard * n
    width = features // group
    add_ref[...] = jnp.zeros_like(add_ref)
    bias = jnp.broadcast_to(bias_ref[...].astype(F32).reshape(1, span), (8, span))

    def mine(d):
        add_ref[:, d * span : (d + 1) * span] = bias
        for m in range(n):
            cols_ref[8 * m : 8 * m + 8, :] = packs[m][:8, d * dshard : (d + 1) * dshard].astype(F32)

    by_index(dp, n, mine)
    lhs = []
    for m in range(n):
        slab_ref[m] = packs[m][8:16, :].astype(F32)
        low, high = cols_ref[8 * m : 8 * m + 4, :], cols_ref[8 * m + 4 : 8 * m + 8, :]
        lhs.append(jnp.where(micro == 0, low, high))
    product = dot_nn(jnp.concatenate(lhs, axis=0).astype(BF), w_ref[...])
    for m in range(n):
        parts[m][...] = product[4 * m : 4 * m + 4, :] + add_ref[:4, :]
    rows = [slab_ref[k ^ dp][:1] for k in range(n)]
    projb_ref[...] = jnp.concatenate([r[:, :dshard] for r in rows], axis=1)
    q_bias = jnp.concatenate([r[:, dshard : 2 * dshard] for r in rows], axis=1)
    v_bias = jnp.concatenate([r[:, 2 * dshard : 3 * dshard] for r in rows], axis=1)

    def step(j):
        part = slice(j * width, (j + 1) * width)
        qkvb_ref[...] = jnp.concatenate([q_bias[:, part], jnp.zeros((1, width), F32), v_bias[:, part]], axis=1)

    by_index(blk % group, group, step)


def mod_all_kernel(*refs):
    parts, out_ref = refs[:-1], refs[-1]
    total = parts[0][...]
    for p in parts[1:]:
        total = total + p[...]
    high = total.astype(BF).astype(F32)
    middle = (total - high).astype(BF).astype(F32)
    low = total - high - middle
    blank = jnp.zeros((32 - 3 * DOCS, total.shape[1]), F32)
    out_ref[...] = jnp.concatenate([high, middle, low, blank], axis=0).astype(BF)


def attn_in_kernel(own_ref, got_ref, pick_ref, mod_ref, out_ref, lat_ref, shift_ref, scale_ref):
    seg, features = own_ref.shape
    lat_ref[:seg, :] = own_ref[...]
    lat_ref[seg:, :] = got_ref[:seg, :]
    shift_ref[...] = dot_nn(pick_ref[...], mod_ref[:, :features])
    scale_ref[...] = dot_nn(pick_ref[...], mod_ref[:, features : 2 * features])

    def step(rows):
        normed, _ = normalize(lat_ref[rows, :].astype(F32))
        out_ref[rows, :] = (normed * (1.0 + scale_ref[rows, :]) + shift_ref[rows, :]).astype(BF)

    by_rows(lat_ref.shape[0], step)


def grad_fc2_kernel(own_ref, got_ref, pick_ref, pickt_ref, mod_ref, out_ref, cot_ref, sums_ref):
    seg, features = own_ref.shape
    cot_ref[:seg, :] = own_ref[...]
    cot_ref[seg:, :] = got_ref[seg:, :]
    gate = dot_nn(pick_ref[...], mod_ref[:, 5 * features : 6 * features])
    out_ref[...] = (gate * cot_ref[...].astype(F32)).astype(BF)
    sums_ref[...] = dot_nn(pickt_ref[...], out_ref[...])


def mix_kernel(group, *refs):
    outs = refs[:group]
    own, other, bias_ref, lat_ref, pick_ref, mod_ref = refs[group : group + 6]
    low_ref, proj_ref, mid_ref, in_ref, heads_ref, w_ref, slab_ref, gate_ref, shift_ref, scale_ref = refs[group + 6 :]
    features = lat_ref.shape[1]
    width = features // group
    mine = lax.axis_index("blk") % group
    size = own.shape[1] // 2
    whole_rows(own, other, w_ref, slice(size, 2 * size), slice(0, features))
    for k in range(group):
        heads_ref[k] = w_ref[k * width : (k + 1) * width, :]
    for m in range(group):
        slab_ref[m] = outs[m][...]
    low_ref[...] = jnp.concatenate([slab_ref[k ^ mine] for k in range(group)], axis=1)
    proj_ref[...] = dot_nn(low_ref[...], w_ref[...]) + bias_ref[...]
    gate_ref[...] = dot_nn(pick_ref[...], mod_ref[:, 2 * features : 3 * features])
    shift_ref[...] = dot_nn(pick_ref[...], mod_ref[:, 3 * features : 4 * features])
    scale_ref[...] = dot_nn(pick_ref[...], mod_ref[:, 4 * features : 5 * features])

    def step(rows):
        mid = lat_ref[rows, :].astype(F32) + gate_ref[rows, :] * proj_ref[rows, :]
        mid_ref[rows, :] = mid
        normed, _ = normalize(mid)
        in_ref[rows, :] = (normed * (1.0 + scale_ref[rows, :]) + shift_ref[rows, :]).astype(BF)

    by_rows(lat_ref.shape[0], step)


def turn_kernel(pieces, group, *refs):
    parts = refs[:pieces]
    cot_ref, mid_ref, proj_ref, heads_ref, pick_ref, pickt_ref, mod_ref = refs[pieces : pieces + 7]
    gmid_ref, gproj_ref, sums_ref = refs[pieces + 7 : pieces + 10]
    grads = refs[pieces + 10 : pieces + 10 + group]
    gate_ref, scale_ref, a_ref, b_ref, c_ref = refs[pieces + 10 + group :]
    features = cot_ref.shape[1]
    mine = lax.axis_index("blk") % group
    gate_ref[...] = dot_nn(pick_ref[...], mod_ref[:, 2 * features : 3 * features])
    scale_ref[...] = dot_nn(pick_ref[...], mod_ref[:, 4 * features : 5 * features])

    def step(rows):
        grad_in = parts[0][rows, :].astype(F32)
        for p in parts[1:]:
            grad_in = grad_in + p[rows, :].astype(F32)
        normed, inverse = normalize(mid_ref[rows, :])
        gmid = cot_ref[rows, :].astype(F32) + normalize_back(
            grad_in * (1.0 + scale_ref[rows, :]), normed, inverse
        )
        gmid_ref[rows, :] = gmid
        gproj_ref[rows, :] = (gate_ref[rows, :] * gmid).astype(BF)
        a_ref[rows, :] = gmid * proj_ref[rows, :]
        b_ref[rows, :] = grad_in
        c_ref[rows, :] = grad_in * normed

    by_rows(cot_ref.shape[0], step)
    for m in range(group):
        grads[m][...] = dot_nt(gproj_ref[...], heads_ref[m ^ mine]).astype(BF)
    pick = pickt_ref[...]
    sums_ref[:, :features] = doc_sums(pick, a_ref[...])
    sums_ref[:, features : 2 * features] = doc_sums(pick, b_ref[...])
    sums_ref[:, 2 * features : 3 * features] = doc_sums(pick, c_ref[...])
    sums_ref[:, 3 * features :] = dot_nn(pick, gproj_ref[...])


def outs_kernel(pieces, *refs):
    parts = refs[:pieces]
    cot_ref, mid_ref, pick_ref, pickt_ref, mod_ref, out_ref, low_ref, sums_ref, hold_ref, gate_ref, a_ref = refs[pieces:]
    features = cot_ref.shape[1]
    gate_ref[...] = dot_nn(pick_ref[...], mod_ref[:, 5 * features : 6 * features])

    def step(rows):
        fc2_out = parts[0][rows, :].astype(F32)
        for p in parts[1:]:
            fc2_out = fc2_out + p[rows, :].astype(F32)
        hold_ref[rows, :] = (mid_ref[rows, :] + gate_ref[rows, :] * fc2_out).astype(BF)
        a_ref[rows, :] = cot_ref[rows, :].astype(F32) * fc2_out

    by_rows(cot_ref.shape[0], step)
    seg = out_ref.shape[0]
    out_ref[...] = hold_ref[:seg, :]
    low_ref[...] = hold_ref[seg:, :]
    sums_ref[...] = doc_sums(pickt_ref[...], a_ref[...])


def finish_kernel(starts, seg, *refs):
    pieces = len(starts)
    parts = [r.at[at : at + 2 * seg, :] for r, at in zip(refs, starts)]
    lat_ref, gmid_ref, pick_ref, pickt_ref, mod_ref, out_ref, low_ref, sums_ref, scale_ref, b_ref, c_ref = refs[
        pieces:
    ]
    features = lat_ref.shape[1]
    scale_ref[...] = dot_nn(pick_ref[...], mod_ref[:, features : 2 * features])

    def rows_step(rows):
        grad_in = parts[0][rows, :].astype(F32)
        for p in parts[1:]:
            grad_in = grad_in + p[rows, :].astype(F32)
        normed, inverse = normalize(lat_ref[rows, :].astype(F32))
        b_ref[rows, :] = grad_in
        c_ref[rows, :] = grad_in * normed
        return gmid_ref[rows, :] + normalize_back(grad_in * (1.0 + scale_ref[rows, :]), normed, inverse)

    def step(rows):
        c_rows = rows
        grad = rows_step(c_rows)
        out_ref[rows, :] = grad

    def step_low(rows):
        out = rows_step(pl.ds(pl.multiple_of(rows.start + seg, CHUNK), CHUNK))
        low_ref[rows, :] = out.astype(BF)

    by_rows(seg, step)
    by_rows(seg, step_low)
    pick = pickt_ref[...]
    sums_ref[:, :features] = doc_sums(pick, b_ref[...])
    sums_ref[:, features:] = doc_sums(pick, c_ref[...])


def attend(row_in, qkv_cols, qkv_b, docq, dock, hpd):
    group, block = len(row_in), row_in[0].shape[0]
    features = row_in[0].shape[1]
    length, width = group * block, hpd * HEAD
    n, size = len(qkv_cols), qkv_cols[0][0].shape[0]
    counts = [len(c) for c in qkv_cols]
    qkv_cols = [c for cs in qkv_cols for c in cs]
    fixed = lambda i: (0, 0)

    def kernel(*refs):
        xs = refs[:group]
        ws, refs = grouped(refs[group:], counts)
        b_ref, docq_ref, dock_ref = refs[:3]
        refs = refs[3:]
        qkv_ref, w_ref = refs[:2]
        outs = refs[2 : group + 2]
        outt_ref, peak_ref, vt_ref, out_ref, slab_ref = refs[group + 2 :]
        i = pl.program_id(0)

        @pl.when(i == 0)
        def _():
            for m in range(n):
                place_rows(ws[m], slab_ref.at[m])
            for k in range(n):
                w_ref[k * size : (k + 1) * size, :] = slab_ref[k ^ lax.axis_index("dp")]
            for m in range(group):
                part = dot_nn(xs[m][...], w_ref[...]) + b_ref[...]
                qkv_ref[m * block : (m + 1) * block, :] = part.astype(BF)

        attend_kernel(hpd, block, qkv_ref, docq_ref, dock_ref, out_ref, outt_ref, peak_ref, vt_ref)
        for m in range(group):

            @pl.when(i == m)
            def _():
                outs[m][...] = out_ref[...]

    got = launch(
        "attend",
        kernel,
        [*row_in, *qkv_cols, qkv_b, docq, dock],
        in_specs=[pl.BlockSpec((block, features), fixed) for _ in range(group)]
        + [pl.BlockSpec(c.shape, fixed) for c in qkv_cols]
        + [
            pl.BlockSpec((1, 3 * width), fixed),
            pl.BlockSpec((1, block), lambda i: (0, i)),
            pl.BlockSpec((length, 128), fixed),
        ],
        out_specs=[pl.BlockSpec((length, 3 * width), fixed), pl.BlockSpec((features, 3 * width), fixed)]
        + [pl.BlockSpec((block, width), fixed) for _ in range(group)]
        + [
            pl.BlockSpec((width, block), lambda i: (0, i)),
            pl.BlockSpec((8, block), lambda i: (0, i)),
        ],
        out_shape=[sds((length, 3 * width), BF), sds((features, 3 * width), BF)]
        + [sds((block, width), BF) for _ in range(group)]
        + [sds((width, length), F32), sds((8, length), F32)],
        scratch=[
            pltpu.VMEM((hpd, HEAD, length), BF),
            pltpu.VMEM((block, width), BF),
            pltpu.VMEM((n, size, 3 * width), BF),
        ],
        grid=(group,),
    )
    return got[0], got[2 : 2 + group], got[2 + group], got[3 + group], got[1]


def attend_back(qkv, grad_out, outt, peak, docq, dock, hpd):
    group, block = len(grad_out), grad_out[0].shape[0]
    length, width = group * block, hpd * HEAD
    fixed = lambda i: (0, 0)

    def kernel(qkv_ref, *refs):
        dos = refs[:group]
        outt_ref, peak_ref, docq_ref, dock_ref = refs[group : group + 4]
        grad_ref, kt_ref, dk_ref, dv_ref, do_ref = refs[group + 4 :]

        @pl.when(pl.program_id(0) == 0)
        def _():
            for m in range(group):
                do_ref[m * block : (m + 1) * block, :] = dos[m][...]

        attend_back_kernel(
            hpd, block, group, qkv_ref, do_ref, outt_ref, peak_ref, docq_ref, dock_ref, grad_ref, kt_ref, dk_ref, dv_ref
        )

    return launch(
        "attend_back",
        kernel,
        [qkv, *grad_out, outt, peak, docq, dock],
        in_specs=[pl.BlockSpec((length, 3 * width), fixed)]
        + [pl.BlockSpec((block, width), fixed) for _ in range(group)]
        + [
            pl.BlockSpec((width, block), lambda i: (0, i)),
            pl.BlockSpec((8, block), lambda i: (0, i)),
            pl.BlockSpec((1, block), lambda i: (0, i)),
            pl.BlockSpec((length, 128), fixed),
        ],
        out_specs=[pl.BlockSpec((length, 3 * width), fixed)],
        out_shape=[sds((length, 3 * width), BF)],
        scratch=[
            pltpu.VMEM((hpd, HEAD, length), BF),
            pltpu.VMEM((hpd, length, HEAD), F32),
            pltpu.VMEM((hpd, length, HEAD), F32),
            pltpu.VMEM((length, width), BF),
        ],
        grid=(group,),
    )[0]


def place_rows(pieces, ref):
    at = 0
    for p in pieces:
        ref[at : at + p.shape[0], :] = p[...]
        at += p.shape[0]


def mlp_kernel(xs, gs, per, refs):
    n = len(xs)
    w_own, w_other, b1_ref, w2_ref, b2_ref = refs[:5]
    act_ref, gf1_ref, sums_ref = refs[5:8]
    backs, parts = refs[8 : 8 + n], refs[8 + n : 8 + 2 * n]
    w1_ref, x_ref, g_ref, back_ref, part_ref, row_ref = refs[8 + 2 * n :]
    i = pl.program_id(0)
    hidden = w1_ref.shape[1]
    block = x_ref.shape[0] // per

    @pl.when(i == 0)
    def _():
        size = w_own.shape[1] // 2
        whole_rows(w_own, w_other, w1_ref, slice(0, size), slice(0, hidden))
        sums_ref[...] = jnp.zeros_like(sums_ref)
        row_ref[...] = jnp.zeros_like(row_ref)
        span = b2_ref.shape[0]

        def bias(d):
            row_ref[0:1, d * span : (d + 1) * span] = b2_ref[...].astype(F32).reshape(1, span)

        by_index(lax.axis_index("dp"), n, bias)

    for m in range(n):

        @pl.when(i == m // per)
        def _():
            at = pl.ds(m % per * block, block)
            place_rows(xs[m], x_ref.at[at, :])
            place_rows(gs[m], g_ref.at[at, :])

    u = dot_nn(x_ref[...], w1_ref[...]) + b1_ref[...].astype(F32).reshape(1, hidden)
    root = 0.7978845608028654
    squared = u * u
    t = jnp.tanh(root * u * (1.0 + 0.044715 * squared))
    act = (0.5 * u * (1.0 + t)).astype(BF)
    act_ref[...] = act
    slope = 0.5 * (1.0 + t) + 0.5 * u * (1.0 - t * t) * (root * (1.0 + 3 * 0.044715 * squared))
    gf1 = (dot_nt(g_ref[...], w2_ref[...]) * slope).astype(BF)
    gf1_ref[...] = gf1
    back_ref[...] = dot_nt(gf1, w1_ref[...]).astype(BF)
    part_ref[...] = (dot_nn(act, w2_ref[...]) + row_ref[0:1, :]).astype(BF)
    for m in range(n):

        @pl.when(i == m // per)
        def _():
            at = slice(m % per * block, (m % per + 1) * block)
            parts[m][...] = part_ref[at, :]
            backs[m][...] = back_ref[at, :]

    sums_ref[0:1, :hidden] += jnp.sum(gf1.astype(F32), axis=0, keepdims=True)


def grouped(refs, counts):
    out, at = [], 0
    for count in counts:
        out.append(refs[at : at + count])
        at += count
    return out, refs[at:]


def mlp(xs, gs, w_own, w_other, b1, w2, b2):
    n = len(xs)
    block, features = sum(p.shape[0] for p in xs[0]), xs[0][0].shape[1]
    hidden = w2.shape[0]
    per = min(4, n)
    fixed = lambda i: (0, 0)
    piece = pl.BlockSpec((block, features), fixed)
    third = pl.BlockSpec(w_own.shape, lambda i: (0, 0, 0))
    flat = [p for ps in list(xs) + list(gs) for p in ps]
    counts = [len(ps) for ps in list(xs) + list(gs)]

    def kernel(*refs):
        pieces, rest = grouped(refs, counts)
        mlp_kernel(pieces[:n], pieces[n:], per, rest)

    got = launch(
        "mlp",
        kernel,
        flat + [w_own, w_other, b1, w2, b2],
        in_specs=[pl.BlockSpec(p.shape, fixed) for p in flat]
        + [third, third, pl.BlockSpec((hidden,), lambda i: (0,)), pl.BlockSpec((hidden, features), fixed)]
        + [pl.BlockSpec(b2.shape, lambda i: (0,))],
        out_specs=[
            pl.BlockSpec((per * block, hidden), lambda i: (i, 0)),
            pl.BlockSpec((per * block, hidden), lambda i: (i, 0)),
            pl.BlockSpec((8, features), fixed),
        ]
        + [piece] * (2 * n),
        out_shape=[
            sds((n * block, hidden), BF),
            sds((n * block, hidden), BF),
            sds((8, features), F32),
        ]
        + [sds((block, features), BF)] * (2 * n),
        scratch=[
            pltpu.VMEM((features, hidden), BF),
            pltpu.VMEM((per * block, features), BF),
            pltpu.VMEM((per * block, features), BF),
            pltpu.VMEM((per * block, features), BF),
            pltpu.VMEM((per * block, features), BF),
            pltpu.VMEM((8, features), F32),
        ],
        grid=(n // per,),
    )
    return got[:3], got[3 : n + 3], got[n + 3 :]


def wgrad(lefts, rights, name):
    rows, cols = lefts[0].shape[1], rights[0].shape[1]
    block = 384 if rows % 384 == 0 else rows

    def kernel(*refs):
        a_refs, b_refs = refs[: len(lefts)], refs[len(lefts) : -1]

        left = jnp.concatenate([r[...] for r in a_refs], axis=0)
        right = jnp.concatenate([r[...] for r in b_refs], axis=0)
        refs[-1][...] = dot_tn(left, right).astype(BF)

    return launch(
        name,
        kernel,
        list(lefts) + list(rights),
        in_specs=[pl.BlockSpec((a.shape[0], block), lambda i: (0, i)) for a in lefts]
        + [pl.BlockSpec(b.shape, lambda i: (0, 0)) for b in rights],
        out_specs=[pl.BlockSpec((block, cols), lambda i: (i, 0))],
        out_shape=[sds((rows, cols), BF)],
        grid=(rows // block,),
    )[0]


def core_rows(ref, groups, k, mine):
    core = lax.axis_index("blk") % 2
    size = ref.shape[0] // (2 * groups)
    low = ref[2 * k * size : (2 * k + 1) * size, :]
    high = ref[(2 * k + 1) * size : (2 * k + 2) * size, :]
    return jnp.where(core == 0, low, high) if mine else jnp.where(core == 0, high, low)


def other_half(x, groups, name):
    rows, cols = x.shape
    size = rows // (2 * groups)

    def kernel(x_ref, out_ref):
        for k in range(groups):
            out_ref[k * size : (k + 1) * size, :] = core_rows(x_ref, groups, k, False)

    return whole_call(kernel, name, [sds((rows // 2, cols), BF)], [x])[0]


def halves(total, bit):
    size = total.shape[0] // 2
    mine = (lax.axis_index("blk") // bit) % 2
    low, high = total[:size], total[size:]
    return jnp.where(mine == 0, low, high), jnp.where(mine == 0, high, low)


def own_half(x, got, groups, bit, name):
    rows, cols = x.shape
    size = rows // (2 * groups)

    def kernel(x_ref, got_ref, keep_ref, send_ref, all_ref):
        for k in range(groups):
            at = slice(k * size, (k + 1) * size)
            mine = core_rows(x_ref, groups, k, True).astype(F32)
            all_ref[at, :] = (mine + got_ref[at, :].astype(F32)).astype(BF)
        keep_ref[...], send_ref[...] = halves(all_ref[...], bit)

    return whole_call(
        kernel, name, [sds((rows // 4, cols), BF)] * 2, [x, got], [pltpu.VMEM((rows // 2, cols), BF)]
    )


def own_blocks(x, got, n, name):
    rows, cols = x.shape
    size = rows // (2 * n)

    def kernel(x_ref, got_ref, *outs):
        def step(d):
            for m in range(n):
                k = m ^ d
                mine = core_rows(x_ref, n, k, True).astype(F32)
                outs[m][...] = (mine + got_ref[k * size : (k + 1) * size, :].astype(F32)).astype(BF)

        by_index(lax.axis_index("dp"), n, step)

    return whole_call(kernel, name, [sds((size, cols), BF)] * n, [x, got])


def give_back(own, other, name):
    seg, features = own.shape

    def kernel(own_ref, other_ref, out_ref):
        micro = lax.axis_index("blk") // (lax.axis_size("blk") // 2)
        out_ref[micro, 0] = own_ref[...]
        out_ref[1 - micro, 0] = other_ref[...].astype(out_ref.dtype)

    return whole_call(kernel, name, [sds((2, 1, seg, features), own.dtype)], [own, other])[0]


def add_up(refs):
    total = refs[0][...].astype(F32)
    for r in refs[1:]:
        total = total + r[...].astype(F32)
    return total


def fold_sum(parts, bit, name):
    def kernel(*refs):
        keep, send = halves(add_up(refs[:-2]), bit)
        refs[-2][...], refs[-1][...] = keep.astype(BF), send.astype(BF)

    rows, cols = parts[0].shape
    return whole_call(kernel, name, [sds((rows // 2, cols), BF)] * 2, list(parts))


def join_rows(own, got, bit, name):
    def kernel(own_ref, got_ref, out_ref):
        low = (lax.axis_index("blk") // bit) % 2 == 0
        size = own_ref.shape[0]
        out_ref[:size, :] = jnp.where(low, own_ref[...], got_ref[...])
        out_ref[size:, :] = jnp.where(low, got_ref[...], own_ref[...])

    return whole_call(kernel, name, [sds((2 * own.shape[0], own.shape[1]), BF)], [own, got])[0]


def join_blocks(own, got, bit, n, name):
    rows, cols = 2 * own.shape[0], own.shape[1]
    size = rows // n

    def kernel(own_ref, got_ref, *refs):
        outs, all_ref = refs[:-1], refs[-1]
        low = (lax.axis_index("blk") // bit) % 2 == 0
        half = own_ref.shape[0]
        all_ref[:half, :] = jnp.where(low, own_ref[...], got_ref[...])
        all_ref[half:, :] = jnp.where(low, got_ref[...], own_ref[...])

        def step(d):
            for m in range(n):
                outs[m][...] = all_ref[(m ^ d) * size : ((m ^ d) + 1) * size, :]

        by_index(lax.axis_index("dp"), n, step)

    return whole_call(kernel, name, [sds((size, cols), BF)] * n, [own, got], [pltpu.VMEM((rows, cols), BF)])


def sum_of(parts, name, dtype=BF):
    def kernel(*refs):
        refs[-1][...] = add_up(refs[:-1]).astype(dtype)

    return whole_call(kernel, name, [sds(parts[0].shape, dtype)], list(parts))[0]


def take_from(x, got, chips, name):
    def kernel(x_ref, got_ref, out_ref):
        chip = lax.axis_index("blk") // 2
        here = functools.reduce(jnp.logical_or, [chip == c for c in chips])
        out_ref[...] = jnp.where(here, got_ref[...].astype(F32), x_ref[...].astype(F32)).astype(BF)

    return whole_call(kernel, name, [sds(x.shape, BF)], [x, got])[0]


def sum_at(parts, count, name):
    def kernel(*refs):
        refs[-1][...] = add_up([r.at[at : at + count, :] for r, (_, at) in zip(refs, parts)]).astype(BF)

    shape = sds((count, parts[0][0].shape[1]), BF)
    return whole_call(kernel, name, [shape], [x for x, _ in parts])[0]


def qkv_wgrad_kernel(n, group, *refs):
    xs, grad_ref = refs[:group], refs[group]
    outs = refs[group + 1 : group + 1 + n]
    bias_ref, acc_ref = refs[group + 1 + n :]
    block, features = xs[0].shape
    size, width = features // n, grad_ref.shape[1] // 3
    mine = lax.axis_index("dp")
    step = 384 if features % 384 == 0 else features
    for at in range(0, features, step):
        total = dot_tn(xs[0][:, at : at + step], grad_ref[:block, :])
        for m in range(1, group):
            total = total + dot_tn(xs[m][:, at : at + step], grad_ref[m * block : (m + 1) * block, :])
        acc_ref[at : at + step, :] = total
    for m in range(n):
        rows = pl.ds(pl.multiple_of((m ^ mine) * size, size), size)
        outs[m][...] = acc_ref[rows, :].astype(BF)
    total = dot_nn(jnp.ones((8, block * group), BF), grad_ref[...])
    bias_ref[...] = jnp.zeros_like(bias_ref)

    def place(j):
        bias_ref[:, j * width : (j + 1) * width] = total[:, :width]
        bias_ref[:, features + j * width : features + (j + 1) * width] = total[:, 2 * width :]

    by_index(lax.axis_index("blk") % group, group, place)


def place_qkv_kernel(group, *refs):
    parts = refs[:group]
    out_ref, slab_ref = refs[group:]
    mine = lax.axis_index("blk") % group
    size = parts[0].shape[1] // 3
    for m in range(group):
        slab_ref[m] = parts[m][...]
    for j in range(group):
        got = slab_ref[j ^ mine].astype(F32)
        for p in range(3):
            at = p * group * size + j * size
            out_ref[:, at : at + size] = got[:, p * size : (p + 1) * size]


def both_cores(own, other):
    core = lax.axis_index("blk") % 2
    return jnp.where(core == 0, own, other), jnp.where(core == 0, other, own)


def place_fc1(own, other, name):
    n = len(own)
    size, cols = own[0].shape
    wide = n if cols % 128 else 1

    def kernel(*refs):
        out_ref = refs[-1]
        for t in range(wide):
            at = slice(t * cols, (t + 1) * cols)

            def step(k):
                low, high = both_cores(refs[k][...].astype(F32), refs[n + k][...].astype(F32))
                out_ref[:size, at] = low
                out_ref[size:, at] = high

            by_index((pl.program_id(0) * wide + t) ^ lax.axis_index("dp"), n, step)

    piece = pl.BlockSpec((size, cols), lambda j: (0, 0))
    return launch(
        name,
        kernel,
        list(own) + list(other),
        [piece] * (2 * n),
        [pl.BlockSpec((2 * size, wide * cols), lambda j: (0, j))],
        [sds((2 * size, n * cols), F32)],
        grid=(n // wide,),
    )[0]


def both_kernel(half, own_ref, got_ref, out_ref):
    first = lax.axis_index("blk") // half == 0
    own, got = own_ref[...].astype(F32), got_ref[...].astype(F32)
    out_ref[...] = jnp.concatenate([jnp.where(first, own, got), jnp.where(first, got, own)], axis=0).astype(BF)


def add_kernel(a_ref, b_ref, out_ref):
    out_ref[...] = (a_ref[...].astype(F32) + b_ref[...].astype(F32)).astype(out_ref.dtype)


def place_cores_kernel(own_ref, other_ref, out_ref):
    size = out_ref.shape[0] // 2
    low, high = both_cores(own_ref[...].astype(F32), other_ref[...].astype(F32))
    out_ref[:size, :] = low
    out_ref[size:, :] = high


def gather_sums_kernel(in_ref, mid_ref, out_ref, fc1_ref, fc2_ref, qv_ref, all_ref):
    features = out_ref.shape[1]
    all_ref[...] = jnp.zeros_like(all_ref)
    all_ref[:DOCS, : 2 * features] = in_ref[:DOCS, :]
    all_ref[:DOCS, 2 * features : 5 * features] = mid_ref[:DOCS, : 3 * features]
    all_ref[:DOCS, 5 * features :] = out_ref[:DOCS, :]
    row = slice(DOCS, DOCS + 1)
    all_ref[row, :features] = fc1_ref[0:1, :]
    all_ref[row, features : 2 * features] = fc2_ref[row, :]
    all_ref[row, 2 * features : 3 * features] = mid_ref[row, 3 * features :]
    all_ref[row, 3 * features : 5 * features] = qv_ref[0:1, :]


def ada_kernel(n, *refs):
    slots = refs[:n]
    cols_ref, w_ref = refs[n : n + 2]
    wgrad_ref, rows_ref = refs[n + 2 : n + 4]
    conds = refs[n + 4 :]
    got, fc1, rest = [], 0.0, 0.0
    for m in range(n):
        got.append(slots[m][:DOCS, :].astype(F32))
        got.append(slots[m][8 : 8 + DOCS, :].astype(F32))
        bias = slots[m][DOCS : DOCS + 1, :].astype(F32) + slots[m][8 + DOCS : 9 + DOCS, :].astype(F32)
        fc1 = bias if m == 0 else fc1
        rest = rest + bias
    got = jnp.concatenate(got, axis=0)
    rows_ref[...] = jnp.concatenate(
        [jnp.sum(got, axis=0, keepdims=True), rest, fc1, jnp.zeros((5, rest.shape[1]), F32)], axis=0
    )
    got = got.astype(BF)
    wgrad_ref[...] = dot_tn(cols_ref[...].astype(BF), got)
    back = dot_nt(got, w_ref[...])
    first = pl.program_id(0) == 0
    for m in range(n):
        part = back[8 * m : 8 * m + 8, :]
        conds[m][...] = part + jnp.where(first, 0.0, conds[m][...])


def ada(slots, cols, weight):
    n = len(slots)
    dshard, span = weight.shape
    block = span // 6
    return launch(
        "ada",
        functools.partial(ada_kernel, n),
        [*slots, cols, weight],
        in_specs=[pl.BlockSpec((16, block), lambda i: (0, i))] * n
        + [pl.BlockSpec(cols.shape, lambda i: (0, 0)), pl.BlockSpec((dshard, block), lambda i: (0, i))],
        out_specs=[pl.BlockSpec((dshard, block), lambda i: (0, i)), pl.BlockSpec((8, block), lambda i: (0, i))]
        + [pl.BlockSpec((8, dshard), lambda i: (0, 0))] * n,
        out_shape=[sds((dshard, span), F32), sds((8, span), F32)] + [sds((8, dshard), F32)] * n,
        grid=(6,),
    )


def biases_kernel(n, rows_ref, ada_ref, qv_ref, proj_ref, fc1_ref, fc2_ref):
    features = rows_ref.shape[1] // 6
    span, size = ada_ref.shape[0], fc2_ref.shape[0]

    def step(d):
        def part(i):
            at = i * features + d * size
            return rows_ref[1:2, at : at + size]

        ada_ref[...] = rows_ref[0:1, d * span : (d + 1) * span].reshape(span)
        fc2_ref[...] = part(1).reshape(size)
        proj_ref[...] = part(2).reshape(size)
        qv_ref[0:1, :] = part(3)
        qv_ref[1:2, :] = part(4)

    by_index(lax.axis_index("dp"), n, step)
    fc1_ref[...] = rows_ref[2:3, : fc1_ref.shape[0]].reshape(fc1_ref.shape[0])


def cond_kernel(n, *refs):
    parts, cond_ref, out_ref, slab_ref = refs[:n], refs[n], refs[n + 1], refs[n + 2]
    dp = lax.axis_index("dp")
    for m in range(n):
        slab_ref[m] = parts[m][...]
    grad = jnp.concatenate([slab_ref[k ^ dp] for k in range(n)], axis=1)
    for u in range(2):
        cond = cond_ref[u, 0].astype(F32)
        sig = 1.0 / (1.0 + jnp.exp(-cond))
        out_ref[u, 0] = grad[u * DOCS : (u + 1) * DOCS] * (sig * (1.0 + cond * (1.0 - sig)))


def local(
    latents,
    conditions,
    doc_lengths,
    cotangent,
    ada_weight,
    ada_bias,
    qkv_weight,
    qv_bias,
    proj_weight,
    proj_bias,
    fc1_weight,
    fc1_bias,
    fc2_weight,
    fc2_bias,
):
    n_dp, n_blk = lax.axis_size("dp"), lax.axis_size("blk")
    dp, blk = lax.axis_index("dp"), lax.axis_index("blk")
    half = n_blk // 2
    group = half
    core, micro = blk % 2, blk // half
    seg, features = latents.shape[2], latents.shape[3]
    hidden = fc1_weight.shape[1] // n_dp
    dshard = features // n_dp
    hpd = HEADS // group
    width = hpd * HEAD
    hhalf, dhalf = hidden // 2, dshard // 2
    tokens = 2 * seg
    LAST.clear()
    masks = [2 * i for i in range(group // 2)] + [2 * i + 1 for i in range(group // 2)]

    act_shape = sds((tokens, features), BF)
    half_shape = sds((seg, features), BF)
    full_shape = sds((tokens, features), F32)
    sums_shape = sds((16, features), F32)
    full_vmem = pltpu.VMEM((tokens, features), F32)
    v = types.SimpleNamespace()
    chip_bits = bits_of(2, n_blk)

    def step_open():
        v.pack, v.lat_own, v.cot_own, across, v.docq, v.dock, v.pick_mod, v.pick_sum = whole_call(
            functools.partial(open_kernel, half),
            "open",
            [sds((16, features), BF)]
            + [half_shape, half_shape, act_shape]
            + [
                sds((1, group * tokens), jnp.int32),
                sds((group * tokens, 128), jnp.int32),
                sds((tokens, 32), BF),
                sds((16, tokens), BF),
            ],
            [conditions, proj_bias, qv_bias, latents, cotangent, doc_lengths],
        )
        v.across = swap(across, "blk", half)
        v.pack = direct({m: v.pack for m in range(n_dp)}, "dp")

    def step_qkv_cols():
        (cols,) = whole_call(
            functools.partial(qkv_cols_kernel, group), "qkv_cols", [sds((dshard, 3 * width), BF)], [qkv_weight]
        )
        v.qkv_cols = spread_dp(cols)

    def step_mod_part():
        *parts, v.cond_cols, v.proj_b, v.qkv_bias = whole_call(
            functools.partial(mod_part_kernel, n_dp, group),
            "mod_part",
            [sds((DOCS, 6 * features), F32)] * n_dp
            + [sds((8 * n_dp, dshard), F32), sds((1, features), F32), sds((1, 3 * width), F32)],
            [v.pack[m] for m in range(n_dp)] + [ada_weight, ada_bias],
            [pltpu.VMEM((8, 6 * features), F32), pltpu.VMEM((n_dp, 8, features), F32)],
        )
        v.mod_parts = direct(dict(enumerate(parts)), "dp")

    def step_mod_all():
        parts = [v.mod_parts[m] for m in range(n_dp)]
        (v.mod,) = whole_call(mod_all_kernel, "mod_all", [sds((32, 6 * features), BF)], parts)

    def step_attn_in():
        attn_in, v.latent = whole_call(
            attn_in_kernel,
            "attn_in",
            [act_shape] * 2,
            [v.lat_own, v.across, v.pick_mod, v.mod],
            [full_vmem] * 2,
        )
        rows = {0: attn_in}
        for bit in bits_of(2, group):
            for m in list(rows):
                rows[m | bit] = swap(rows[m], "blk", bit)
        for m in list(rows):
            rows[m | 1] = swap(rows[m], "blk", 1)
        v.row_in = [rows[m] for m in masks]

    def step_grad_fc2():
        grad_fc2, v.cot, v.sums_fc2 = whole_call(
            grad_fc2_kernel,
            "grad_fc2",
            [act_shape, act_shape, sums_shape],
            [v.cot_own, v.across, v.pick_mod, v.pick_sum, v.mod],
        )
        v.all_grad = spread_dp(grad_fc2)

    def step_cuts():
        move = whole_call(
            functools.partial(cuts_kernel, n_dp),
            "cuts",
            [sds((2 * dhalf, features), BF)] * n_dp,
            [fc1_weight, proj_weight],
        )
        v.move = direct(dict(enumerate(move)), "dp")

    def step_attend():
        v.qkv, outs, v.outt, v.peak, v.qkv_w = attend(
            v.row_in, v.qkv_cols, v.qkv_bias, v.docq, v.dock, hpd
        )
        v.outs = direct(dict(zip(masks, outs)), "blk")

    def step_stack():
        (v.move_own,) = whole_call(
            functools.partial(stack_kernel, n_dp),
            "stack",
            [sds((n_dp, 2 * dhalf, features), BF)],
            [v.move[m] for m in range(n_dp)],
        )
        v.move_other = swap(v.move_own, "blk", 1)

    def step_mix():
        v.low, v.attn_proj, v.mid, mlp_in, v.proj_w = whole_call(
            functools.partial(mix_kernel, group),
            "mix",
            [act_shape, full_shape, full_shape, act_shape, sds((group, width, features), BF)],
            [v.outs[m] for m in range(group)]
            + [v.move_own, v.move_other, v.proj_b, v.latent, v.pick_mod, v.mod],
            [pltpu.VMEM((features, features), BF), pltpu.VMEM((group, tokens, width), BF)] + [full_vmem] * 3,
        )
        v.all_in = spread_dp(mlp_in)

    def step_mlp():
        (v.act, v.grad_fc1, v.sums_fc1), back, part = mlp(
            v.all_in, v.all_grad, v.move_own, v.move_other, fc1_bias, fc2_weight, fc2_bias
        )
        v.back = direct(dict(enumerate(back)), "dp")
        v.part = direct(dict(enumerate(part)), "dp")

    def flat(pieces):
        return [p for ps in pieces for p in ps]

    def step_fc2_wgrad():
        v.fc2_g = wgrad([v.act], flat(v.all_grad), "fc2_wgrad")

    def step_fc1_wgrad():
        v.fc1_g = wgrad(flat(v.all_in), [v.grad_fc1], "fc1_wgrad")

    def step_turn():
        v.gmid, v.grad_proj, v.sums_mid, *grad_attn = whole_call(
            functools.partial(turn_kernel, n_dp, group),
            "turn",
            [full_shape, act_shape, sds((16, 4 * features), F32)] + [sds((tokens, width), BF)] * group,
            [v.back[m] for m in range(n_dp)]
            + [v.cot, v.mid, v.attn_proj, v.proj_w, v.pick_mod, v.pick_sum, v.mod],
            [full_vmem] * 5,
        )
        v.grad_attn = direct(dict(enumerate(grad_attn)), "blk")

    def step_proj_wgrad():
        v.proj_g = wgrad([v.low], [v.grad_proj], "proj_wgrad")

    def halve(x, groups, name):
        return swap(other_half(x, groups, name), "blk", 1)

    def step_fc2_other():
        v.fc2_got = halve(v.fc2_g, 1, "fc2_other")

    def step_fc1_other():
        v.fc1_got = halve(v.fc1_g, n_dp, "fc1_other")

    def step_proj_other():
        v.proj_got = halve(v.proj_g, n_dp, "proj_other")

    def step_fc2_own():
        v.fc2 = CubeSum(*own_half(v.fc2_g, v.fc2_got, 1, chip_bits[0], "fc2_own"), chip_bits, "fc2_cube")

    def step_fc1_own():
        v.fc1 = CubeSum(*own_half(v.fc1_g, v.fc1_got, n_dp, chip_bits[0], "fc1_own"), chip_bits, "fc1_cube")

    def step_fc2_a():
        v.fc2.fold()

    def step_fc2_b():
        v.fc2.total()

    def step_fc2_j():
        v.fc2.join()

    def step_fc1_a():
        v.fc1.fold()

    def step_fc1_b():
        v.fc1.total()

    def step_fc1_j():
        v.fc1.join()

    def step_proj_a():
        v.proj.until(2)

    def step_proj_b():
        v.proj.until(1)

    def step_fc2_c():
        v.fc2_own = join_rows(v.fc2.x, v.fc2.got, chip_bits[0], "fc2_cube")
        v.fc2_other = swap(v.fc2_own, "blk", 1)

    def step_fc1_c():
        blocks = join_blocks(v.fc1.x, v.fc1.got, chip_bits[0], n_dp, "fc1_cube")
        blocks = direct(dict(enumerate(blocks)), "dp")
        v.fc1_own = [blocks[m] for m in range(n_dp)]
        v.fc1_other = [swap(x, "blk", 1) for x in v.fc1_own]

    def step_proj_blocks():
        v.proj_parts = direct(
            dict(enumerate(own_blocks(v.proj_g, v.proj_got, n_dp, "proj_blocks"))), "dp"
        )

    def step_proj_sum():
        v.proj = LineSum(sum_of([v.proj_parts[m] for m in range(n_dp)], "proj_sum"), "proj_line")

    def step_proj_c():
        v.proj.until(0)
        v.proj_other = swap(v.proj.x, "blk", 1)

    def step_attend_back():
        grad_qkv = attend_back(
            v.qkv, [v.grad_attn[m] for m in masks], v.outt, v.peak, v.docq, v.dock, hpd
        )
        v.grad_qkv = grad_qkv
        count = (group // 2) * tokens
        send = swap(dot_nt(grad_qkv[count:], v.qkv_w).astype(BF), "blk", 1)
        keep = dot_nt(grad_qkv[:count], v.qkv_w).astype(BF)
        v.blocks = {m: [(keep, i * tokens), (send, i * tokens)] for i, m in enumerate(masks[: group // 2])}

    def step_qkv_wgrad():
        *qkv_g, v.sums_qv = whole_call(
            functools.partial(qkv_wgrad_kernel, n_dp, group),
            "qkv_wgrad",
            [sds((dshard, 3 * width), BF)] * n_dp + [sds((8, 2 * features), F32)],
            v.row_in + [v.grad_qkv],
            [pltpu.VMEM((features, 3 * width), F32)],
        )
        v.qkv_g = direct(dict(enumerate(qkv_g)), "dp")

    def step_outs():
        v.block_own, other, v.sums_out = whole_call(
            functools.partial(outs_kernel, n_dp),
            "outs",
            [half_shape, half_shape, sums_shape],
            [v.part[m] for m in range(n_dp)] + [v.cot, v.mid, v.pick_mod, v.pick_sum, v.mod],
            [pltpu.VMEM((tokens, features), BF)] + [full_vmem] * 2,
        )
        v.block_other = swap(other, "blk", half)

    def step_attn_sum():
        blocks = v.blocks
        for bit in reversed(bits_of(2, group)):
            for m in [m for m in blocks if m & bit]:
                blocks[m ^ bit].append((swap(sum_at(blocks.pop(m), tokens, "attn_sum"), "blk", bit), 0))

    def step_finish():
        parts = v.blocks[0]
        v.latent_own, other, v.sums_in = whole_call(
            functools.partial(finish_kernel, [at for _, at in parts], seg),
            "finish",
            [sds((seg, features), F32), half_shape, sds((16, 2 * features), F32)],
            [x for x, _ in parts] + [v.latent, v.gmid, v.pick_mod, v.pick_sum, v.mod],
            [full_vmem] * 3,
        )
        v.latent_other = swap(other, "blk", half)

    def step_qkv_sum():
        v.qkv_x = sum_of([v.qkv_g[m] for m in range(n_dp)], "qkv_sum")
        v.qkv_got = swap(v.qkv_x, "blk", half)

    def step_qkv_sum2():
        parts = {0: sum_of([v.qkv_x, v.qkv_got], "qkv_sum")}
        for bit in bits_of(2, group):
            for m in list(parts):
                parts[m | bit] = swap(parts[m], "blk", bit)
        for m in list(parts):
            parts[m | 1] = swap(parts[m], "blk", 1)
        v.qkv_parts = parts

    def step_gather_sums():
        (v.sums,) = whole_call(
            gather_sums_kernel,
            "gather_sums",
            [sds((8, 6 * features), F32)],
            [v.sums_in, v.sums_mid, v.sums_out, v.sums_fc1, v.sums_fc2, v.sums_qv],
        )
        v.sums_got = swap(v.sums, "blk", 1)

    def step_sums_c():
        for bit in bits_of(2, group):
            (v.sums,) = whole_call(add_kernel, "sums", [sds(v.sums.shape, BF)], [v.sums, v.sums_got])
            v.sums_got = swap(v.sums, "blk", bit)

    def step_sums_g():
        (v.sums,) = whole_call(add_kernel, "sums", [sds(v.sums.shape, BF)], [v.sums, v.sums_got])
        v.sums_got = swap(v.sums, "blk", half)

    def step_sums_h():
        (both,) = whole_call(
            functools.partial(both_kernel, half), "both", [sds((16, 6 * features), BF)], [v.sums, v.sums_got]
        )
        v.slots = direct({m: both for m in range(n_dp)}, "dp")

    def step_ada():
        v.ada_wgrad, v.rows_sum, *parts = ada([v.slots[m] for m in range(n_dp)], v.cond_cols, ada_weight)
        v.cond_parts = direct(dict(enumerate(parts)), "dp")

    def step_biases():
        spans = [ada_bias.shape, (2, dshard), (dshard,), (hidden,), (dshard,)]
        v.ada_bgrad, v.qv_bgrad, v.proj_bgrad, v.fc1_bgrad, v.fc2_bgrad = whole_call(
            functools.partial(biases_kernel, n_dp), "biases", [sds(x, F32) for x in spans], [v.rows_sum]
        )

    def step_cond():
        (v.cond_grad,) = whole_call(
            functools.partial(cond_kernel, n_dp),
            "cond_grad",
            [sds((2, 1, DOCS, features), F32)],
            [v.cond_parts[m] for m in range(n_dp)] + [conditions],
            [pltpu.VMEM((n_dp, 8, dshard), F32)],
        )

    def step_place_qkv():
        (v.qkv_wgrad,) = whole_call(
            functools.partial(place_qkv_kernel, group),
            "place_qkv",
            [sds((dshard, 3 * features), F32)],
            [v.qkv_parts[m] for m in range(group)],
            [pltpu.VMEM((group, dshard, 3 * width), BF)],
        )

    def step_place_fc2():
        (v.fc2_wgrad,) = whole_call(
            place_cores_kernel, "place_fc2", [sds((hidden, features), F32)], [v.fc2_own, v.fc2_other]
        )

    def step_place_proj():
        (v.proj_wgrad,) = whole_call(
            place_cores_kernel, "place_proj", [sds((dshard, features), F32)], [v.proj.x, v.proj_other]
        )

    def step_place_fc1():
        v.fc1_wgrad = place_fc1(v.fc1_own, v.fc1_other, "place_fc1")

    def step_block_out():
        v.block_out = give_back(v.block_own, v.block_other, "block_out")

    def step_latent_grad():
        v.latent_grad = give_back(v.latent_own, v.latent_other, "latent_grad")

    for step in (
        step_open, step_qkv_cols, step_mod_part, step_cuts, step_mod_all, step_attn_in, step_attend, step_grad_fc2,
        step_stack, step_mix, step_mlp, step_fc2_wgrad, step_fc1_wgrad, step_turn, step_fc2_other, step_fc2_own,
        step_fc1_other, step_attend_back, step_attn_sum, step_fc2_a, step_fc1_own, step_qkv_wgrad, step_finish,
        step_proj_wgrad, step_outs, step_fc2_b, step_gather_sums, step_qkv_sum, step_sums_c, step_fc1_a,
        step_fc2_j, step_sums_g, step_proj_other, step_proj_blocks, step_fc1_b, step_proj_sum, step_sums_h,
        step_fc2_c, step_ada, step_qkv_sum2, step_proj_a, step_place_fc2, step_fc1_j, step_fc1_c, step_biases, step_cond,
        step_proj_b, step_place_qkv, step_latent_grad, step_proj_c, step_place_fc1, step_place_proj,
        step_block_out,
    ):
        step()

    return (
        v.block_out,
        v.latent_grad,
        v.cond_grad,
        v.ada_wgrad,
        v.ada_bgrad,
        v.qkv_wgrad,
        v.qv_bgrad,
        v.proj_wgrad,
        v.proj_bgrad,
        v.fc1_wgrad,
        v.fc1_bgrad,
        v.fc2_wgrad,
        v.fc2_bgrad,
    )


def solution(mesh):
    in_specs = (
        P(None, "dp", "blk", None),
        P(None, "dp", None, None),
        P(None, "dp", None),
        P(None, "dp", "blk", None),
        P("dp", None),
        P("dp"),
        P("dp", None),
        P(None, "dp"),
        P("dp", None),
        P("dp"),
        P("dp", None),
        P("dp"),
        P("dp", None),
        P("dp"),
    )
    out_specs = (
        P(None, "dp", "blk", None),
        P(None, "dp", "blk", None),
        P(None, "dp", None, None),
        P("dp", None),
        P("dp"),
        P("dp", None),
        P(None, "dp"),
        P("dp", None),
        P("dp"),
        P("dp", None),
        P("dp"),
        P("dp", None),
        P("dp"),
    )
    return jax.shard_map(local, mesh=mesh, in_specs=in_specs, out_specs=out_specs, check_vma=False)
```

```python
import functools
import math
import types

import jax
import jax.numpy as jnp
from jax import lax
from jax.experimental import pallas as pl
from jax.experimental.pallas import tpu as pltpu
from jax.sharding import PartitionSpec as P

HEADS = 16
HEAD = 72
DOCS = 4
NORM_EPS = 1e-06
MASKED = -1e30
LOG2E = 1.4426950408889634
SCALE = HEAD ** (-0.5)
VMEM_LIMIT = 56 * 1024 * 1024
HIGHEST = lax.Precision.HIGHEST
BF = jnp.bfloat16
F32 = jnp.float32


def normalize(values):
    center = jnp.mean(values, axis=-1, keepdims=True)
    centred = values - center
    inverse = lax.rsqrt(jnp.mean(centred * centred, axis=-1, keepdims=True) + NORM_EPS)
    return centred * inverse, inverse


def normalize_back(grad, normed, inverse):
    first = jnp.mean(grad, axis=-1, keepdims=True)
    second = jnp.mean(grad * normed, axis=-1, keepdims=True)
    return inverse * (grad - first - normed * second)


def dot_nn(a, b):
    return lax.dot_general(a, b, (((1,), (0,)), ((), ())), preferred_element_type=F32)


def dot_nt(a, b):
    return lax.dot_general(a, b, (((1,), (1,)), ((), ())), preferred_element_type=F32)


def dot_tn(a, b):
    return lax.dot_general(a, b, (((0,), (0,)), ((), ())), preferred_element_type=F32)


def swap(x, axis, mask):
    count = lax.axis_size(axis)
    return lax.ppermute(x, axis, [(i, i ^ mask) for i in range(count)])


def bits_of(low, high):
    out = []
    while low < high:
        out.append(low)
        low *= 2
    return out


def direct(blocks, axis):
    return {m: (b if m == 0 else swap(b, axis, m)) for m, b in blocks.items()}


def spread_dp(x):
    n = lax.axis_size("dp")
    blocks = {0: [x]}
    if n == 4:
        cut = x.shape[0] // 2
        one, two = swap(x, "dp", 1), swap(x, "dp", 2)
        blocks[1], blocks[2] = [one], [two]
        blocks[3] = [swap(one[:cut], "dp", 2), swap(two[cut:], "dp", 1)]
        return [blocks[m] for m in range(n)]
    for bit in bits_of(1, n):
        for mask in list(blocks):
            blocks[mask | bit] = [swap(blocks[mask][0], "dp", bit)]
    return [blocks[m] for m in range(n)]


def line_pairs():
    chips = lax.axis_size("blk") // 2
    mid = chips // 2
    inward = [[(s, s + 1), (chips - 1 - s, chips - 2 - s)] for s in range(mid - 1)]
    outward = [[(mid - 1 - s, mid - 2 - s), (mid + s, mid + s + 1)] for s in range(mid - 1)]
    return inward, [(mid - 1, mid), (mid, mid - 1)], outward


def along(x, pairs):
    return lax.ppermute(x, "blk", [(2 * a + c, 2 * b + c) for a, b in pairs for c in range(2)])


class LineSum:
    def __init__(self, x, name):
        inward, middle, outward = line_pairs()
        self.steps = [("add", p) for p in inward] + [("add", middle)] + [("take", p) for p in outward]
        self.x, self.name, self.at = x, name, 0
        self.got = along(x, self.steps[0][1])

    def step(self):
        kind, pairs = self.steps[self.at]
        if kind == "add":
            self.x = sum_of([self.x, self.got], self.name)
        else:
            self.x = take_from(self.x, self.got, [b for _, b in pairs], self.name)
        self.at += 1
        if self.at < len(self.steps):
            self.got = along(self.x, self.steps[self.at][1])

    def until(self, left):
        while len(self.steps) - self.at > left:
            self.step()


class CubeSum:
    def __init__(self, keep, send, bits, name):
        self.x, self.bits, self.name = keep, bits, name
        self.got = swap(send, "blk", bits[0])

    def fold(self):
        for bit in self.bits[1:]:
            self.x, send = fold_sum([self.x, self.got], bit, self.name)
            self.got = swap(send, "blk", bit)

    def total(self):
        self.x = sum_of([self.x, self.got], self.name)
        self.got = swap(self.x, "blk", self.bits[-1])

    def join(self):
        for i in range(len(self.bits) - 1, 0, -1):
            self.x = join_rows(self.x, self.got, self.bits[i], self.name)
            self.got = swap(self.x, "blk", self.bits[i - 1])


def allowed_mask(dock_ref, docq_ref, width):
    keys = dock_ref[...]
    keys = jnp.concatenate([keys] * (width // keys.shape[1]), axis=1)
    return keys == docq_ref[...]


def attend_kernel(hpd, block, qkv_ref, docq_ref, dock_ref, out_ref, outt_ref, peak_ref, vt_ref):
    i = pl.program_id(0)
    width = hpd * HEAD
    rows = pl.ds(pl.multiple_of(i * block, block), block)

    @pl.when(i == 0)
    def _():
        for h in range(hpd):
            v = qkv_ref[:, 2 * width + h * HEAD : 2 * width + (h + 1) * HEAD]
            vt_ref[h] = v.astype(F32).T.astype(BF)

    allowed = allowed_mask(dock_ref, docq_ref, block)
    outs, peaks = [], []
    for h in range(hpd):
        q = qkv_ref[rows, h * HEAD : (h + 1) * HEAD]
        k = qkv_ref[:, width + h * HEAD : width + (h + 1) * HEAD]
        scores = jnp.where(allowed, dot_nt(k, q), MASKED)
        peak = jnp.max(scores, axis=0, keepdims=True)
        weight = jnp.exp2((scores - peak) * (SCALE * LOG2E))
        total = jnp.sum(weight, axis=0, keepdims=True)
        outs.append(dot_nn(vt_ref[h], weight.astype(BF)) / total)
        peaks.append(peak + jnp.log(total) * (1.0 / SCALE))
    out = jnp.concatenate(outs, axis=0)
    outt_ref[...] = out
    out_ref[...] = out.T.astype(BF)
    peaks.append(jnp.zeros((8 - hpd, block), F32))
    peak_ref[...] = jnp.concatenate(peaks, axis=0)


def attend_back_kernel(
    hpd, block, steps, qkv_ref, do_ref, outt_ref, peak_ref, docq_ref, dock_ref, grad_ref, kt_ref, dk_ref, dv_ref
):
    i = pl.program_id(0)
    width = hpd * HEAD
    rows = pl.ds(pl.multiple_of(i * block, block), block)

    @pl.when(i == 0)
    def _():
        for h in range(hpd):
            k = qkv_ref[:, width + h * HEAD : width + (h + 1) * HEAD]
            kt_ref[h] = k.astype(F32).T.astype(BF)
        dk_ref[...] = jnp.zeros_like(dk_ref)
        dv_ref[...] = jnp.zeros_like(dv_ref)

    allowed = allowed_mask(dock_ref, docq_ref, block)
    dots = do_ref[rows, :].astype(F32).T * outt_ref[...]
    dqs = []
    for h in range(hpd):
        part = slice(h * HEAD, (h + 1) * HEAD)
        q = qkv_ref[rows, part]
        k = qkv_ref[:, width + h * HEAD : width + (h + 1) * HEAD]
        v = qkv_ref[:, 2 * width + h * HEAD : 2 * width + (h + 1) * HEAD]
        do = do_ref[rows, part]
        row_dot = jnp.sum(dots[part], axis=0, keepdims=True)
        scores = jnp.where(allowed, dot_nt(k, q), MASKED)
        probs = jnp.exp2((scores - peak_ref[h : h + 1, :]) * (SCALE * LOG2E))
        grad_scores = (probs * (dot_nt(v, do) - row_dot)).astype(BF)
        dv_ref[h] += dot_nn(probs.astype(BF), do)
        dk_ref[h] += dot_nn(grad_scores, q)
        dqs.append(dot_nn(kt_ref[h], grad_scores))
    grad_ref[rows, :width] = (jnp.concatenate(dqs, axis=0) * SCALE).T.astype(BF)

    @pl.when(i == steps - 1)
    def _():
        dk = jnp.concatenate([dk_ref[h] for h in range(hpd)], axis=1) * SCALE
        dv = jnp.concatenate([dv_ref[h] for h in range(hpd)], axis=1)
        grad_ref[:, width : 2 * width] = dk.astype(BF)
        grad_ref[:, 2 * width :] = dv.astype(BF)


WORK = {"attend": 6, "attend_back": 8, "mlp": 4, "qkv_wgrad": 12, "mod_part": 8}


def params(name, grid, arrays, scratch):
    held = sum(a.size * a.dtype.itemsize for a in arrays) * (1 if grid is None or grid == (1,) else 2)
    held += sum(math.prod(x.shape) * jnp.dtype(x.dtype).itemsize for x in scratch)
    limit = min(VMEM_LIMIT, held + WORK.get(name, 6) * 1024 * 1024)
    return pltpu.CompilerParams(
        vmem_limit_bytes=limit, dimension_semantics=None if grid is None else ("arbitrary",)
    )


LIGHT = pl.CostEstimate(flops=1000, bytes_accessed=1000, transcendentals=0)
VM = pl.BlockSpec(memory_space=pltpu.VMEM)
SM = pl.BlockSpec(memory_space=pltpu.SMEM)
ANY = pl.BlockSpec(memory_space=pl.ANY)


def sds(shape, dtype):
    return jax.ShapeDtypeStruct(shape, dtype)


LAST = []


def launch(name, kernel, args, in_specs, out_specs, out_shape, scratch=(), grid=None):
    count, after = len(args), list(LAST)

    def body(*refs):
        kernel(*refs[:count], *refs[count + len(after) :])

    got = pl.pallas_call(
        body,
        **({} if grid is None else {"grid": grid}),
        in_specs=list(in_specs) + [ANY] * len(after),
        out_specs=list(out_specs),
        out_shape=list(out_shape),
        scratch_shapes=list(scratch),
        compiler_params=params(name, grid, list(args) + list(out_shape), scratch),
        cost_estimate=LIGHT,
        name=name,
    )(*args, *after)
    LAST[:] = [min(got, key=lambda a: a.size)]
    return got


def whole_call(kernel, name, outs, args, scratch=()):
    specs = [SM if a.dtype == jnp.int32 and a.ndim != 2 else VM for a in args]
    return launch(name, kernel, args, specs, [VM] * len(outs), outs, scratch)


CHUNK = 32


def by_rows(count, step):
    def inner(i, carry):
        step(pl.ds(pl.multiple_of(i * CHUNK, CHUNK), CHUNK))
        return carry

    lax.fori_loop(0, count // CHUNK, inner, 0, unroll=2)


def doc_sums(pick, grads):
    high = grads.astype(BF)
    low = (grads - high.astype(F32)).astype(BF)
    return dot_nn(pick, high) + dot_nn(pick, low)


def by_index(index, count, step):
    for i in range(count):

        @pl.when(index == i)
        def _():
            step(i)


def part_ways_kernel(half, x_ref, own_ref, send_ref):
    micro = lax.axis_index("blk") // half
    own_ref[...] = x_ref[micro, 0]
    send_ref[...] = x_ref[1 - micro, 0]


def open_kernel(half, seg, cond_ref, bias_ref, qv_ref, lengths_ref, *refs):
    pack_ref, docq_ref, dock_ref, mod_ref, sum_ref = refs
    blk = lax.axis_index("blk")
    micro = blk // half
    group = half
    features = pack_ref.shape[1]
    tokens = 2 * seg
    dshard = qv_ref.shape[1]
    cond = jnp.concatenate([cond_ref[0, 0], cond_ref[1, 0]], axis=0).astype(F32)
    silu = cond / (1.0 + jnp.exp(-cond))
    small = jnp.concatenate(
        [bias_ref[...].astype(F32).reshape(1, dshard), qv_ref[0:1, :].astype(F32), qv_ref[1:2, :].astype(F32)], axis=1
    )
    small = jnp.pad(small, ((0, 7), (0, features - 3 * dshard)))
    pack_ref[...] = jnp.concatenate([silu, small], axis=0).astype(BF)
    ends, last = [], 0
    for d in range(DOCS):
        last = last + lengths_ref[micro, 0, d]
        ends.append(last)

    def docs(index, shape, dim):
        spot = lax.broadcasted_iota(jnp.int32, shape, dim) + index * seg
        found = jnp.zeros(shape, jnp.int32)
        for d in range(DOCS):
            found = found + jnp.where(spot >= ends[d], 1, 0)
        return found

    for i in range(group):
        mask = 2 * (i % (group // 2)) + i // (group // 2)
        for part in range(2):
            at = i * tokens + part * seg
            index = (blk ^ mask) ^ (half * part)
            dock_ref[at : at + seg, :] = docs(index, (seg, 128), 0)
            docq_ref[:, at : at + seg] = docs(index, (8, seg), 1)[:1]
    for part in range(2):
        at = part * seg
        index = blk ^ (half * part)
        col = lax.broadcasted_iota(jnp.int32, (seg, 32), 1)
        same = (col % DOCS == docs(index, (seg, 32), 0)) & (col < 3 * DOCS)
        mod_ref[at : at + seg, :] = jnp.where(same, 1.0, 0.0).astype(BF)
        row = lax.broadcasted_iota(jnp.int32, (16, seg), 0)
        same = (row == docs(index, (16, seg), 1)) | (row == DOCS)
        sum_ref[:, at : at + seg] = jnp.where(same, 1.0, 0.0).astype(BF)


def qkv_cols_kernel(group, w_ref, out_ref):
    width = out_ref.shape[1] // 3

    def step(j):
        for p in range(3):
            at = p * group * width + j * width
            out_ref[:, p * width : (p + 1) * width] = w_ref[:, at : at + width]

    by_index(lax.axis_index("blk") % group, group, step)


def cuts_kernel(n, fc1_ref, proj_ref, *outs):
    core = lax.axis_index("blk") % 2
    size = outs[0].shape[0] // 2
    hidden = fc1_ref.shape[1] // n

    def half(ref, cols):
        return jnp.where(core == 0, ref[:size, cols], ref[size:, cols])

    def step(d):
        for m in range(n):
            outs[m][:size, :hidden] = half(fc1_ref, slice((d ^ m) * hidden, ((d ^ m) + 1) * hidden))

    by_index(lax.axis_index("dp"), n, step)
    for m in range(n):
        outs[m][size:, :] = half(proj_ref, slice(None))


def stack_kernel(n, *refs):
    for m in range(n):
        refs[-1][m] = refs[m][...]


def whole_rows(own_ref, other_ref, out_ref, rows, cols):
    dp, core = lax.axis_index("dp"), lax.axis_index("blk") % 2
    n, size = own_ref.shape[0], rows.stop - rows.start
    for k in range(n):
        own, other = own_ref[k ^ dp, rows, cols], other_ref[k ^ dp, rows, cols]
        out_ref[2 * k * size : (2 * k + 1) * size, :] = jnp.where(core == 0, own, other)
        out_ref[(2 * k + 1) * size : (2 * k + 2) * size, :] = jnp.where(core == 0, other, own)


def mod_part_kernel(n, group, *refs):
    packs = refs[:n]
    w_ref, bias_ref = refs[n : n + 2]
    parts = refs[n + 2 : 2 * n + 2]
    cols_ref, projb_ref, qkvb_ref, add_ref, slab_ref = refs[2 * n + 2 :]
    dp, blk = lax.axis_index("dp"), lax.axis_index("blk")
    micro = blk // group
    dshard, span = w_ref.shape[0], bias_ref.shape[0]
    features = dshard * n
    width = features // group
    add_ref[...] = jnp.zeros_like(add_ref)
    bias = jnp.broadcast_to(bias_ref[...].astype(F32).reshape(1, span), (8, span))

    def mine(d):
        add_ref[:, d * span : (d + 1) * span] = bias
        for m in range(n):
            cols_ref[8 * m : 8 * m + 8, :] = packs[m][:8, d * dshard : (d + 1) * dshard].astype(F32)

    by_index(dp, n, mine)
    lhs = []
    for m in range(n):
        slab_ref[m] = packs[m][8:16, :].astype(F32)
        low, high = cols_ref[8 * m : 8 * m + 4, :], cols_ref[8 * m + 4 : 8 * m + 8, :]
        lhs.append(jnp.where(micro == 0, low, high))
    product = dot_nn(jnp.concatenate(lhs, axis=0).astype(BF), w_ref[...])
    for m in range(n):
        parts[m][...] = product[4 * m : 4 * m + 4, :] + add_ref[:4, :]
    rows = [slab_ref[k ^ dp][:1] for k in range(n)]
    projb_ref[...] = jnp.concatenate([r[:, :dshard] for r in rows], axis=1)
    q_bias = jnp.concatenate([r[:, dshard : 2 * dshard] for r in rows], axis=1)
    v_bias = jnp.concatenate([r[:, 2 * dshard : 3 * dshard] for r in rows], axis=1)

    def step(j):
        part = slice(j * width, (j + 1) * width)
        qkvb_ref[...] = jnp.concatenate([q_bias[:, part], jnp.zeros((1, width), F32), v_bias[:, part]], axis=1)

    by_index(blk % group, group, step)


def mod_all_kernel(*refs):
    parts, out_ref = refs[:-1], refs[-1]
    total = parts[0][...]
    for p in parts[1:]:
        total = total + p[...]
    high = total.astype(BF).astype(F32)
    middle = (total - high).astype(BF).astype(F32)
    low = total - high - middle
    blank = jnp.zeros((32 - 3 * DOCS, total.shape[1]), F32)
    out_ref[...] = jnp.concatenate([high, middle, low, blank], axis=0).astype(BF)


def attn_in_kernel(own_ref, got_ref, pick_ref, mod_ref, out_ref, lat_ref, shift_ref, scale_ref):
    seg, features = own_ref.shape
    lat_ref[:seg, :] = own_ref[...]
    lat_ref[seg:, :] = got_ref[...]
    shift_ref[...] = dot_nn(pick_ref[...], mod_ref[:, :features])
    scale_ref[...] = dot_nn(pick_ref[...], mod_ref[:, features : 2 * features])

    def step(rows):
        normed, _ = normalize(lat_ref[rows, :].astype(F32))
        out_ref[rows, :] = (normed * (1.0 + scale_ref[rows, :]) + shift_ref[rows, :]).astype(BF)

    by_rows(lat_ref.shape[0], step)


def grad_fc2_kernel(own_ref, got_ref, pick_ref, pickt_ref, mod_ref, out_ref, cot_ref, sums_ref):
    seg, features = own_ref.shape
    cot_ref[:seg, :] = own_ref[...]
    cot_ref[seg:, :] = got_ref[...]
    gate = dot_nn(pick_ref[...], mod_ref[:, 5 * features : 6 * features])
    out_ref[...] = (gate * cot_ref[...].astype(F32)).astype(BF)
    sums_ref[...] = dot_nn(pickt_ref[...], out_ref[...])


def mix_kernel(group, *refs):
    outs = refs[:group]
    own, other, bias_ref, lat_ref, pick_ref, mod_ref = refs[group : group + 6]
    low_ref, proj_ref, mid_ref, in_ref, heads_ref, w_ref, slab_ref, gate_ref, shift_ref, scale_ref = refs[group + 6 :]
    features = lat_ref.shape[1]
    width = features // group
    mine = lax.axis_index("blk") % group
    size = own.shape[1] // 2
    whole_rows(own, other, w_ref, slice(size, 2 * size), slice(0, features))
    for k in range(group):
        heads_ref[k] = w_ref[k * width : (k + 1) * width, :]
    for m in range(group):
        slab_ref[m] = outs[m][...]
    low_ref[...] = jnp.concatenate([slab_ref[k ^ mine] for k in range(group)], axis=1)
    proj_ref[...] = dot_nn(low_ref[...], w_ref[...]) + bias_ref[...]
    gate_ref[...] = dot_nn(pick_ref[...], mod_ref[:, 2 * features : 3 * features])
    shift_ref[...] = dot_nn(pick_ref[...], mod_ref[:, 3 * features : 4 * features])
    scale_ref[...] = dot_nn(pick_ref[...], mod_ref[:, 4 * features : 5 * features])

    def step(rows):
        mid = lat_ref[rows, :].astype(F32) + gate_ref[rows, :] * proj_ref[rows, :]
        mid_ref[rows, :] = mid
        normed, _ = normalize(mid)
        in_ref[rows, :] = (normed * (1.0 + scale_ref[rows, :]) + shift_ref[rows, :]).astype(BF)

    by_rows(lat_ref.shape[0], step)


def turn_kernel(pieces, group, *refs):
    parts = refs[:pieces]
    cot_ref, mid_ref, proj_ref, heads_ref, pick_ref, pickt_ref, mod_ref = refs[pieces : pieces + 7]
    gmid_ref, gproj_ref, sums_ref = refs[pieces + 7 : pieces + 10]
    grads = refs[pieces + 10 : pieces + 10 + group]
    gate_ref, scale_ref, a_ref, b_ref, c_ref = refs[pieces + 10 + group :]
    features = cot_ref.shape[1]
    mine = lax.axis_index("blk") % group
    gate_ref[...] = dot_nn(pick_ref[...], mod_ref[:, 2 * features : 3 * features])
    scale_ref[...] = dot_nn(pick_ref[...], mod_ref[:, 4 * features : 5 * features])

    def step(rows):
        grad_in = parts[0][rows, :].astype(F32)
        for p in parts[1:]:
            grad_in = grad_in + p[rows, :].astype(F32)
        normed, inverse = normalize(mid_ref[rows, :])
        gmid = cot_ref[rows, :].astype(F32) + normalize_back(
            grad_in * (1.0 + scale_ref[rows, :]), normed, inverse
        )
        gmid_ref[rows, :] = gmid
        gproj_ref[rows, :] = (gate_ref[rows, :] * gmid).astype(BF)
        a_ref[rows, :] = gmid * proj_ref[rows, :]
        b_ref[rows, :] = grad_in
        c_ref[rows, :] = grad_in * normed

    by_rows(cot_ref.shape[0], step)
    for m in range(group):
        grads[m][...] = dot_nt(gproj_ref[...], heads_ref[m ^ mine]).astype(BF)
    pick = pickt_ref[...]
    sums_ref[:, :features] = doc_sums(pick, a_ref[...])
    sums_ref[:, features : 2 * features] = doc_sums(pick, b_ref[...])
    sums_ref[:, 2 * features : 3 * features] = doc_sums(pick, c_ref[...])
    sums_ref[:, 3 * features :] = dot_nn(pick, gproj_ref[...])


def outs_kernel(pieces, *refs):
    parts = refs[:pieces]
    cot_ref, mid_ref, pick_ref, pickt_ref, mod_ref, out_ref, low_ref, sums_ref, hold_ref, gate_ref, a_ref = refs[pieces:]
    features = cot_ref.shape[1]
    gate_ref[...] = dot_nn(pick_ref[...], mod_ref[:, 5 * features : 6 * features])

    def step(rows):
        fc2_out = parts[0][rows, :].astype(F32)
        for p in parts[1:]:
            fc2_out = fc2_out + p[rows, :].astype(F32)
        hold_ref[rows, :] = (mid_ref[rows, :] + gate_ref[rows, :] * fc2_out).astype(BF)
        a_ref[rows, :] = cot_ref[rows, :].astype(F32) * fc2_out

    by_rows(cot_ref.shape[0], step)
    seg = out_ref.shape[0]
    out_ref[...] = hold_ref[:seg, :]
    low_ref[...] = hold_ref[seg:, :]
    sums_ref[...] = doc_sums(pickt_ref[...], a_ref[...])


def finish_kernel(starts, seg, *refs):
    pieces = len(starts)
    parts = [r.at[at : at + 2 * seg, :] for r, at in zip(refs, starts)]
    lat_ref, gmid_ref, pick_ref, pickt_ref, mod_ref, out_ref, low_ref, sums_ref, scale_ref, b_ref, c_ref = refs[
        pieces:
    ]
    features = lat_ref.shape[1]
    scale_ref[...] = dot_nn(pick_ref[...], mod_ref[:, features : 2 * features])

    def rows_step(rows):
        grad_in = parts[0][rows, :].astype(F32)
        for p in parts[1:]:
            grad_in = grad_in + p[rows, :].astype(F32)
        normed, inverse = normalize(lat_ref[rows, :].astype(F32))
        b_ref[rows, :] = grad_in
        c_ref[rows, :] = grad_in * normed
        return gmid_ref[rows, :] + normalize_back(grad_in * (1.0 + scale_ref[rows, :]), normed, inverse)

    def step(rows):
        c_rows = rows
        grad = rows_step(c_rows)
        out_ref[rows, :] = grad

    def step_low(rows):
        out = rows_step(pl.ds(pl.multiple_of(rows.start + seg, CHUNK), CHUNK))
        low_ref[rows, :] = out.astype(BF)

    by_rows(seg, step)
    by_rows(seg, step_low)
    pick = pickt_ref[...]
    sums_ref[:, :features] = doc_sums(pick, b_ref[...])
    sums_ref[:, features:] = doc_sums(pick, c_ref[...])


def attend(row_in, qkv_cols, qkv_b, docq, dock, hpd):
    group, block = len(row_in), row_in[0].shape[0]
    features = row_in[0].shape[1]
    length, width = group * block, hpd * HEAD
    n, size = len(qkv_cols), qkv_cols[0][0].shape[0]
    counts = [len(c) for c in qkv_cols]
    qkv_cols = [c for cs in qkv_cols for c in cs]
    fixed = lambda i: (0, 0)

    def kernel(*refs):
        xs = refs[:group]
        ws, refs = grouped(refs[group:], counts)
        b_ref, docq_ref, dock_ref = refs[:3]
        refs = refs[3:]
        qkv_ref, w_ref = refs[:2]
        outs = refs[2 : group + 2]
        outt_ref, peak_ref, vt_ref, out_ref, slab_ref = refs[group + 2 :]
        i = pl.program_id(0)

        @pl.when(i == 0)
        def _():
            for m in range(n):
                place_rows(ws[m], slab_ref.at[m])
            for k in range(n):
                w_ref[k * size : (k + 1) * size, :] = slab_ref[k ^ lax.axis_index("dp")]
            for m in range(group):
                part = dot_nn(xs[m][...], w_ref[...]) + b_ref[...]
                qkv_ref[m * block : (m + 1) * block, :] = part.astype(BF)

        attend_kernel(hpd, block, qkv_ref, docq_ref, dock_ref, out_ref, outt_ref, peak_ref, vt_ref)
        for m in range(group):

            @pl.when(i == m)
            def _():
                outs[m][...] = out_ref[...]

    got = launch(
        "attend",
        kernel,
        [*row_in, *qkv_cols, qkv_b, docq, dock],
        in_specs=[pl.BlockSpec((block, features), fixed) for _ in range(group)]
        + [pl.BlockSpec(c.shape, fixed) for c in qkv_cols]
        + [
            pl.BlockSpec((1, 3 * width), fixed),
            pl.BlockSpec((1, block), lambda i: (0, i)),
            pl.BlockSpec((length, 128), fixed),
        ],
        out_specs=[pl.BlockSpec((length, 3 * width), fixed), pl.BlockSpec((features, 3 * width), fixed)]
        + [pl.BlockSpec((block, width), fixed) for _ in range(group)]
        + [
            pl.BlockSpec((width, block), lambda i: (0, i)),
            pl.BlockSpec((8, block), lambda i: (0, i)),
        ],
        out_shape=[sds((length, 3 * width), BF), sds((features, 3 * width), BF)]
        + [sds((block, width), BF) for _ in range(group)]
        + [sds((width, length), F32), sds((8, length), F32)],
        scratch=[
            pltpu.VMEM((hpd, HEAD, length), BF),
            pltpu.VMEM((block, width), BF),
            pltpu.VMEM((n, size, 3 * width), BF),
        ],
        grid=(group,),
    )
    return got[0], got[2 : 2 + group], got[2 + group], got[3 + group], got[1]


def attend_back(qkv, grad_out, outt, peak, docq, dock, hpd):
    group, block = len(grad_out), grad_out[0].shape[0]
    length, width = group * block, hpd * HEAD
    fixed = lambda i: (0, 0)

    def kernel(qkv_ref, *refs):
        dos = refs[:group]
        outt_ref, peak_ref, docq_ref, dock_ref = refs[group : group + 4]
        grad_ref, kt_ref, dk_ref, dv_ref, do_ref = refs[group + 4 :]

        @pl.when(pl.program_id(0) == 0)
        def _():
            for m in range(group):
                do_ref[m * block : (m + 1) * block, :] = dos[m][...]

        attend_back_kernel(
            hpd, block, group, qkv_ref, do_ref, outt_ref, peak_ref, docq_ref, dock_ref, grad_ref, kt_ref, dk_ref, dv_ref
        )

    return launch(
        "attend_back",
        kernel,
        [qkv, *grad_out, outt, peak, docq, dock],
        in_specs=[pl.BlockSpec((length, 3 * width), fixed)]
        + [pl.BlockSpec((block, width), fixed) for _ in range(group)]
        + [
            pl.BlockSpec((width, block), lambda i: (0, i)),
            pl.BlockSpec((8, block), lambda i: (0, i)),
            pl.BlockSpec((1, block), lambda i: (0, i)),
            pl.BlockSpec((length, 128), fixed),
        ],
        out_specs=[pl.BlockSpec((length, 3 * width), fixed)],
        out_shape=[sds((length, 3 * width), BF)],
        scratch=[
            pltpu.VMEM((hpd, HEAD, length), BF),
            pltpu.VMEM((hpd, length, HEAD), F32),
            pltpu.VMEM((hpd, length, HEAD), F32),
            pltpu.VMEM((length, width), BF),
        ],
        grid=(group,),
    )[0]


def place_rows(pieces, ref):
    at = 0
    for p in pieces:
        ref[at : at + p.shape[0], :] = p[...]
        at += p.shape[0]


def mlp_kernel(xs, gs, per, refs):
    n = len(xs)
    w_own, w_other, b1_ref, w2_ref, b2_ref = refs[:5]
    act_ref, gf1_ref, sums_ref = refs[5:8]
    backs, parts = refs[8 : 8 + n], refs[8 + n : 8 + 2 * n]
    w1_ref, x_ref, g_ref, back_ref, part_ref, row_ref = refs[8 + 2 * n :]
    i = pl.program_id(0)
    hidden = w1_ref.shape[1]
    block = x_ref.shape[0] // per

    @pl.when(i == 0)
    def _():
        size = w_own.shape[1] // 2
        whole_rows(w_own, w_other, w1_ref, slice(0, size), slice(0, hidden))
        sums_ref[...] = jnp.zeros_like(sums_ref)
        row_ref[...] = jnp.zeros_like(row_ref)
        span = b2_ref.shape[0]

        def bias(d):
            row_ref[0:1, d * span : (d + 1) * span] = b2_ref[...].astype(F32).reshape(1, span)

        by_index(lax.axis_index("dp"), n, bias)

    for m in range(n):

        @pl.when(i == m // per)
        def _():
            at = pl.ds(m % per * block, block)
            place_rows(xs[m], x_ref.at[at, :])
            place_rows(gs[m], g_ref.at[at, :])

    u = dot_nn(x_ref[...], w1_ref[...]) + b1_ref[...].astype(F32).reshape(1, hidden)
    root = 0.7978845608028654
    squared = u * u
    t = jnp.tanh(root * u * (1.0 + 0.044715 * squared))
    act = (0.5 * u * (1.0 + t)).astype(BF)
    act_ref[...] = act
    slope = 0.5 * (1.0 + t) + 0.5 * u * (1.0 - t * t) * (root * (1.0 + 3 * 0.044715 * squared))
    gf1 = (dot_nt(g_ref[...], w2_ref[...]) * slope).astype(BF)
    gf1_ref[...] = gf1
    back_ref[...] = dot_nt(gf1, w1_ref[...]).astype(BF)
    part_ref[...] = (dot_nn(act, w2_ref[...]) + row_ref[0:1, :]).astype(BF)
    for m in range(n):

        @pl.when(i == m // per)
        def _():
            at = slice(m % per * block, (m % per + 1) * block)
            parts[m][...] = part_ref[at, :]
            backs[m][...] = back_ref[at, :]

    sums_ref[0:1, :hidden] += jnp.sum(gf1.astype(F32), axis=0, keepdims=True)


def grouped(refs, counts):
    out, at = [], 0
    for count in counts:
        out.append(refs[at : at + count])
        at += count
    return out, refs[at:]


def mlp(xs, gs, w_own, w_other, b1, w2, b2):
    n = len(xs)
    block, features = sum(p.shape[0] for p in xs[0]), xs[0][0].shape[1]
    hidden = w2.shape[0]
    per = min(4, n)
    fixed = lambda i: (0, 0)
    piece = pl.BlockSpec((block, features), fixed)
    third = pl.BlockSpec(w_own.shape, lambda i: (0, 0, 0))
    flat = [p for ps in list(xs) + list(gs) for p in ps]
    counts = [len(ps) for ps in list(xs) + list(gs)]

    def kernel(*refs):
        pieces, rest = grouped(refs, counts)
        mlp_kernel(pieces[:n], pieces[n:], per, rest)

    got = launch(
        "mlp",
        kernel,
        flat + [w_own, w_other, b1, w2, b2],
        in_specs=[pl.BlockSpec(p.shape, fixed) for p in flat]
        + [third, third, pl.BlockSpec((hidden,), lambda i: (0,)), pl.BlockSpec((hidden, features), fixed)]
        + [pl.BlockSpec(b2.shape, lambda i: (0,))],
        out_specs=[
            pl.BlockSpec((per * block, hidden), lambda i: (i, 0)),
            pl.BlockSpec((per * block, hidden), lambda i: (i, 0)),
            pl.BlockSpec((8, features), fixed),
        ]
        + [piece] * (2 * n),
        out_shape=[
            sds((n * block, hidden), BF),
            sds((n * block, hidden), BF),
            sds((8, features), F32),
        ]
        + [sds((block, features), BF)] * (2 * n),
        scratch=[
            pltpu.VMEM((features, hidden), BF),
            pltpu.VMEM((per * block, features), BF),
            pltpu.VMEM((per * block, features), BF),
            pltpu.VMEM((per * block, features), BF),
            pltpu.VMEM((per * block, features), BF),
            pltpu.VMEM((8, features), F32),
        ],
        grid=(n // per,),
    )
    return got[:3], got[3 : n + 3], got[n + 3 :]


def wgrad(lefts, rights, name):
    rows, cols = lefts[0].shape[1], rights[0].shape[1]
    block = 384 if rows % 384 == 0 else rows

    def kernel(*refs):
        a_refs, b_refs = refs[: len(lefts)], refs[len(lefts) : -1]

        left = jnp.concatenate([r[...] for r in a_refs], axis=0)
        right = jnp.concatenate([r[...] for r in b_refs], axis=0)
        refs[-1][...] = dot_tn(left, right).astype(BF)

    return launch(
        name,
        kernel,
        list(lefts) + list(rights),
        in_specs=[pl.BlockSpec((a.shape[0], block), lambda i: (0, i)) for a in lefts]
        + [pl.BlockSpec(b.shape, lambda i: (0, 0)) for b in rights],
        out_specs=[pl.BlockSpec((block, cols), lambda i: (i, 0))],
        out_shape=[sds((rows, cols), BF)],
        grid=(rows // block,),
    )[0]


def core_rows(ref, groups, k, mine):
    core = lax.axis_index("blk") % 2
    size = ref.shape[0] // (2 * groups)
    low = ref[2 * k * size : (2 * k + 1) * size, :]
    high = ref[(2 * k + 1) * size : (2 * k + 2) * size, :]
    return jnp.where(core == 0, low, high) if mine else jnp.where(core == 0, high, low)


def other_half(x, groups, name):
    rows, cols = x.shape
    size = rows // (2 * groups)

    def kernel(x_ref, out_ref):
        for k in range(groups):
            out_ref[k * size : (k + 1) * size, :] = core_rows(x_ref, groups, k, False)

    return whole_call(kernel, name, [sds((rows // 2, cols), BF)], [x])[0]


def halves(total, bit):
    size = total.shape[0] // 2
    mine = (lax.axis_index("blk") // bit) % 2
    low, high = total[:size], total[size:]
    return jnp.where(mine == 0, low, high), jnp.where(mine == 0, high, low)


def own_half(x, got, groups, bit, name):
    rows, cols = x.shape
    size = rows // (2 * groups)

    def kernel(x_ref, got_ref, keep_ref, send_ref, all_ref):
        for k in range(groups):
            at = slice(k * size, (k + 1) * size)
            mine = core_rows(x_ref, groups, k, True).astype(F32)
            all_ref[at, :] = (mine + got_ref[at, :].astype(F32)).astype(BF)
        keep_ref[...], send_ref[...] = halves(all_ref[...], bit)

    return whole_call(
        kernel, name, [sds((rows // 4, cols), BF)] * 2, [x, got], [pltpu.VMEM((rows // 2, cols), BF)]
    )


def own_blocks(x, got, n, name):
    rows, cols = x.shape
    size = rows // (2 * n)

    def kernel(x_ref, got_ref, *outs):
        def step(d):
            for m in range(n):
                k = m ^ d
                mine = core_rows(x_ref, n, k, True).astype(F32)
                outs[m][...] = (mine + got_ref[k * size : (k + 1) * size, :].astype(F32)).astype(BF)

        by_index(lax.axis_index("dp"), n, step)

    return whole_call(kernel, name, [sds((size, cols), BF)] * n, [x, got])


def give_back(own, other, name):
    seg, features = own.shape

    def kernel(own_ref, other_ref, out_ref):
        micro = lax.axis_index("blk") // (lax.axis_size("blk") // 2)
        out_ref[micro, 0] = own_ref[...]
        out_ref[1 - micro, 0] = other_ref[...].astype(out_ref.dtype)

    return whole_call(kernel, name, [sds((2, 1, seg, features), own.dtype)], [own, other])[0]


def add_up(refs):
    total = refs[0][...].astype(F32)
    for r in refs[1:]:
        total = total + r[...].astype(F32)
    return total


def fold_sum(parts, bit, name):
    def kernel(*refs):
        keep, send = halves(add_up(refs[:-2]), bit)
        refs[-2][...], refs[-1][...] = keep.astype(BF), send.astype(BF)

    rows, cols = parts[0].shape
    return whole_call(kernel, name, [sds((rows // 2, cols), BF)] * 2, list(parts))


def join_rows(own, got, bit, name):
    def kernel(own_ref, got_ref, out_ref):
        low = (lax.axis_index("blk") // bit) % 2 == 0
        size = own_ref.shape[0]
        out_ref[:size, :] = jnp.where(low, own_ref[...], got_ref[...])
        out_ref[size:, :] = jnp.where(low, got_ref[...], own_ref[...])

    return whole_call(kernel, name, [sds((2 * own.shape[0], own.shape[1]), BF)], [own, got])[0]


def join_blocks(own, got, bit, n, name):
    rows, cols = 2 * own.shape[0], own.shape[1]
    size = rows // n

    def kernel(own_ref, got_ref, *refs):
        outs, all_ref = refs[:-1], refs[-1]
        low = (lax.axis_index("blk") // bit) % 2 == 0
        half = own_ref.shape[0]
        all_ref[:half, :] = jnp.where(low, own_ref[...], got_ref[...])
        all_ref[half:, :] = jnp.where(low, got_ref[...], own_ref[...])

        def step(d):
            for m in range(n):
                outs[m][...] = all_ref[(m ^ d) * size : ((m ^ d) + 1) * size, :]

        by_index(lax.axis_index("dp"), n, step)

    return whole_call(kernel, name, [sds((size, cols), BF)] * n, [own, got], [pltpu.VMEM((rows, cols), BF)])


def sum_of(parts, name, dtype=BF):
    def kernel(*refs):
        refs[-1][...] = add_up(refs[:-1]).astype(dtype)

    return whole_call(kernel, name, [sds(parts[0].shape, dtype)], list(parts))[0]


def take_from(x, got, chips, name):
    def kernel(x_ref, got_ref, out_ref):
        chip = lax.axis_index("blk") // 2
        here = functools.reduce(jnp.logical_or, [chip == c for c in chips])
        out_ref[...] = jnp.where(here, got_ref[...].astype(F32), x_ref[...].astype(F32)).astype(BF)

    return whole_call(kernel, name, [sds(x.shape, BF)], [x, got])[0]


def sum_at(parts, count, name):
    def kernel(*refs):
        refs[-1][...] = add_up([r.at[at : at + count, :] for r, (_, at) in zip(refs, parts)]).astype(BF)

    shape = sds((count, parts[0][0].shape[1]), BF)
    return whole_call(kernel, name, [shape], [x for x, _ in parts])[0]


def qkv_wgrad_kernel(n, group, *refs):
    xs, grad_ref = refs[:group], refs[group]
    outs = refs[group + 1 : group + 1 + n]
    bias_ref, acc_ref = refs[group + 1 + n :]
    block, features = xs[0].shape
    size, width = features // n, grad_ref.shape[1] // 3
    mine = lax.axis_index("dp")
    step = 384 if features % 384 == 0 else features
    for at in range(0, features, step):
        total = dot_tn(xs[0][:, at : at + step], grad_ref[:block, :])
        for m in range(1, group):
            total = total + dot_tn(xs[m][:, at : at + step], grad_ref[m * block : (m + 1) * block, :])
        acc_ref[at : at + step, :] = total
    for m in range(n):
        rows = pl.ds(pl.multiple_of((m ^ mine) * size, size), size)
        outs[m][...] = acc_ref[rows, :].astype(BF)
    total = dot_nn(jnp.ones((8, block * group), BF), grad_ref[...])
    bias_ref[...] = jnp.zeros_like(bias_ref)

    def place(j):
        bias_ref[:, j * width : (j + 1) * width] = total[:, :width]
        bias_ref[:, features + j * width : features + (j + 1) * width] = total[:, 2 * width :]

    by_index(lax.axis_index("blk") % group, group, place)


def place_qkv_kernel(group, *refs):
    parts = refs[:group]
    out_ref, slab_ref = refs[group:]
    mine = lax.axis_index("blk") % group
    size = parts[0].shape[1] // 3
    for m in range(group):
        slab_ref[m] = parts[m][...]
    for j in range(group):
        got = slab_ref[j ^ mine].astype(F32)
        for p in range(3):
            at = p * group * size + j * size
            out_ref[:, at : at + size] = got[:, p * size : (p + 1) * size]


def both_cores(own, other):
    core = lax.axis_index("blk") % 2
    return jnp.where(core == 0, own, other), jnp.where(core == 0, other, own)


def place_fc1(own, other, name):
    n = len(own)
    size, cols = own[0].shape
    wide = n if cols % 128 else 1

    def kernel(*refs):
        out_ref = refs[-1]
        for t in range(wide):
            at = slice(t * cols, (t + 1) * cols)

            def step(k):
                low, high = both_cores(refs[k][...].astype(F32), refs[n + k][...].astype(F32))
                out_ref[:size, at] = low
                out_ref[size:, at] = high

            by_index((pl.program_id(0) * wide + t) ^ lax.axis_index("dp"), n, step)

    piece = pl.BlockSpec((size, cols), lambda j: (0, 0))
    return launch(
        name,
        kernel,
        list(own) + list(other),
        [piece] * (2 * n),
        [pl.BlockSpec((2 * size, wide * cols), lambda j: (0, j))],
        [sds((2 * size, n * cols), F32)],
        grid=(n // wide,),
    )[0]


def both_kernel(half, own_ref, got_ref, out_ref):
    first = lax.axis_index("blk") // half == 0
    own, got = own_ref[...].astype(F32), got_ref[...].astype(F32)
    out_ref[...] = jnp.concatenate([jnp.where(first, own, got), jnp.where(first, got, own)], axis=0).astype(BF)


def add_kernel(a_ref, b_ref, out_ref):
    out_ref[...] = (a_ref[...].astype(F32) + b_ref[...].astype(F32)).astype(out_ref.dtype)


def place_cores_kernel(own_ref, other_ref, out_ref):
    size = out_ref.shape[0] // 2
    low, high = both_cores(own_ref[...].astype(F32), other_ref[...].astype(F32))
    out_ref[:size, :] = low
    out_ref[size:, :] = high


def gather_sums_kernel(in_ref, mid_ref, out_ref, fc1_ref, fc2_ref, qv_ref, all_ref):
    features = out_ref.shape[1]
    all_ref[...] = jnp.zeros_like(all_ref)
    all_ref[:DOCS, : 2 * features] = in_ref[:DOCS, :]
    all_ref[:DOCS, 2 * features : 5 * features] = mid_ref[:DOCS, : 3 * features]
    all_ref[:DOCS, 5 * features :] = out_ref[:DOCS, :]
    row = slice(DOCS, DOCS + 1)
    all_ref[row, :features] = fc1_ref[0:1, :]
    all_ref[row, features : 2 * features] = fc2_ref[row, :]
    all_ref[row, 2 * features : 3 * features] = mid_ref[row, 3 * features :]
    all_ref[row, 3 * features : 5 * features] = qv_ref[0:1, :]


def ada_kernel(n, *refs):
    slots = refs[:n]
    cols_ref, w_ref = refs[n : n + 2]
    wgrad_ref, rows_ref = refs[n + 2 : n + 4]
    conds = refs[n + 4 :]
    got, fc1, rest = [], 0.0, 0.0
    for m in range(n):
        got.append(slots[m][:DOCS, :].astype(F32))
        got.append(slots[m][8 : 8 + DOCS, :].astype(F32))
        bias = slots[m][DOCS : DOCS + 1, :].astype(F32) + slots[m][8 + DOCS : 9 + DOCS, :].astype(F32)
        fc1 = bias if m == 0 else fc1
        rest = rest + bias
    got = jnp.concatenate(got, axis=0)
    rows_ref[...] = jnp.concatenate(
        [jnp.sum(got, axis=0, keepdims=True), rest, fc1, jnp.zeros((5, rest.shape[1]), F32)], axis=0
    )
    got = got.astype(BF)
    wgrad_ref[...] = dot_tn(cols_ref[...].astype(BF), got)
    back = dot_nt(got, w_ref[...])
    first = pl.program_id(0) == 0
    for m in range(n):
        part = back[8 * m : 8 * m + 8, :]
        conds[m][...] = part + jnp.where(first, 0.0, conds[m][...])


def ada(slots, cols, weight):
    n = len(slots)
    dshard, span = weight.shape
    block = span // 6
    return launch(
        "ada",
        functools.partial(ada_kernel, n),
        [*slots, cols, weight],
        in_specs=[pl.BlockSpec((16, block), lambda i: (0, i))] * n
        + [pl.BlockSpec(cols.shape, lambda i: (0, 0)), pl.BlockSpec((dshard, block), lambda i: (0, i))],
        out_specs=[pl.BlockSpec((dshard, block), lambda i: (0, i)), pl.BlockSpec((8, block), lambda i: (0, i))]
        + [pl.BlockSpec((8, dshard), lambda i: (0, 0))] * n,
        out_shape=[sds((dshard, span), F32), sds((8, span), F32)] + [sds((8, dshard), F32)] * n,
        grid=(6,),
    )


def biases_kernel(n, rows_ref, ada_ref, qv_ref, proj_ref, fc1_ref, fc2_ref):
    features = rows_ref.shape[1] // 6
    span, size = ada_ref.shape[0], fc2_ref.shape[0]

    def step(d):
        def part(i):
            at = i * features + d * size
            return rows_ref[1:2, at : at + size]

        ada_ref[...] = rows_ref[0:1, d * span : (d + 1) * span].reshape(span)
        fc2_ref[...] = part(1).reshape(size)
        proj_ref[...] = part(2).reshape(size)
        qv_ref[0:1, :] = part(3)
        qv_ref[1:2, :] = part(4)

    by_index(lax.axis_index("dp"), n, step)
    fc1_ref[...] = rows_ref[2:3, : fc1_ref.shape[0]].reshape(fc1_ref.shape[0])


def cond_kernel(n, *refs):
    parts, cond_ref, out_ref, slab_ref = refs[:n], refs[n], refs[n + 1], refs[n + 2]
    dp = lax.axis_index("dp")
    for m in range(n):
        slab_ref[m] = parts[m][...]
    grad = jnp.concatenate([slab_ref[k ^ dp] for k in range(n)], axis=1)
    for u in range(2):
        cond = cond_ref[u, 0].astype(F32)
        sig = 1.0 / (1.0 + jnp.exp(-cond))
        out_ref[u, 0] = grad[u * DOCS : (u + 1) * DOCS] * (sig * (1.0 + cond * (1.0 - sig)))


def local(
    latents,
    conditions,
    doc_lengths,
    cotangent,
    ada_weight,
    ada_bias,
    qkv_weight,
    qv_bias,
    proj_weight,
    proj_bias,
    fc1_weight,
    fc1_bias,
    fc2_weight,
    fc2_bias,
):
    n_dp, n_blk = lax.axis_size("dp"), lax.axis_size("blk")
    dp, blk = lax.axis_index("dp"), lax.axis_index("blk")
    half = n_blk // 2
    group = half
    core, micro = blk % 2, blk // half
    seg, features = latents.shape[2], latents.shape[3]
    hidden = fc1_weight.shape[1] // n_dp
    dshard = features // n_dp
    hpd = HEADS // group
    width = hpd * HEAD
    hhalf, dhalf = hidden // 2, dshard // 2
    tokens = 2 * seg
    LAST.clear()
    masks = [2 * i for i in range(group // 2)] + [2 * i + 1 for i in range(group // 2)]

    act_shape = sds((tokens, features), BF)
    half_shape = sds((seg, features), BF)
    full_shape = sds((tokens, features), F32)
    sums_shape = sds((16, features), F32)
    full_vmem = pltpu.VMEM((tokens, features), F32)
    v = types.SimpleNamespace()
    chip_bits = bits_of(2, n_blk)

    def step_open():
        args = [conditions, proj_bias, qv_bias, doc_lengths]
        v.pack, v.docq, v.dock, v.pick_mod, v.pick_sum = launch(
            "open",
            functools.partial(open_kernel, half, seg),
            args,
            [pl.BlockSpec(x.shape, lambda i, n=x.ndim: (0,) * n) for x in args[:3]] + [SM],
            [VM] * 5,
            [
                sds((16, features), BF),
                sds((1, group * tokens), jnp.int32),
                sds((group * tokens, 128), jnp.int32),
                sds((tokens, 32), BF),
                sds((16, tokens), BF),
            ],
            grid=(1,),
        )
        v.pack = direct({m: v.pack for m in range(n_dp)}, "dp")

    def step_lat():
        v.lat_own, send = whole_call(functools.partial(part_ways_kernel, half), "lat", [half_shape] * 2, [latents])
        v.lat_got = swap(send, "blk", half)

    def step_cot():
        v.cot_own, send = whole_call(functools.partial(part_ways_kernel, half), "cot", [half_shape] * 2, [cotangent])
        v.cot_got = swap(send, "blk", half)

    def step_qkv_cols():
        (cols,) = whole_call(
            functools.partial(qkv_cols_kernel, group), "qkv_cols", [sds((dshard, 3 * width), BF)], [qkv_weight]
        )
        v.qkv_cols = spread_dp(cols)

    def step_mod_part():
        *parts, v.cond_cols, v.proj_b, v.qkv_bias = whole_call(
            functools.partial(mod_part_kernel, n_dp, group),
            "mod_part",
            [sds((DOCS, 6 * features), F32)] * n_dp
            + [sds((8 * n_dp, dshard), F32), sds((1, features), F32), sds((1, 3 * width), F32)],
            [v.pack[m] for m in range(n_dp)] + [ada_weight, ada_bias],
            [pltpu.VMEM((8, 6 * features), F32), pltpu.VMEM((n_dp, 8, features), F32)],
        )
        v.mod_parts = direct(dict(enumerate(parts)), "dp")

    def step_mod_all():
        parts = [v.mod_parts[m] for m in range(n_dp)]
        (v.mod,) = whole_call(mod_all_kernel, "mod_all", [sds((32, 6 * features), BF)], parts)

    def step_attn_in():
        attn_in, v.latent = whole_call(
            attn_in_kernel,
            "attn_in",
            [act_shape] * 2,
            [v.lat_own, v.lat_got, v.pick_mod, v.mod],
            [full_vmem] * 2,
        )
        rows = {0: attn_in}
        for bit in bits_of(2, group):
            for m in list(rows):
                rows[m | bit] = swap(rows[m], "blk", bit)
        for m in list(rows):
            rows[m | 1] = swap(rows[m], "blk", 1)
        v.row_in = [rows[m] for m in masks]

    def step_grad_fc2():
        grad_fc2, v.cot, v.sums_fc2 = whole_call(
            grad_fc2_kernel,
            "grad_fc2",
            [act_shape, act_shape, sums_shape],
            [v.cot_own, v.cot_got, v.pick_mod, v.pick_sum, v.mod],
        )
        v.all_grad = spread_dp(grad_fc2)

    def step_cuts():
        move = whole_call(
            functools.partial(cuts_kernel, n_dp),
            "cuts",
            [sds((2 * dhalf, features), BF)] * n_dp,
            [fc1_weight, proj_weight],
        )
        v.move = direct(dict(enumerate(move)), "dp")

    def step_attend():
        v.qkv, outs, v.outt, v.peak, v.qkv_w = attend(
            v.row_in, v.qkv_cols, v.qkv_bias, v.docq, v.dock, hpd
        )
        v.outs = direct(dict(zip(masks, outs)), "blk")

    def step_stack():
        (v.move_own,) = whole_call(
            functools.partial(stack_kernel, n_dp),
            "stack",
            [sds((n_dp, 2 * dhalf, features), BF)],
            [v.move[m] for m in range(n_dp)],
        )
        v.move_other = swap(v.move_own, "blk", 1)

    def step_mix():
        v.low, v.attn_proj, v.mid, mlp_in, v.proj_w = whole_call(
            functools.partial(mix_kernel, group),
            "mix",
            [act_shape, full_shape, full_shape, act_shape, sds((group, width, features), BF)],
            [v.outs[m] for m in range(group)]
            + [v.move_own, v.move_other, v.proj_b, v.latent, v.pick_mod, v.mod],
            [pltpu.VMEM((features, features), BF), pltpu.VMEM((group, tokens, width), BF)] + [full_vmem] * 3,
        )
        v.all_in = spread_dp(mlp_in)

    def step_mlp():
        (v.act, v.grad_fc1, v.sums_fc1), back, part = mlp(
            v.all_in, v.all_grad, v.move_own, v.move_other, fc1_bias, fc2_weight, fc2_bias
        )
        v.back = direct(dict(enumerate(back)), "dp")
        v.part = direct(dict(enumerate(part)), "dp")

    def flat(pieces):
        return [p for ps in pieces for p in ps]

    def step_fc2_wgrad():
        v.fc2_g = wgrad([v.act], flat(v.all_grad), "fc2_wgrad")

    def step_fc1_wgrad():
        v.fc1_g = wgrad(flat(v.all_in), [v.grad_fc1], "fc1_wgrad")

    def step_turn():
        v.gmid, v.grad_proj, v.sums_mid, *grad_attn = whole_call(
            functools.partial(turn_kernel, n_dp, group),
            "turn",
            [full_shape, act_shape, sds((16, 4 * features), F32)] + [sds((tokens, width), BF)] * group,
            [v.back[m] for m in range(n_dp)]
            + [v.cot, v.mid, v.attn_proj, v.proj_w, v.pick_mod, v.pick_sum, v.mod],
            [full_vmem] * 5,
        )
        v.grad_attn = direct(dict(enumerate(grad_attn)), "blk")

    def step_proj_wgrad():
        v.proj_g = wgrad([v.low], [v.grad_proj], "proj_wgrad")

    def halve(x, groups, name):
        return swap(other_half(x, groups, name), "blk", 1)

    def step_fc2_other():
        v.fc2_got = halve(v.fc2_g, 1, "fc2_other")

    def step_fc1_other():
        v.fc1_got = halve(v.fc1_g, n_dp, "fc1_other")

    def step_proj_other():
        v.proj_got = halve(v.proj_g, n_dp, "proj_other")

    def step_fc2_own():
        v.fc2 = CubeSum(*own_half(v.fc2_g, v.fc2_got, 1, chip_bits[0], "fc2_own"), chip_bits, "fc2_cube")

    def step_fc1_own():
        v.fc1 = CubeSum(*own_half(v.fc1_g, v.fc1_got, n_dp, chip_bits[0], "fc1_own"), chip_bits, "fc1_cube")

    def step_fc2_a():
        v.fc2.fold()

    def step_fc2_b():
        v.fc2.total()

    def step_fc2_j():
        v.fc2.join()

    def step_fc1_a():
        v.fc1.fold()

    def step_fc1_b():
        v.fc1.total()

    def step_fc1_j():
        v.fc1.join()

    def step_proj_a():
        v.proj.until(2)

    def step_proj_b():
        v.proj.until(1)

    def step_fc2_c():
        v.fc2_own = join_rows(v.fc2.x, v.fc2.got, chip_bits[0], "fc2_cube")
        v.fc2_other = swap(v.fc2_own, "blk", 1)

    def step_fc1_c():
        blocks = join_blocks(v.fc1.x, v.fc1.got, chip_bits[0], n_dp, "fc1_cube")
        blocks = direct(dict(enumerate(blocks)), "dp")
        v.fc1_own = [blocks[m] for m in range(n_dp)]
        v.fc1_other = [swap(x, "blk", 1) for x in v.fc1_own]

    def step_proj_blocks():
        v.proj_parts = direct(
            dict(enumerate(own_blocks(v.proj_g, v.proj_got, n_dp, "proj_blocks"))), "dp"
        )

    def step_proj_sum():
        v.proj = LineSum(sum_of([v.proj_parts[m] for m in range(n_dp)], "proj_sum"), "proj_line")

    def step_proj_c():
        v.proj.until(0)
        v.proj_other = swap(v.proj.x, "blk", 1)

    def step_attend_back():
        grad_qkv = attend_back(
            v.qkv, [v.grad_attn[m] for m in masks], v.outt, v.peak, v.docq, v.dock, hpd
        )
        v.grad_qkv = grad_qkv
        count = (group // 2) * tokens
        send = swap(dot_nt(grad_qkv[count:], v.qkv_w).astype(BF), "blk", 1)
        keep = dot_nt(grad_qkv[:count], v.qkv_w).astype(BF)
        v.blocks = {m: [(keep, i * tokens), (send, i * tokens)] for i, m in enumerate(masks[: group // 2])}

    def step_qkv_wgrad():
        *qkv_g, v.sums_qv = whole_call(
            functools.partial(qkv_wgrad_kernel, n_dp, group),
            "qkv_wgrad",
            [sds((dshard, 3 * width), BF)] * n_dp + [sds((8, 2 * features), F32)],
            v.row_in + [v.grad_qkv],
            [pltpu.VMEM((features, 3 * width), F32)],
        )
        v.qkv_g = direct(dict(enumerate(qkv_g)), "dp")

    def step_outs():
        v.block_own, other, v.sums_out = whole_call(
            functools.partial(outs_kernel, n_dp),
            "outs",
            [half_shape, half_shape, sums_shape],
            [v.part[m] for m in range(n_dp)] + [v.cot, v.mid, v.pick_mod, v.pick_sum, v.mod],
            [pltpu.VMEM((tokens, features), BF)] + [full_vmem] * 2,
        )
        v.block_other = swap(other, "blk", half)

    def step_attn_sum():
        blocks = v.blocks
        for bit in reversed(bits_of(2, group)):
            for m in [m for m in blocks if m & bit]:
                blocks[m ^ bit].append((swap(sum_at(blocks.pop(m), tokens, "attn_sum"), "blk", bit), 0))

    def step_finish():
        parts = v.blocks[0]
        v.latent_own, other, v.sums_in = whole_call(
            functools.partial(finish_kernel, [at for _, at in parts], seg),
            "finish",
            [sds((seg, features), F32), half_shape, sds((16, 2 * features), F32)],
            [x for x, _ in parts] + [v.latent, v.gmid, v.pick_mod, v.pick_sum, v.mod],
            [full_vmem] * 3,
        )
        v.latent_other = swap(other, "blk", half)

    def step_qkv_sum():
        v.qkv_x = sum_of([v.qkv_g[m] for m in range(n_dp)], "qkv_sum")
        v.qkv_got = swap(v.qkv_x, "blk", half)

    def step_qkv_sum2():
        parts = {0: sum_of([v.qkv_x, v.qkv_got], "qkv_sum")}
        for bit in bits_of(2, group):
            for m in list(parts):
                parts[m | bit] = swap(parts[m], "blk", bit)
        for m in list(parts):
            parts[m | 1] = swap(parts[m], "blk", 1)
        v.qkv_parts = parts

    def step_gather_sums():
        (v.sums,) = whole_call(
            gather_sums_kernel,
            "gather_sums",
            [sds((8, 6 * features), F32)],
            [v.sums_in, v.sums_mid, v.sums_out, v.sums_fc1, v.sums_fc2, v.sums_qv],
        )
        v.sums_got = swap(v.sums, "blk", 1)

    def step_sums_c():
        for bit in bits_of(2, group):
            (v.sums,) = whole_call(add_kernel, "sums", [sds(v.sums.shape, BF)], [v.sums, v.sums_got])
            v.sums_got = swap(v.sums, "blk", bit)

    def step_sums_g():
        (v.sums,) = whole_call(add_kernel, "sums", [sds(v.sums.shape, BF)], [v.sums, v.sums_got])
        v.sums_got = swap(v.sums, "blk", half)

    def step_sums_h():
        (both,) = whole_call(
            functools.partial(both_kernel, half), "both", [sds((16, 6 * features), BF)], [v.sums, v.sums_got]
        )
        v.slots = direct({m: both for m in range(n_dp)}, "dp")

    def step_ada():
        v.ada_wgrad, v.rows_sum, *parts = ada([v.slots[m] for m in range(n_dp)], v.cond_cols, ada_weight)
        v.cond_parts = direct(dict(enumerate(parts)), "dp")

    def step_biases():
        spans = [ada_bias.shape, (2, dshard), (dshard,), (hidden,), (dshard,)]
        v.ada_bgrad, v.qv_bgrad, v.proj_bgrad, v.fc1_bgrad, v.fc2_bgrad = whole_call(
            functools.partial(biases_kernel, n_dp), "biases", [sds(x, F32) for x in spans], [v.rows_sum]
        )

    def step_cond():
        (v.cond_grad,) = whole_call(
            functools.partial(cond_kernel, n_dp),
            "cond_grad",
            [sds((2, 1, DOCS, features), F32)],
            [v.cond_parts[m] for m in range(n_dp)] + [conditions],
            [pltpu.VMEM((n_dp, 8, dshard), F32)],
        )

    def step_place_qkv():
        (v.qkv_wgrad,) = whole_call(
            functools.partial(place_qkv_kernel, group),
            "place_qkv",
            [sds((dshard, 3 * features), F32)],
            [v.qkv_parts[m] for m in range(group)],
            [pltpu.VMEM((group, dshard, 3 * width), BF)],
        )

    def step_place_fc2():
        (v.fc2_wgrad,) = whole_call(
            place_cores_kernel, "place_fc2", [sds((hidden, features), F32)], [v.fc2_own, v.fc2_other]
        )

    def step_place_proj():
        (v.proj_wgrad,) = whole_call(
            place_cores_kernel, "place_proj", [sds((dshard, features), F32)], [v.proj.x, v.proj_other]
        )

    def step_place_fc1():
        v.fc1_wgrad = place_fc1(v.fc1_own, v.fc1_other, "place_fc1")

    def step_block_out():
        v.block_out = give_back(v.block_own, v.block_other, "block_out")

    def step_latent_grad():
        v.latent_grad = give_back(v.latent_own, v.latent_other, "latent_grad")

    for step in (
        step_cuts, step_lat, step_open, step_qkv_cols, step_mod_part, step_mod_all, step_attn_in, step_cot,
        step_attend, step_grad_fc2, step_stack, step_mix, step_mlp, step_fc2_wgrad, step_fc1_wgrad, step_turn,
        step_fc2_other, step_fc1_other, step_fc2_own, step_attend_back, step_attn_sum, step_fc1_own,
        step_qkv_wgrad, step_fc2_a, step_proj_wgrad, step_outs, step_finish, step_gather_sums, step_fc2_b,
        step_sums_c, step_qkv_sum, step_fc1_a, step_fc2_j, step_sums_g, step_proj_other, step_proj_blocks,
        step_sums_h, step_fc1_b, step_proj_sum, step_fc2_c, step_ada, step_proj_a, step_biases, step_qkv_sum2,
        step_place_fc2, step_cond, step_fc1_j, step_proj_b, step_fc1_c, step_latent_grad, step_place_qkv,
        step_proj_c, step_block_out, step_place_proj, step_place_fc1,
    ):
        step()

    return (
        v.block_out,
        v.latent_grad,
        v.cond_grad,
        v.ada_wgrad,
        v.ada_bgrad,
        v.qkv_wgrad,
        v.qv_bgrad,
        v.proj_wgrad,
        v.proj_bgrad,
        v.fc1_wgrad,
        v.fc1_bgrad,
        v.fc2_wgrad,
        v.fc2_bgrad,
    )


def solution(mesh):
    in_specs = (
        P(None, "dp", "blk", None),
        P(None, "dp", None, None),
        P(None, "dp", None),
        P(None, "dp", "blk", None),
        P("dp", None),
        P("dp"),
        P("dp", None),
        P(None, "dp"),
        P("dp", None),
        P("dp"),
        P("dp", None),
        P("dp"),
        P("dp", None),
        P("dp"),
    )
    out_specs = (
        P(None, "dp", "blk", None),
        P(None, "dp", "blk", None),
        P(None, "dp", None, None),
        P("dp", None),
        P("dp"),
        P("dp", None),
        P(None, "dp"),
        P("dp", None),
        P("dp"),
        P("dp", None),
        P("dp"),
        P("dp", None),
        P("dp"),
    )
    return jax.shard_map(local, mesh=mesh, in_specs=in_specs, out_specs=out_specs, check_vma=False)
```

```python
import functools
import math
import types

import jax
import jax.numpy as jnp
from jax import lax
from jax.experimental import pallas as pl
from jax.experimental.pallas import tpu as pltpu
from jax.sharding import PartitionSpec as P

HEADS = 16
HEAD = 72
DOCS = 4
NORM_EPS = 1e-06
MASKED = -1e30
LOG2E = 1.4426950408889634
SCALE = HEAD ** (-0.5)
VMEM_LIMIT = 56 * 1024 * 1024
HIGHEST = lax.Precision.HIGHEST
BF = jnp.bfloat16
F32 = jnp.float32


def normalize(values):
    center = jnp.mean(values, axis=-1, keepdims=True)
    centred = values - center
    inverse = lax.rsqrt(jnp.mean(centred * centred, axis=-1, keepdims=True) + NORM_EPS)
    return centred * inverse, inverse


def normalize_back(grad, normed, inverse):
    first = jnp.mean(grad, axis=-1, keepdims=True)
    second = jnp.mean(grad * normed, axis=-1, keepdims=True)
    return inverse * (grad - first - normed * second)


def dot_nn(a, b):
    return lax.dot_general(a, b, (((1,), (0,)), ((), ())), preferred_element_type=F32)


def dot_nt(a, b):
    return lax.dot_general(a, b, (((1,), (1,)), ((), ())), preferred_element_type=F32)


def dot_tn(a, b):
    return lax.dot_general(a, b, (((0,), (0,)), ((), ())), preferred_element_type=F32)


def swap(x, axis, mask):
    count = lax.axis_size(axis)
    return lax.ppermute(x, axis, [(i, i ^ mask) for i in range(count)])


def bits_of(low, high):
    out = []
    while low < high:
        out.append(low)
        low *= 2
    return out


def direct(blocks, axis):
    return {m: (b if m == 0 else swap(b, axis, m)) for m, b in blocks.items()}


def spread_dp(x):
    n = lax.axis_size("dp")
    blocks = {0: [x]}
    if n == 4:
        cut = x.shape[0] // 2
        one, two = swap(x, "dp", 1), swap(x, "dp", 2)
        blocks[1], blocks[2] = [one], [two]
        blocks[3] = [swap(one[:cut], "dp", 2), swap(two[cut:], "dp", 1)]
        return [blocks[m] for m in range(n)]
    for bit in bits_of(1, n):
        for mask in list(blocks):
            blocks[mask | bit] = [swap(blocks[mask][0], "dp", bit)]
    return [blocks[m] for m in range(n)]


def line_pairs():
    chips = lax.axis_size("blk") // 2
    mid = chips // 2
    inward = [[(s, s + 1), (chips - 1 - s, chips - 2 - s)] for s in range(mid - 1)]
    outward = [[(mid - 1 - s, mid - 2 - s), (mid + s, mid + s + 1)] for s in range(mid - 1)]
    return inward, [(mid - 1, mid), (mid, mid - 1)], outward


def along(x, pairs):
    return lax.ppermute(x, "blk", [(2 * a + c, 2 * b + c) for a, b in pairs for c in range(2)])


class LineSum:
    def __init__(self, x, name):
        inward, middle, outward = line_pairs()
        self.steps = [("add", p) for p in inward] + [("add", middle)] + [("take", p) for p in outward]
        self.x, self.name, self.at = x, name, 0
        self.got = along(x, self.steps[0][1])

    def step(self):
        kind, pairs = self.steps[self.at]
        if kind == "add":
            self.x = sum_of([self.x, self.got], self.name)
        else:
            self.x = take_from(self.x, self.got, [b for _, b in pairs], self.name)
        self.at += 1
        if self.at < len(self.steps):
            self.got = along(self.x, self.steps[self.at][1])

    def until(self, left):
        while len(self.steps) - self.at > left:
            self.step()


class CubeSum:
    def __init__(self, keep, send, bits, name):
        self.x, self.bits, self.name = keep, bits, name
        self.got = swap(send, "blk", bits[0])

    def fold(self):
        for bit in self.bits[1:]:
            self.x, send = fold_sum([self.x, self.got], bit, self.name)
            self.got = swap(send, "blk", bit)

    def total(self):
        self.x = sum_of([self.x, self.got], self.name)
        self.got = swap(self.x, "blk", self.bits[-1])

    def join(self):
        for i in range(len(self.bits) - 1, 0, -1):
            self.x = join_rows(self.x, self.got, self.bits[i], self.name)
            self.got = swap(self.x, "blk", self.bits[i - 1])


def allowed_mask(dock_ref, docq_ref, width):
    keys = dock_ref[...]
    keys = jnp.concatenate([keys] * (width // keys.shape[1]), axis=1)
    return keys == docq_ref[...]


def attend_kernel(hpd, block, qkv_ref, docq_ref, dock_ref, out_ref, outt_ref, peak_ref, vt_ref):
    i = pl.program_id(0)
    width = hpd * HEAD
    rows = pl.ds(pl.multiple_of(i * block, block), block)

    @pl.when(i == 0)
    def _():
        for h in range(hpd):
            v = qkv_ref[:, 2 * width + h * HEAD : 2 * width + (h + 1) * HEAD]
            vt_ref[h] = v.astype(F32).T.astype(BF)

    allowed = allowed_mask(dock_ref, docq_ref, block)
    outs, peaks = [], []
    for h in range(hpd):
        q = qkv_ref[rows, h * HEAD : (h + 1) * HEAD]
        k = qkv_ref[:, width + h * HEAD : width + (h + 1) * HEAD]
        scores = jnp.where(allowed, dot_nt(k, q), MASKED)
        peak = jnp.max(scores, axis=0, keepdims=True)
        weight = jnp.exp2((scores - peak) * (SCALE * LOG2E))
        total = jnp.sum(weight, axis=0, keepdims=True)
        outs.append(dot_nn(vt_ref[h], weight.astype(BF)) / total)
        peaks.append(peak + jnp.log(total) * (1.0 / SCALE))
    out = jnp.concatenate(outs, axis=0)
    outt_ref[...] = out
    out_ref[...] = out.T.astype(BF)
    peaks.append(jnp.zeros((8 - hpd, block), F32))
    peak_ref[...] = jnp.concatenate(peaks, axis=0)


def attend_back_kernel(
    hpd, block, steps, qkv_ref, do_ref, outt_ref, peak_ref, docq_ref, dock_ref, grad_ref, kt_ref, dk_ref, dv_ref
):
    i = pl.program_id(0)
    width = hpd * HEAD
    rows = pl.ds(pl.multiple_of(i * block, block), block)

    @pl.when(i == 0)
    def _():
        for h in range(hpd):
            k = qkv_ref[:, width + h * HEAD : width + (h + 1) * HEAD]
            kt_ref[h] = k.astype(F32).T.astype(BF)
        dk_ref[...] = jnp.zeros_like(dk_ref)
        dv_ref[...] = jnp.zeros_like(dv_ref)

    allowed = allowed_mask(dock_ref, docq_ref, block)
    dots = do_ref[rows, :].astype(F32).T * outt_ref[...]
    dqs = []
    for h in range(hpd):
        part = slice(h * HEAD, (h + 1) * HEAD)
        q = qkv_ref[rows, part]
        k = qkv_ref[:, width + h * HEAD : width + (h + 1) * HEAD]
        v = qkv_ref[:, 2 * width + h * HEAD : 2 * width + (h + 1) * HEAD]
        do = do_ref[rows, part]
        row_dot = jnp.sum(dots[part], axis=0, keepdims=True)
        scores = jnp.where(allowed, dot_nt(k, q), MASKED)
        probs = jnp.exp2((scores - peak_ref[h : h + 1, :]) * (SCALE * LOG2E))
        grad_scores = (probs * (dot_nt(v, do) - row_dot)).astype(BF)
        dv_ref[h] += dot_nn(probs.astype(BF), do)
        dk_ref[h] += dot_nn(grad_scores, q)
        dqs.append(dot_nn(kt_ref[h], grad_scores))
    grad_ref[rows, :width] = (jnp.concatenate(dqs, axis=0) * SCALE).T.astype(BF)

    @pl.when(i == steps - 1)
    def _():
        dk = jnp.concatenate([dk_ref[h] for h in range(hpd)], axis=1) * SCALE
        dv = jnp.concatenate([dv_ref[h] for h in range(hpd)], axis=1)
        grad_ref[:, width : 2 * width] = dk.astype(BF)
        grad_ref[:, 2 * width :] = dv.astype(BF)


WORK = {"attend": 6, "attend_back": 8, "mlp": 4, "qkv_wgrad": 12, "mod_part": 8}


def params(name, grid, arrays, scratch):
    held = sum(a.size * a.dtype.itemsize for a in arrays) * (1 if grid is None or grid == (1,) else 2)
    held += sum(math.prod(x.shape) * jnp.dtype(x.dtype).itemsize for x in scratch)
    limit = min(VMEM_LIMIT, held + WORK.get(name, 6) * 1024 * 1024)
    return pltpu.CompilerParams(
        vmem_limit_bytes=limit, dimension_semantics=None if grid is None else ("arbitrary",)
    )


LIGHT = pl.CostEstimate(flops=1000, bytes_accessed=1000, transcendentals=0)
VM = pl.BlockSpec(memory_space=pltpu.VMEM)
SM = pl.BlockSpec(memory_space=pltpu.SMEM)
ANY = pl.BlockSpec(memory_space=pl.ANY)


def sds(shape, dtype):
    return jax.ShapeDtypeStruct(shape, dtype)


LAST = []


def launch(name, kernel, args, in_specs, out_specs, out_shape, scratch=(), grid=None):
    count, after = len(args), list(LAST)

    def body(*refs):
        kernel(*refs[:count], *refs[count + len(after) :])

    got = pl.pallas_call(
        body,
        **({} if grid is None else {"grid": grid}),
        in_specs=list(in_specs) + [ANY] * len(after),
        out_specs=list(out_specs),
        out_shape=list(out_shape),
        scratch_shapes=list(scratch),
        compiler_params=params(name, grid, list(args) + list(out_shape), scratch),
        cost_estimate=LIGHT,
        name=name,
    )(*args, *after)
    LAST[:] = [min(got, key=lambda a: a.size)]
    return got


def whole_call(kernel, name, outs, args, scratch=()):
    specs = [SM if a.dtype == jnp.int32 and a.ndim != 2 else VM for a in args]
    return launch(name, kernel, args, specs, [VM] * len(outs), outs, scratch)


CHUNK = 32


def by_rows(count, step):
    def inner(i, carry):
        step(pl.ds(pl.multiple_of(i * CHUNK, CHUNK), CHUNK))
        return carry

    lax.fori_loop(0, count // CHUNK, inner, 0, unroll=2)


def doc_sums(pick, grads):
    high = grads.astype(BF)
    low = (grads - high.astype(F32)).astype(BF)
    return dot_nn(pick, high) + dot_nn(pick, low)


def by_index(index, count, step):
    for i in range(count):

        @pl.when(index == i)
        def _():
            step(i)


def part_ways_kernel(half, x_ref, own_ref, send_ref):
    micro = lax.axis_index("blk") // half
    own_ref[...] = x_ref[micro, 0]
    send_ref[...] = x_ref[1 - micro, 0]


def open_kernel(half, seg, cond_ref, bias_ref, qv_ref, lengths_ref, *refs):
    pack_ref, docq_ref, dock_ref, mod_ref, sum_ref = refs
    blk = lax.axis_index("blk")
    micro = blk // half
    group = half
    features = pack_ref.shape[1]
    tokens = 2 * seg
    dshard = qv_ref.shape[1]
    cond = jnp.concatenate([cond_ref[0, 0], cond_ref[1, 0]], axis=0).astype(F32)
    silu = cond / (1.0 + jnp.exp(-cond))
    small = jnp.concatenate(
        [bias_ref[...].astype(F32).reshape(1, dshard), qv_ref[0:1, :].astype(F32), qv_ref[1:2, :].astype(F32)], axis=1
    )
    small = jnp.pad(small, ((0, 7), (0, features - 3 * dshard)))
    pack_ref[...] = jnp.concatenate([silu, small], axis=0).astype(BF)
    ends, last = [], 0
    for d in range(DOCS):
        last = last + lengths_ref[micro, 0, d]
        ends.append(last)

    def docs(index, shape, dim):
        spot = lax.broadcasted_iota(jnp.int32, shape, dim) + index * seg
        found = jnp.zeros(shape, jnp.int32)
        for d in range(DOCS):
            found = found + jnp.where(spot >= ends[d], 1, 0)
        return found

    for i in range(group):
        mask = 2 * (i % (group // 2)) + i // (group // 2)
        for part in range(2):
            at = i * tokens + part * seg
            index = (blk ^ mask) ^ (half * part)
            dock_ref[at : at + seg, :] = docs(index, (seg, 128), 0)
            docq_ref[:, at : at + seg] = docs(index, (8, seg), 1)[:1]
    for part in range(2):
        at = part * seg
        index = blk ^ (half * part)
        col = lax.broadcasted_iota(jnp.int32, (seg, 32), 1)
        same = (col % DOCS == docs(index, (seg, 32), 0)) & (col < 3 * DOCS)
        mod_ref[at : at + seg, :] = jnp.where(same, 1.0, 0.0).astype(BF)
        row = lax.broadcasted_iota(jnp.int32, (16, seg), 0)
        same = (row == docs(index, (16, seg), 1)) | (row == DOCS)
        sum_ref[:, at : at + seg] = jnp.where(same, 1.0, 0.0).astype(BF)


def qkv_cols_kernel(group, w_ref, out_ref):
    width = out_ref.shape[1] // 3

    def step(j):
        for p in range(3):
            at = p * group * width + j * width
            out_ref[:, p * width : (p + 1) * width] = w_ref[:, at : at + width]

    by_index(lax.axis_index("blk") % group, group, step)


def cuts_kernel(n, fc1_ref, proj_ref, *outs):
    core = lax.axis_index("blk") % 2
    size = outs[0].shape[0] // 2
    hidden = fc1_ref.shape[1] // n

    def half(ref, cols):
        return jnp.where(core == 0, ref[:size, cols], ref[size:, cols])

    def step(d):
        for m in range(n):
            outs[m][:size, :hidden] = half(fc1_ref, slice((d ^ m) * hidden, ((d ^ m) + 1) * hidden))

    by_index(lax.axis_index("dp"), n, step)
    for m in range(n):
        outs[m][size:, :] = half(proj_ref, slice(None))


def stack_kernel(n, *refs):
    for m in range(n):
        refs[-1][m] = refs[m][...]


def whole_rows(own_ref, other_ref, out_ref, rows, cols):
    dp, core = lax.axis_index("dp"), lax.axis_index("blk") % 2
    n, size = own_ref.shape[0], rows.stop - rows.start
    for k in range(n):
        own, other = own_ref[k ^ dp, rows, cols], other_ref[k ^ dp, rows, cols]
        out_ref[2 * k * size : (2 * k + 1) * size, :] = jnp.where(core == 0, own, other)
        out_ref[(2 * k + 1) * size : (2 * k + 2) * size, :] = jnp.where(core == 0, other, own)


def mod_part_kernel(n, group, *refs):
    packs = refs[:n]
    w_ref, bias_ref = refs[n : n + 2]
    parts = refs[n + 2 : 2 * n + 2]
    cols_ref, projb_ref, qkvb_ref, add_ref, slab_ref = refs[2 * n + 2 :]
    dp, blk = lax.axis_index("dp"), lax.axis_index("blk")
    micro = blk // group
    dshard, span = w_ref.shape[0], bias_ref.shape[0]
    features = dshard * n
    width = features // group
    add_ref[...] = jnp.zeros_like(add_ref)
    bias = jnp.broadcast_to(bias_ref[...].astype(F32).reshape(1, span), (8, span))

    def mine(d):
        add_ref[:, d * span : (d + 1) * span] = bias
        for m in range(n):
            cols_ref[8 * m : 8 * m + 8, :] = packs[m][:8, d * dshard : (d + 1) * dshard].astype(F32)

    by_index(dp, n, mine)
    lhs = []
    for m in range(n):
        slab_ref[m] = packs[m][8:16, :].astype(F32)
        low, high = cols_ref[8 * m : 8 * m + 4, :], cols_ref[8 * m + 4 : 8 * m + 8, :]
        lhs.append(jnp.where(micro == 0, low, high))
    product = dot_nn(jnp.concatenate(lhs, axis=0).astype(BF), w_ref[...])
    for m in range(n):
        parts[m][...] = product[4 * m : 4 * m + 4, :] + add_ref[:4, :]
    rows = [slab_ref[k ^ dp][:1] for k in range(n)]
    projb_ref[...] = jnp.concatenate([r[:, :dshard] for r in rows], axis=1)
    q_bias = jnp.concatenate([r[:, dshard : 2 * dshard] for r in rows], axis=1)
    v_bias = jnp.concatenate([r[:, 2 * dshard : 3 * dshard] for r in rows], axis=1)

    def step(j):
        part = slice(j * width, (j + 1) * width)
        qkvb_ref[...] = jnp.concatenate([q_bias[:, part], jnp.zeros((1, width), F32), v_bias[:, part]], axis=1)

    by_index(blk % group, group, step)


def mod_all_kernel(*refs):
    parts, out_ref = refs[:-1], refs[-1]
    total = parts[0][...]
    for p in parts[1:]:
        total = total + p[...]
    high = total.astype(BF).astype(F32)
    middle = (total - high).astype(BF).astype(F32)
    low = total - high - middle
    blank = jnp.zeros((32 - 3 * DOCS, total.shape[1]), F32)
    out_ref[...] = jnp.concatenate([high, middle, low, blank], axis=0).astype(BF)


def attn_in_kernel(own_ref, got_ref, pick_ref, mod_ref, out_ref, lat_ref, shift_ref, scale_ref):
    seg, features = own_ref.shape
    lat_ref[:seg, :] = own_ref[...]
    lat_ref[seg:, :] = got_ref[...]
    shift_ref[...] = dot_nn(pick_ref[...], mod_ref[:, :features])
    scale_ref[...] = dot_nn(pick_ref[...], mod_ref[:, features : 2 * features])

    def step(rows):
        normed, _ = normalize(lat_ref[rows, :].astype(F32))
        out_ref[rows, :] = (normed * (1.0 + scale_ref[rows, :]) + shift_ref[rows, :]).astype(BF)

    by_rows(lat_ref.shape[0], step)


def grad_fc2_kernel(own_ref, got_ref, pick_ref, pickt_ref, mod_ref, out_ref, cot_ref, sums_ref):
    seg, features = own_ref.shape
    cot_ref[:seg, :] = own_ref[...]
    cot_ref[seg:, :] = got_ref[...]
    gate = dot_nn(pick_ref[...], mod_ref[:, 5 * features : 6 * features])
    out_ref[...] = (gate * cot_ref[...].astype(F32)).astype(BF)
    sums_ref[...] = dot_nn(pickt_ref[...], out_ref[...])


def mix_kernel(group, *refs):
    outs = refs[:group]
    own, other, bias_ref, lat_ref, pick_ref, mod_ref = refs[group : group + 6]
    low_ref, proj_ref, mid_ref, in_ref, heads_ref, w_ref, slab_ref, gate_ref, shift_ref, scale_ref = refs[group + 6 :]
    features = lat_ref.shape[1]
    width = features // group
    mine = lax.axis_index("blk") % group
    size = own.shape[1] // 2
    whole_rows(own, other, w_ref, slice(size, 2 * size), slice(0, features))
    for k in range(group):
        heads_ref[k] = w_ref[k * width : (k + 1) * width, :]
    for m in range(group):
        slab_ref[m] = outs[m][...]
    low_ref[...] = jnp.concatenate([slab_ref[k ^ mine] for k in range(group)], axis=1)
    proj_ref[...] = dot_nn(low_ref[...], w_ref[...]) + bias_ref[...]
    gate_ref[...] = dot_nn(pick_ref[...], mod_ref[:, 2 * features : 3 * features])
    shift_ref[...] = dot_nn(pick_ref[...], mod_ref[:, 3 * features : 4 * features])
    scale_ref[...] = dot_nn(pick_ref[...], mod_ref[:, 4 * features : 5 * features])

    def step(rows):
        mid = lat_ref[rows, :].astype(F32) + gate_ref[rows, :] * proj_ref[rows, :]
        mid_ref[rows, :] = mid
        normed, _ = normalize(mid)
        in_ref[rows, :] = (normed * (1.0 + scale_ref[rows, :]) + shift_ref[rows, :]).astype(BF)

    by_rows(lat_ref.shape[0], step)


def turn_kernel(pieces, group, *refs):
    parts = refs[:pieces]
    cot_ref, mid_ref, proj_ref, heads_ref, pick_ref, pickt_ref, mod_ref = refs[pieces : pieces + 7]
    gmid_ref, gproj_ref, sums_ref = refs[pieces + 7 : pieces + 10]
    grads = refs[pieces + 10 : pieces + 10 + group]
    gate_ref, scale_ref, a_ref, b_ref, c_ref = refs[pieces + 10 + group :]
    features = cot_ref.shape[1]
    mine = lax.axis_index("blk") % group
    gate_ref[...] = dot_nn(pick_ref[...], mod_ref[:, 2 * features : 3 * features])
    scale_ref[...] = dot_nn(pick_ref[...], mod_ref[:, 4 * features : 5 * features])

    def step(rows):
        grad_in = parts[0][rows, :].astype(F32)
        for p in parts[1:]:
            grad_in = grad_in + p[rows, :].astype(F32)
        normed, inverse = normalize(mid_ref[rows, :])
        gmid = cot_ref[rows, :].astype(F32) + normalize_back(
            grad_in * (1.0 + scale_ref[rows, :]), normed, inverse
        )
        gmid_ref[rows, :] = gmid
        gproj_ref[rows, :] = (gate_ref[rows, :] * gmid).astype(BF)
        a_ref[rows, :] = gmid * proj_ref[rows, :]
        b_ref[rows, :] = grad_in
        c_ref[rows, :] = grad_in * normed

    by_rows(cot_ref.shape[0], step)
    for m in range(group):
        grads[m][...] = dot_nt(gproj_ref[...], heads_ref[m ^ mine]).astype(BF)
    pick = pickt_ref[...]
    sums_ref[:, :features] = doc_sums(pick, a_ref[...])
    sums_ref[:, features : 2 * features] = doc_sums(pick, b_ref[...])
    sums_ref[:, 2 * features : 3 * features] = doc_sums(pick, c_ref[...])
    sums_ref[:, 3 * features :] = dot_nn(pick, gproj_ref[...])


def outs_kernel(pieces, *refs):
    parts = refs[:pieces]
    cot_ref, mid_ref, pick_ref, pickt_ref, mod_ref, out_ref, low_ref, sums_ref, hold_ref, gate_ref, a_ref = refs[pieces:]
    features = cot_ref.shape[1]
    gate_ref[...] = dot_nn(pick_ref[...], mod_ref[:, 5 * features : 6 * features])

    def step(rows):
        fc2_out = parts[0][rows, :].astype(F32)
        for p in parts[1:]:
            fc2_out = fc2_out + p[rows, :].astype(F32)
        hold_ref[rows, :] = (mid_ref[rows, :] + gate_ref[rows, :] * fc2_out).astype(BF)
        a_ref[rows, :] = cot_ref[rows, :].astype(F32) * fc2_out

    by_rows(cot_ref.shape[0], step)
    seg = out_ref.shape[0]
    out_ref[...] = hold_ref[:seg, :]
    low_ref[...] = hold_ref[seg:, :]
    sums_ref[...] = doc_sums(pickt_ref[...], a_ref[...])


def finish_kernel(starts, seg, *refs):
    pieces = len(starts)
    parts = [r.at[at : at + 2 * seg, :] for r, at in zip(refs, starts)]
    lat_ref, gmid_ref, pick_ref, pickt_ref, mod_ref, out_ref, low_ref, sums_ref, scale_ref, b_ref, c_ref = refs[
        pieces:
    ]
    features = lat_ref.shape[1]
    scale_ref[...] = dot_nn(pick_ref[...], mod_ref[:, features : 2 * features])

    def rows_step(rows):
        grad_in = parts[0][rows, :].astype(F32)
        for p in parts[1:]:
            grad_in = grad_in + p[rows, :].astype(F32)
        normed, inverse = normalize(lat_ref[rows, :].astype(F32))
        b_ref[rows, :] = grad_in
        c_ref[rows, :] = grad_in * normed
        return gmid_ref[rows, :] + normalize_back(grad_in * (1.0 + scale_ref[rows, :]), normed, inverse)

    def step(rows):
        c_rows = rows
        grad = rows_step(c_rows)
        out_ref[rows, :] = grad

    def step_low(rows):
        out = rows_step(pl.ds(pl.multiple_of(rows.start + seg, CHUNK), CHUNK))
        low_ref[rows, :] = out.astype(BF)

    by_rows(seg, step)
    by_rows(seg, step_low)
    pick = pickt_ref[...]
    sums_ref[:, :features] = doc_sums(pick, b_ref[...])
    sums_ref[:, features:] = doc_sums(pick, c_ref[...])


def attend(row_in, qkv_cols, qkv_b, docq, dock, hpd):
    group, block = len(row_in), row_in[0].shape[0]
    features = row_in[0].shape[1]
    length, width = group * block, hpd * HEAD
    n, size = len(qkv_cols), qkv_cols[0][0].shape[0]
    counts = [len(c) for c in qkv_cols]
    qkv_cols = [c for cs in qkv_cols for c in cs]
    fixed = lambda i: (0, 0)

    def kernel(*refs):
        xs = refs[:group]
        ws, refs = grouped(refs[group:], counts)
        b_ref, docq_ref, dock_ref = refs[:3]
        refs = refs[3:]
        qkv_ref, w_ref = refs[:2]
        outs = refs[2 : group + 2]
        outt_ref, peak_ref, vt_ref, out_ref, slab_ref = refs[group + 2 :]
        i = pl.program_id(0)

        @pl.when(i == 0)
        def _():
            for m in range(n):
                place_rows(ws[m], slab_ref.at[m])
            for k in range(n):
                w_ref[k * size : (k + 1) * size, :] = slab_ref[k ^ lax.axis_index("dp")]
            for m in range(group):
                part = dot_nn(xs[m][...], w_ref[...]) + b_ref[...]
                qkv_ref[m * block : (m + 1) * block, :] = part.astype(BF)

        attend_kernel(hpd, block, qkv_ref, docq_ref, dock_ref, out_ref, outt_ref, peak_ref, vt_ref)
        for m in range(group):

            @pl.when(i == m)
            def _():
                outs[m][...] = out_ref[...]

    got = launch(
        "attend",
        kernel,
        [*row_in, *qkv_cols, qkv_b, docq, dock],
        in_specs=[pl.BlockSpec((block, features), fixed) for _ in range(group)]
        + [pl.BlockSpec(c.shape, fixed) for c in qkv_cols]
        + [
            pl.BlockSpec((1, 3 * width), fixed),
            pl.BlockSpec((1, block), lambda i: (0, i)),
            pl.BlockSpec((length, 128), fixed),
        ],
        out_specs=[pl.BlockSpec((length, 3 * width), fixed), pl.BlockSpec((features, 3 * width), fixed)]
        + [pl.BlockSpec((block, width), fixed) for _ in range(group)]
        + [
            pl.BlockSpec((width, block), lambda i: (0, i)),
            pl.BlockSpec((8, block), lambda i: (0, i)),
        ],
        out_shape=[sds((length, 3 * width), BF), sds((features, 3 * width), BF)]
        + [sds((block, width), BF) for _ in range(group)]
        + [sds((width, length), F32), sds((8, length), F32)],
        scratch=[
            pltpu.VMEM((hpd, HEAD, length), BF),
            pltpu.VMEM((block, width), BF),
            pltpu.VMEM((n, size, 3 * width), BF),
        ],
        grid=(group,),
    )
    return got[0], got[2 : 2 + group], got[2 + group], got[3 + group], got[1]


def attend_back(qkv, grad_out, outt, peak, docq, dock, hpd):
    group, block = len(grad_out), grad_out[0].shape[0]
    length, width = group * block, hpd * HEAD
    fixed = lambda i: (0, 0)

    def kernel(qkv_ref, *refs):
        dos = refs[:group]
        outt_ref, peak_ref, docq_ref, dock_ref = refs[group : group + 4]
        grad_ref, kt_ref, dk_ref, dv_ref, do_ref = refs[group + 4 :]

        @pl.when(pl.program_id(0) == 0)
        def _():
            for m in range(group):
                do_ref[m * block : (m + 1) * block, :] = dos[m][...]

        attend_back_kernel(
            hpd, block, group, qkv_ref, do_ref, outt_ref, peak_ref, docq_ref, dock_ref, grad_ref, kt_ref, dk_ref, dv_ref
        )

    return launch(
        "attend_back",
        kernel,
        [qkv, *grad_out, outt, peak, docq, dock],
        in_specs=[pl.BlockSpec((length, 3 * width), fixed)]
        + [pl.BlockSpec((block, width), fixed) for _ in range(group)]
        + [
            pl.BlockSpec((width, block), lambda i: (0, i)),
            pl.BlockSpec((8, block), lambda i: (0, i)),
            pl.BlockSpec((1, block), lambda i: (0, i)),
            pl.BlockSpec((length, 128), fixed),
        ],
        out_specs=[pl.BlockSpec((length, 3 * width), fixed)],
        out_shape=[sds((length, 3 * width), BF)],
        scratch=[
            pltpu.VMEM((hpd, HEAD, length), BF),
            pltpu.VMEM((hpd, length, HEAD), F32),
            pltpu.VMEM((hpd, length, HEAD), F32),
            pltpu.VMEM((length, width), BF),
        ],
        grid=(group,),
    )[0]


def place_rows(pieces, ref):
    at = 0
    for p in pieces:
        ref[at : at + p.shape[0], :] = p[...]
        at += p.shape[0]


def mlp_kernel(xs, gs, per, refs):
    n = len(xs)
    w_own, w_other, b1_ref, w2_ref, b2_ref = refs[:5]
    act_ref, gf1_ref, sums_ref = refs[5:8]
    backs, parts = refs[8 : 8 + n], refs[8 + n : 8 + 2 * n]
    w1_ref, x_ref, g_ref, back_ref, part_ref, row_ref = refs[8 + 2 * n :]
    i = pl.program_id(0)
    hidden = w1_ref.shape[1]
    block = x_ref.shape[0] // per

    @pl.when(i == 0)
    def _():
        size = w_own.shape[1] // 2
        whole_rows(w_own, w_other, w1_ref, slice(0, size), slice(0, hidden))
        sums_ref[...] = jnp.zeros_like(sums_ref)
        row_ref[...] = jnp.zeros_like(row_ref)
        span = b2_ref.shape[0]

        def bias(d):
            row_ref[0:1, d * span : (d + 1) * span] = b2_ref[...].astype(F32).reshape(1, span)

        by_index(lax.axis_index("dp"), n, bias)

    for m in range(n):

        @pl.when(i == m // per)
        def _():
            at = pl.ds(m % per * block, block)
            place_rows(xs[m], x_ref.at[at, :])
            place_rows(gs[m], g_ref.at[at, :])

    u = dot_nn(x_ref[...], w1_ref[...]) + b1_ref[...].astype(F32).reshape(1, hidden)
    root = 0.7978845608028654
    squared = u * u
    t = jnp.tanh(root * u * (1.0 + 0.044715 * squared))
    act = (0.5 * u * (1.0 + t)).astype(BF)
    act_ref[...] = act
    slope = 0.5 * (1.0 + t) + 0.5 * u * (1.0 - t * t) * (root * (1.0 + 3 * 0.044715 * squared))
    gf1 = (dot_nt(g_ref[...], w2_ref[...]) * slope).astype(BF)
    gf1_ref[...] = gf1
    back_ref[...] = dot_nt(gf1, w1_ref[...]).astype(BF)
    part_ref[...] = (dot_nn(act, w2_ref[...]) + row_ref[0:1, :]).astype(BF)
    for m in range(n):

        @pl.when(i == m // per)
        def _():
            at = slice(m % per * block, (m % per + 1) * block)
            parts[m][...] = part_ref[at, :]
            backs[m][...] = back_ref[at, :]

    sums_ref[0:1, :hidden] += jnp.sum(gf1.astype(F32), axis=0, keepdims=True)


def grouped(refs, counts):
    out, at = [], 0
    for count in counts:
        out.append(refs[at : at + count])
        at += count
    return out, refs[at:]


def mlp(xs, gs, w_own, w_other, b1, w2, b2):
    n = len(xs)
    block, features = sum(p.shape[0] for p in xs[0]), xs[0][0].shape[1]
    hidden = w2.shape[0]
    per = min(4, n)
    fixed = lambda i: (0, 0)
    piece = pl.BlockSpec((block, features), fixed)
    third = pl.BlockSpec(w_own.shape, lambda i: (0, 0, 0))
    flat = [p for ps in list(xs) + list(gs) for p in ps]
    counts = [len(ps) for ps in list(xs) + list(gs)]

    def kernel(*refs):
        pieces, rest = grouped(refs, counts)
        mlp_kernel(pieces[:n], pieces[n:], per, rest)

    got = launch(
        "mlp",
        kernel,
        flat + [w_own, w_other, b1, w2, b2],
        in_specs=[pl.BlockSpec(p.shape, fixed) for p in flat]
        + [third, third, pl.BlockSpec((hidden,), lambda i: (0,)), pl.BlockSpec((hidden, features), fixed)]
        + [pl.BlockSpec(b2.shape, lambda i: (0,))],
        out_specs=[
            pl.BlockSpec((per * block, hidden), lambda i: (i, 0)),
            pl.BlockSpec((per * block, hidden), lambda i: (i, 0)),
            pl.BlockSpec((8, features), fixed),
        ]
        + [piece] * (2 * n),
        out_shape=[
            sds((n * block, hidden), BF),
            sds((n * block, hidden), BF),
            sds((8, features), F32),
        ]
        + [sds((block, features), BF)] * (2 * n),
        scratch=[
            pltpu.VMEM((features, hidden), BF),
            pltpu.VMEM((per * block, features), BF),
            pltpu.VMEM((per * block, features), BF),
            pltpu.VMEM((per * block, features), BF),
            pltpu.VMEM((per * block, features), BF),
            pltpu.VMEM((8, features), F32),
        ],
        grid=(n // per,),
    )
    return got[:3], got[3 : n + 3], got[n + 3 :]


def wgrad(lefts, rights, name):
    rows, cols = lefts[0].shape[1], rights[0].shape[1]
    block = 384 if rows % 384 == 0 else rows

    def kernel(*refs):
        a_refs, b_refs = refs[: len(lefts)], refs[len(lefts) : -1]

        left = jnp.concatenate([r[...] for r in a_refs], axis=0)
        right = jnp.concatenate([r[...] for r in b_refs], axis=0)
        refs[-1][...] = dot_tn(left, right).astype(BF)

    return launch(
        name,
        kernel,
        list(lefts) + list(rights),
        in_specs=[pl.BlockSpec((a.shape[0], block), lambda i: (0, i)) for a in lefts]
        + [pl.BlockSpec(b.shape, lambda i: (0, 0)) for b in rights],
        out_specs=[pl.BlockSpec((block, cols), lambda i: (i, 0))],
        out_shape=[sds((rows, cols), BF)],
        grid=(rows // block,),
    )[0]


def core_rows(ref, groups, k, mine):
    core = lax.axis_index("blk") % 2
    size = ref.shape[0] // (2 * groups)
    low = ref[2 * k * size : (2 * k + 1) * size, :]
    high = ref[(2 * k + 1) * size : (2 * k + 2) * size, :]
    return jnp.where(core == 0, low, high) if mine else jnp.where(core == 0, high, low)


def other_half(x, groups, name):
    rows, cols = x.shape
    size = rows // (2 * groups)

    def kernel(x_ref, out_ref):
        for k in range(groups):
            out_ref[k * size : (k + 1) * size, :] = core_rows(x_ref, groups, k, False)

    return whole_call(kernel, name, [sds((rows // 2, cols), BF)], [x])[0]


def halves(total, bit):
    size = total.shape[0] // 2
    mine = (lax.axis_index("blk") // bit) % 2
    low, high = total[:size], total[size:]
    return jnp.where(mine == 0, low, high), jnp.where(mine == 0, high, low)


def own_half(x, got, groups, bit, name):
    rows, cols = x.shape
    size = rows // (2 * groups)

    def kernel(x_ref, got_ref, keep_ref, send_ref, all_ref):
        for k in range(groups):
            at = slice(k * size, (k + 1) * size)
            mine = core_rows(x_ref, groups, k, True).astype(F32)
            all_ref[at, :] = (mine + got_ref[at, :].astype(F32)).astype(BF)
        keep_ref[...], send_ref[...] = halves(all_ref[...], bit)

    return whole_call(
        kernel, name, [sds((rows // 4, cols), BF)] * 2, [x, got], [pltpu.VMEM((rows // 2, cols), BF)]
    )


def own_blocks(x, got, n, name):
    rows, cols = x.shape
    size = rows // (2 * n)

    def kernel(x_ref, got_ref, *outs):
        def step(d):
            for m in range(n):
                k = m ^ d
                mine = core_rows(x_ref, n, k, True).astype(F32)
                outs[m][...] = (mine + got_ref[k * size : (k + 1) * size, :].astype(F32)).astype(BF)

        by_index(lax.axis_index("dp"), n, step)

    return whole_call(kernel, name, [sds((size, cols), BF)] * n, [x, got])


def give_back(own, other, name):
    seg, features = own.shape

    def kernel(own_ref, other_ref, out_ref):
        micro = lax.axis_index("blk") // (lax.axis_size("blk") // 2)
        out_ref[micro, 0] = own_ref[...]
        out_ref[1 - micro, 0] = other_ref[...].astype(out_ref.dtype)

    return whole_call(kernel, name, [sds((2, 1, seg, features), own.dtype)], [own, other])[0]


def add_up(refs):
    total = refs[0][...].astype(F32)
    for r in refs[1:]:
        total = total + r[...].astype(F32)
    return total


def fold_sum(parts, bit, name):
    def kernel(*refs):
        keep, send = halves(add_up(refs[:-2]), bit)
        refs[-2][...], refs[-1][...] = keep.astype(BF), send.astype(BF)

    rows, cols = parts[0].shape
    return whole_call(kernel, name, [sds((rows // 2, cols), BF)] * 2, list(parts))


def join_rows(own, got, bit, name):
    def kernel(own_ref, got_ref, out_ref):
        low = (lax.axis_index("blk") // bit) % 2 == 0
        size = own_ref.shape[0]
        out_ref[:size, :] = jnp.where(low, own_ref[...], got_ref[...])
        out_ref[size:, :] = jnp.where(low, got_ref[...], own_ref[...])

    return whole_call(kernel, name, [sds((2 * own.shape[0], own.shape[1]), BF)], [own, got])[0]


def join_blocks(own, got, bit, n, name):
    rows, cols = 2 * own.shape[0], own.shape[1]
    size = rows // n

    def kernel(own_ref, got_ref, *refs):
        outs, all_ref = refs[:-1], refs[-1]
        low = (lax.axis_index("blk") // bit) % 2 == 0
        half = own_ref.shape[0]
        all_ref[:half, :] = jnp.where(low, own_ref[...], got_ref[...])
        all_ref[half:, :] = jnp.where(low, got_ref[...], own_ref[...])

        def step(d):
            for m in range(n):
                outs[m][...] = all_ref[(m ^ d) * size : ((m ^ d) + 1) * size, :]

        by_index(lax.axis_index("dp"), n, step)

    return whole_call(kernel, name, [sds((size, cols), BF)] * n, [own, got], [pltpu.VMEM((rows, cols), BF)])


def sum_of(parts, name, dtype=BF):
    def kernel(*refs):
        refs[-1][...] = add_up(refs[:-1]).astype(dtype)

    return whole_call(kernel, name, [sds(parts[0].shape, dtype)], list(parts))[0]


def take_from(x, got, chips, name):
    def kernel(x_ref, got_ref, out_ref):
        chip = lax.axis_index("blk") // 2
        here = functools.reduce(jnp.logical_or, [chip == c for c in chips])
        out_ref[...] = jnp.where(here, got_ref[...].astype(F32), x_ref[...].astype(F32)).astype(BF)

    return whole_call(kernel, name, [sds(x.shape, BF)], [x, got])[0]


def sum_at(parts, count, name):
    def kernel(*refs):
        refs[-1][...] = add_up([r.at[at : at + count, :] for r, (_, at) in zip(refs, parts)]).astype(BF)

    shape = sds((count, parts[0][0].shape[1]), BF)
    return whole_call(kernel, name, [shape], [x for x, _ in parts])[0]


def qkv_wgrad_kernel(n, group, *refs):
    xs, grad_ref = refs[:group], refs[group]
    outs = refs[group + 1 : group + 1 + n]
    bias_ref, acc_ref = refs[group + 1 + n :]
    block, features = xs[0].shape
    size, width = features // n, grad_ref.shape[1] // 3
    mine = lax.axis_index("dp")
    step = 384 if features % 384 == 0 else features
    for at in range(0, features, step):
        total = dot_tn(xs[0][:, at : at + step], grad_ref[:block, :])
        for m in range(1, group):
            total = total + dot_tn(xs[m][:, at : at + step], grad_ref[m * block : (m + 1) * block, :])
        acc_ref[at : at + step, :] = total
    for m in range(n):
        rows = pl.ds(pl.multiple_of((m ^ mine) * size, size), size)
        outs[m][...] = acc_ref[rows, :].astype(BF)
    total = dot_nn(jnp.ones((8, block * group), BF), grad_ref[...])
    bias_ref[...] = jnp.zeros_like(bias_ref)

    def place(j):
        bias_ref[:, j * width : (j + 1) * width] = total[:, :width]
        bias_ref[:, features + j * width : features + (j + 1) * width] = total[:, 2 * width :]

    by_index(lax.axis_index("blk") % group, group, place)


def place_qkv_kernel(group, *refs):
    parts = refs[:group]
    out_ref, slab_ref = refs[group:]
    mine = lax.axis_index("blk") % group
    size = parts[0].shape[1] // 3
    for m in range(group):
        slab_ref[m] = parts[m][...]
    for j in range(group):
        got = slab_ref[j ^ mine].astype(F32)
        for p in range(3):
            at = p * group * size + j * size
            out_ref[:, at : at + size] = got[:, p * size : (p + 1) * size]


def both_cores(own, other):
    core = lax.axis_index("blk") % 2
    return jnp.where(core == 0, own, other), jnp.where(core == 0, other, own)


def place_fc1(own, other, name):
    n = len(own)
    size, cols = own[0].shape
    wide = n if cols % 128 else 1

    def kernel(*refs):
        out_ref = refs[-1]
        for t in range(wide):
            at = slice(t * cols, (t + 1) * cols)

            def step(k):
                low, high = both_cores(refs[k][...].astype(F32), refs[n + k][...].astype(F32))
                out_ref[:size, at] = low
                out_ref[size:, at] = high

            by_index((pl.program_id(0) * wide + t) ^ lax.axis_index("dp"), n, step)

    piece = pl.BlockSpec((size, cols), lambda j: (0, 0))
    return launch(
        name,
        kernel,
        list(own) + list(other),
        [piece] * (2 * n),
        [pl.BlockSpec((2 * size, wide * cols), lambda j: (0, j))],
        [sds((2 * size, n * cols), F32)],
        grid=(n // wide,),
    )[0]


def both_kernel(half, own_ref, got_ref, out_ref):
    first = lax.axis_index("blk") // half == 0
    own, got = own_ref[...].astype(F32), got_ref[...].astype(F32)
    out_ref[...] = jnp.concatenate([jnp.where(first, own, got), jnp.where(first, got, own)], axis=0).astype(BF)


def add_kernel(a_ref, b_ref, out_ref):
    out_ref[...] = (a_ref[...].astype(F32) + b_ref[...].astype(F32)).astype(out_ref.dtype)


def place_cores_kernel(own_ref, other_ref, out_ref):
    size = out_ref.shape[0] // 2
    low, high = both_cores(own_ref[...].astype(F32), other_ref[...].astype(F32))
    out_ref[:size, :] = low
    out_ref[size:, :] = high


def gather_sums_kernel(in_ref, mid_ref, out_ref, fc1_ref, fc2_ref, qv_ref, all_ref):
    features = out_ref.shape[1]
    all_ref[...] = jnp.zeros_like(all_ref)
    all_ref[:DOCS, : 2 * features] = in_ref[:DOCS, :]
    all_ref[:DOCS, 2 * features : 5 * features] = mid_ref[:DOCS, : 3 * features]
    all_ref[:DOCS, 5 * features :] = out_ref[:DOCS, :]
    row = slice(DOCS, DOCS + 1)
    all_ref[row, :features] = fc1_ref[0:1, :]
    all_ref[row, features : 2 * features] = fc2_ref[row, :]
    all_ref[row, 2 * features : 3 * features] = mid_ref[row, 3 * features :]
    all_ref[row, 3 * features : 5 * features] = qv_ref[0:1, :]


def ada_kernel(n, *refs):
    slots = refs[:n]
    cols_ref, w_ref = refs[n : n + 2]
    wgrad_ref, rows_ref = refs[n + 2 : n + 4]
    conds = refs[n + 4 :]
    got, fc1, rest = [], 0.0, 0.0
    for m in range(n):
        got.append(slots[m][:DOCS, :].astype(F32))
        got.append(slots[m][8 : 8 + DOCS, :].astype(F32))
        bias = slots[m][DOCS : DOCS + 1, :].astype(F32) + slots[m][8 + DOCS : 9 + DOCS, :].astype(F32)
        fc1 = bias if m == 0 else fc1
        rest = rest + bias
    got = jnp.concatenate(got, axis=0)
    rows_ref[...] = jnp.concatenate(
        [jnp.sum(got, axis=0, keepdims=True), rest, fc1, jnp.zeros((5, rest.shape[1]), F32)], axis=0
    )
    got = got.astype(BF)
    wgrad_ref[...] = dot_tn(cols_ref[...].astype(BF), got)
    back = dot_nt(got, w_ref[...])
    first = pl.program_id(0) == 0
    for m in range(n):
        part = back[8 * m : 8 * m + 8, :]
        conds[m][...] = part + jnp.where(first, 0.0, conds[m][...])


def ada(slots, cols, weight):
    n = len(slots)
    dshard, span = weight.shape
    block = span // 6
    return launch(
        "ada",
        functools.partial(ada_kernel, n),
        [*slots, cols, weight],
        in_specs=[pl.BlockSpec((16, block), lambda i: (0, i))] * n
        + [pl.BlockSpec(cols.shape, lambda i: (0, 0)), pl.BlockSpec((dshard, block), lambda i: (0, i))],
        out_specs=[pl.BlockSpec((dshard, block), lambda i: (0, i)), pl.BlockSpec((8, block), lambda i: (0, i))]
        + [pl.BlockSpec((8, dshard), lambda i: (0, 0))] * n,
        out_shape=[sds((dshard, span), F32), sds((8, span), F32)] + [sds((8, dshard), F32)] * n,
        grid=(6,),
    )


def biases_kernel(n, rows_ref, ada_ref, qv_ref, proj_ref, fc1_ref, fc2_ref):
    features = rows_ref.shape[1] // 6
    span, size = ada_ref.shape[0], fc2_ref.shape[0]

    def step(d):
        def part(i):
            at = i * features + d * size
            return rows_ref[1:2, at : at + size]

        ada_ref[...] = rows_ref[0:1, d * span : (d + 1) * span].reshape(span)
        fc2_ref[...] = part(1).reshape(size)
        proj_ref[...] = part(2).reshape(size)
        qv_ref[0:1, :] = part(3)
        qv_ref[1:2, :] = part(4)

    by_index(lax.axis_index("dp"), n, step)
    fc1_ref[...] = rows_ref[2:3, : fc1_ref.shape[0]].reshape(fc1_ref.shape[0])


def cond_kernel(n, *refs):
    parts, cond_ref, out_ref, slab_ref = refs[:n], refs[n], refs[n + 1], refs[n + 2]
    dp = lax.axis_index("dp")
    for m in range(n):
        slab_ref[m] = parts[m][...]
    grad = jnp.concatenate([slab_ref[k ^ dp] for k in range(n)], axis=1)
    for u in range(2):
        cond = cond_ref[u, 0].astype(F32)
        sig = 1.0 / (1.0 + jnp.exp(-cond))
        out_ref[u, 0] = grad[u * DOCS : (u + 1) * DOCS] * (sig * (1.0 + cond * (1.0 - sig)))


def local(
    latents,
    conditions,
    doc_lengths,
    cotangent,
    ada_weight,
    ada_bias,
    qkv_weight,
    qv_bias,
    proj_weight,
    proj_bias,
    fc1_weight,
    fc1_bias,
    fc2_weight,
    fc2_bias,
):
    n_dp, n_blk = lax.axis_size("dp"), lax.axis_size("blk")
    dp, blk = lax.axis_index("dp"), lax.axis_index("blk")
    half = n_blk // 2
    group = half
    core, micro = blk % 2, blk // half
    seg, features = latents.shape[2], latents.shape[3]
    hidden = fc1_weight.shape[1] // n_dp
    dshard = features // n_dp
    hpd = HEADS // group
    width = hpd * HEAD
    hhalf, dhalf = hidden // 2, dshard // 2
    tokens = 2 * seg
    LAST.clear()
    masks = [2 * i for i in range(group // 2)] + [2 * i + 1 for i in range(group // 2)]

    act_shape = sds((tokens, features), BF)
    half_shape = sds((seg, features), BF)
    full_shape = sds((tokens, features), F32)
    sums_shape = sds((16, features), F32)
    full_vmem = pltpu.VMEM((tokens, features), F32)
    v = types.SimpleNamespace()
    chip_bits = bits_of(2, n_blk)

    def step_open():
        args = [conditions, proj_bias, qv_bias, doc_lengths]
        v.pack, v.docq, v.dock, v.pick_mod, v.pick_sum = launch(
            "open",
            functools.partial(open_kernel, half, seg),
            args,
            [pl.BlockSpec(x.shape, lambda i, n=x.ndim: (0,) * n) for x in args[:3]] + [SM],
            [VM] * 5,
            [
                sds((16, features), BF),
                sds((1, group * tokens), jnp.int32),
                sds((group * tokens, 128), jnp.int32),
                sds((tokens, 32), BF),
                sds((16, tokens), BF),
            ],
            grid=(1,),
        )
        v.pack = direct({m: v.pack for m in range(n_dp)}, "dp")

    def step_lat():
        v.lat_own, send = whole_call(functools.partial(part_ways_kernel, half), "lat", [half_shape] * 2, [latents])
        v.lat_got = swap(send, "blk", half)

    def step_cot():
        v.cot_own, send = whole_call(functools.partial(part_ways_kernel, half), "cot", [half_shape] * 2, [cotangent])
        v.cot_got = swap(send, "blk", half)

    def step_qkv_cols():
        (cols,) = whole_call(
            functools.partial(qkv_cols_kernel, group), "qkv_cols", [sds((dshard, 3 * width), BF)], [qkv_weight]
        )
        v.qkv_cols = spread_dp(cols)

    def step_mod_part():
        *parts, v.cond_cols, v.proj_b, v.qkv_bias = whole_call(
            functools.partial(mod_part_kernel, n_dp, group),
            "mod_part",
            [sds((DOCS, 6 * features), F32)] * n_dp
            + [sds((8 * n_dp, dshard), F32), sds((1, features), F32), sds((1, 3 * width), F32)],
            [v.pack[m] for m in range(n_dp)] + [ada_weight, ada_bias],
            [pltpu.VMEM((8, 6 * features), F32), pltpu.VMEM((n_dp, 8, features), F32)],
        )
        v.mod_parts = direct(dict(enumerate(parts)), "dp")

    def step_mod_all():
        parts = [v.mod_parts[m] for m in range(n_dp)]
        (v.mod,) = whole_call(mod_all_kernel, "mod_all", [sds((32, 6 * features), BF)], parts)

    def step_attn_in():
        attn_in, v.latent = whole_call(
            attn_in_kernel,
            "attn_in",
            [act_shape] * 2,
            [v.lat_own, v.lat_got, v.pick_mod, v.mod],
            [full_vmem] * 2,
        )
        rows = {0: attn_in}
        for bit in bits_of(2, group):
            for m in list(rows):
                rows[m | bit] = swap(rows[m], "blk", bit)
        for m in list(rows):
            rows[m | 1] = swap(rows[m], "blk", 1)
        v.row_in = [rows[m] for m in masks]

    def step_grad_fc2():
        grad_fc2, v.cot, v.sums_fc2 = whole_call(
            grad_fc2_kernel,
            "grad_fc2",
            [act_shape, act_shape, sums_shape],
            [v.cot_own, v.cot_got, v.pick_mod, v.pick_sum, v.mod],
        )
        v.all_grad = spread_dp(grad_fc2)

    def step_cuts():
        move = whole_call(
            functools.partial(cuts_kernel, n_dp),
            "cuts",
            [sds((2 * dhalf, features), BF)] * n_dp,
            [fc1_weight, proj_weight],
        )
        v.move = direct(dict(enumerate(move)), "dp")

    def step_attend():
        v.qkv, outs, v.outt, v.peak, v.qkv_w = attend(
            v.row_in, v.qkv_cols, v.qkv_bias, v.docq, v.dock, hpd
        )
        v.outs = direct(dict(zip(masks, outs)), "blk")

    def step_stack():
        (v.move_own,) = whole_call(
            functools.partial(stack_kernel, n_dp),
            "stack",
            [sds((n_dp, 2 * dhalf, features), BF)],
            [v.move[m] for m in range(n_dp)],
        )
        v.move_other = swap(v.move_own, "blk", 1)

    def step_mix():
        v.low, v.attn_proj, v.mid, mlp_in, v.proj_w = whole_call(
            functools.partial(mix_kernel, group),
            "mix",
            [act_shape, full_shape, full_shape, act_shape, sds((group, width, features), BF)],
            [v.outs[m] for m in range(group)]
            + [v.move_own, v.move_other, v.proj_b, v.latent, v.pick_mod, v.mod],
            [pltpu.VMEM((features, features), BF), pltpu.VMEM((group, tokens, width), BF)] + [full_vmem] * 3,
        )
        v.all_in = spread_dp(mlp_in)

    def step_mlp():
        (v.act, v.grad_fc1, v.sums_fc1), back, part = mlp(
            v.all_in, v.all_grad, v.move_own, v.move_other, fc1_bias, fc2_weight, fc2_bias
        )
        v.back = direct(dict(enumerate(back)), "dp")
        v.part = direct(dict(enumerate(part)), "dp")

    def flat(pieces):
        return [p for ps in pieces for p in ps]

    def step_fc2_wgrad():
        v.fc2_g = wgrad([v.act], flat(v.all_grad), "fc2_wgrad")

    def step_fc1_wgrad():
        v.fc1_g = wgrad(flat(v.all_in), [v.grad_fc1], "fc1_wgrad")

    def step_turn():
        v.gmid, v.grad_proj, v.sums_mid, *grad_attn = whole_call(
            functools.partial(turn_kernel, n_dp, group),
            "turn",
            [full_shape, act_shape, sds((16, 4 * features), F32)] + [sds((tokens, width), BF)] * group,
            [v.back[m] for m in range(n_dp)]
            + [v.cot, v.mid, v.attn_proj, v.proj_w, v.pick_mod, v.pick_sum, v.mod],
            [full_vmem] * 5,
        )
        v.grad_attn = direct(dict(enumerate(grad_attn)), "blk")

    def step_proj_wgrad():
        v.proj_g = wgrad([v.low], [v.grad_proj], "proj_wgrad")

    def halve(x, groups, name):
        return swap(other_half(x, groups, name), "blk", 1)

    def step_fc2_other():
        v.fc2_got = halve(v.fc2_g, 1, "fc2_other")

    def step_fc1_other():
        v.fc1_got = halve(v.fc1_g, n_dp, "fc1_other")

    def step_proj_other():
        v.proj_got = halve(v.proj_g, n_dp, "proj_other")

    def step_fc2_own():
        v.fc2 = CubeSum(*own_half(v.fc2_g, v.fc2_got, 1, chip_bits[0], "fc2_own"), chip_bits, "fc2_cube")

    def step_fc1_own():
        v.fc1 = CubeSum(*own_half(v.fc1_g, v.fc1_got, n_dp, chip_bits[0], "fc1_own"), chip_bits, "fc1_cube")

    def step_fc2_a():
        v.fc2.fold()

    def step_fc2_b():
        v.fc2.total()

    def step_fc2_j():
        v.fc2.join()

    def step_fc1_a():
        v.fc1.fold()

    def step_fc1_b():
        v.fc1.total()

    def step_fc1_j():
        v.fc1.join()

    def step_proj_a():
        v.proj.until(2)

    def step_proj_b():
        v.proj.until(1)

    def step_fc2_c():
        v.fc2_own = join_rows(v.fc2.x, v.fc2.got, chip_bits[0], "fc2_cube")
        v.fc2_other = swap(v.fc2_own, "blk", 1)

    def step_fc1_c():
        blocks = join_blocks(v.fc1.x, v.fc1.got, chip_bits[0], n_dp, "fc1_cube")
        blocks = direct(dict(enumerate(blocks)), "dp")
        v.fc1_own = [blocks[m] for m in range(n_dp)]
        v.fc1_other = [swap(x, "blk", 1) for x in v.fc1_own]

    def step_proj_blocks():
        v.proj_parts = direct(
            dict(enumerate(own_blocks(v.proj_g, v.proj_got, n_dp, "proj_blocks"))), "dp"
        )

    def step_proj_sum():
        v.proj = LineSum(sum_of([v.proj_parts[m] for m in range(n_dp)], "proj_sum"), "proj_line")

    def step_proj_c():
        v.proj.until(0)
        v.proj_other = swap(v.proj.x, "blk", 1)

    def step_attend_back():
        grad_qkv = attend_back(
            v.qkv, [v.grad_attn[m] for m in masks], v.outt, v.peak, v.docq, v.dock, hpd
        )
        v.grad_qkv = grad_qkv
        count = (group // 2) * tokens
        send = swap(dot_nt(grad_qkv[count:], v.qkv_w).astype(BF), "blk", 1)
        keep = dot_nt(grad_qkv[:count], v.qkv_w).astype(BF)
        v.blocks = {m: [(keep, i * tokens), (send, i * tokens)] for i, m in enumerate(masks[: group // 2])}

    def step_qkv_wgrad():
        *qkv_g, v.sums_qv = whole_call(
            functools.partial(qkv_wgrad_kernel, n_dp, group),
            "qkv_wgrad",
            [sds((dshard, 3 * width), BF)] * n_dp + [sds((8, 2 * features), F32)],
            v.row_in + [v.grad_qkv],
            [pltpu.VMEM((features, 3 * width), F32)],
        )
        v.qkv_g = direct(dict(enumerate(qkv_g)), "dp")

    def step_outs():
        v.block_own, other, v.sums_out = whole_call(
            functools.partial(outs_kernel, n_dp),
            "outs",
            [half_shape, half_shape, sums_shape],
            [v.part[m] for m in range(n_dp)] + [v.cot, v.mid, v.pick_mod, v.pick_sum, v.mod],
            [pltpu.VMEM((tokens, features), BF)] + [full_vmem] * 2,
        )
        v.block_other = swap(other, "blk", half)

    def step_attn_sum():
        blocks = v.blocks
        for bit in reversed(bits_of(2, group)):
            for m in [m for m in blocks if m & bit]:
                blocks[m ^ bit].append((swap(sum_at(blocks.pop(m), tokens, "attn_sum"), "blk", bit), 0))

    def step_finish():
        parts = v.blocks[0]
        v.latent_own, other, v.sums_in = whole_call(
            functools.partial(finish_kernel, [at for _, at in parts], seg),
            "finish",
            [sds((seg, features), F32), half_shape, sds((16, 2 * features), F32)],
            [x for x, _ in parts] + [v.latent, v.gmid, v.pick_mod, v.pick_sum, v.mod],
            [full_vmem] * 3,
        )
        v.latent_other = swap(other, "blk", half)

    def step_qkv_sum():
        v.qkv_x = sum_of([v.qkv_g[m] for m in range(n_dp)], "qkv_sum")
        v.qkv_got = swap(v.qkv_x, "blk", half)

    def step_qkv_sum2():
        parts = {0: sum_of([v.qkv_x, v.qkv_got], "qkv_sum")}
        for bit in bits_of(2, group):
            for m in list(parts):
                parts[m | bit] = swap(parts[m], "blk", bit)
        for m in list(parts):
            parts[m | 1] = swap(parts[m], "blk", 1)
        v.qkv_parts = parts

    def step_gather_sums():
        (v.sums,) = whole_call(
            gather_sums_kernel,
            "gather_sums",
            [sds((8, 6 * features), F32)],
            [v.sums_in, v.sums_mid, v.sums_out, v.sums_fc1, v.sums_fc2, v.sums_qv],
        )
        v.sums_got = swap(v.sums, "blk", 1)

    def step_sums_c():
        for bit in bits_of(2, group):
            (v.sums,) = whole_call(add_kernel, "sums", [sds(v.sums.shape, BF)], [v.sums, v.sums_got])
            v.sums_got = swap(v.sums, "blk", bit)

    def step_sums_g():
        (v.sums,) = whole_call(add_kernel, "sums", [sds(v.sums.shape, BF)], [v.sums, v.sums_got])
        v.sums_got = swap(v.sums, "blk", half)

    def step_sums_h():
        (both,) = whole_call(
            functools.partial(both_kernel, half), "both", [sds((16, 6 * features), BF)], [v.sums, v.sums_got]
        )
        v.slots = direct({m: both for m in range(n_dp)}, "dp")

    def step_ada():
        v.ada_wgrad, v.rows_sum, *parts = ada([v.slots[m] for m in range(n_dp)], v.cond_cols, ada_weight)
        v.cond_parts = direct(dict(enumerate(parts)), "dp")

    def step_biases():
        spans = [ada_bias.shape, (2, dshard), (dshard,), (hidden,), (dshard,)]
        v.ada_bgrad, v.qv_bgrad, v.proj_bgrad, v.fc1_bgrad, v.fc2_bgrad = whole_call(
            functools.partial(biases_kernel, n_dp), "biases", [sds(x, F32) for x in spans], [v.rows_sum]
        )

    def step_cond():
        (v.cond_grad,) = whole_call(
            functools.partial(cond_kernel, n_dp),
            "cond_grad",
            [sds((2, 1, DOCS, features), F32)],
            [v.cond_parts[m] for m in range(n_dp)] + [conditions],
            [pltpu.VMEM((n_dp, 8, dshard), F32)],
        )

    def step_place_qkv():
        (v.qkv_wgrad,) = whole_call(
            functools.partial(place_qkv_kernel, group),
            "place_qkv",
            [sds((dshard, 3 * features), F32)],
            [v.qkv_parts[m] for m in range(group)],
            [pltpu.VMEM((group, dshard, 3 * width), BF)],
        )

    def step_place_fc2():
        (v.fc2_wgrad,) = whole_call(
            place_cores_kernel, "place_fc2", [sds((hidden, features), F32)], [v.fc2_own, v.fc2_other]
        )

    def step_place_proj():
        (v.proj_wgrad,) = whole_call(
            place_cores_kernel, "place_proj", [sds((dshard, features), F32)], [v.proj.x, v.proj_other]
        )

    def step_place_fc1():
        v.fc1_wgrad = place_fc1(v.fc1_own, v.fc1_other, "place_fc1")

    def step_block_out():
        v.block_out = give_back(v.block_own, v.block_other, "block_out")

    def step_latent_grad():
        v.latent_grad = give_back(v.latent_own, v.latent_other, "latent_grad")

    for step in (
        step_cuts, step_lat, step_open, step_qkv_cols, step_mod_part, step_mod_all, step_attn_in, step_cot,
        step_attend, step_grad_fc2, step_stack, step_mix, step_mlp, step_fc2_wgrad, step_fc1_wgrad, step_turn,
        step_fc2_other, step_fc1_other, step_fc2_own, step_attend_back, step_attn_sum, step_fc1_own,
        step_qkv_wgrad, step_fc2_a, step_proj_wgrad, step_outs, step_finish, step_gather_sums, step_fc2_b,
        step_sums_c, step_qkv_sum, step_fc1_a, step_fc2_j, step_sums_g, step_proj_other, step_proj_blocks,
        step_sums_h, step_fc1_b, step_proj_sum, step_fc2_c, step_ada, step_proj_a, step_qkv_sum2, step_place_fc2,
        step_cond, step_fc1_j, step_proj_b, step_biases, step_place_qkv, step_fc1_c, step_block_out, step_proj_c,
        step_latent_grad, step_place_proj, step_place_fc1,
    ):
        step()

    return (
        v.block_out,
        v.latent_grad,
        v.cond_grad,
        v.ada_wgrad,
        v.ada_bgrad,
        v.qkv_wgrad,
        v.qv_bgrad,
        v.proj_wgrad,
        v.proj_bgrad,
        v.fc1_wgrad,
        v.fc1_bgrad,
        v.fc2_wgrad,
        v.fc2_bgrad,
    )


def solution(mesh):
    in_specs = (
        P(None, "dp", "blk", None),
        P(None, "dp", None, None),
        P(None, "dp", None),
        P(None, "dp", "blk", None),
        P("dp", None),
        P("dp"),
        P("dp", None),
        P(None, "dp"),
        P("dp", None),
        P("dp"),
        P("dp", None),
        P("dp"),
        P("dp", None),
        P("dp"),
    )
    out_specs = (
        P(None, "dp", "blk", None),
        P(None, "dp", "blk", None),
        P(None, "dp", None, None),
        P("dp", None),
        P("dp"),
        P("dp", None),
        P(None, "dp"),
        P("dp", None),
        P("dp"),
        P("dp", None),
        P("dp"),
        P("dp", None),
        P("dp"),
    )
    return jax.shard_map(local, mesh=mesh, in_specs=in_specs, out_specs=out_specs, check_vma=False)
```
